32 devices in a mesh: dp: 8 (over z, y), shard: 4 (over x, core).
Axes of the slice: x: 2, y: 2, z: 4, core: 2. Of those that a mesh axis runs over, the one named last changes fastest.
Arguments:
- tokens: float32 [36864, 768], P(('dp', 'shard')), may hold values from -6 to 6
- cotangent: float32 [36864, 768], P(('dp', 'shard')), may hold values from -6 to 6
- lengths: int32 [128], P(('dp', 'shard')), may hold values from 64 to 288, as said below
- null_flags: int32 [128], P(('dp', 'shard')), may hold values 0 or 1
- weights: float32 [768, 9216], P(('dp', 'shard')), as said below
- moment1: float32 [768, 9216], P(('dp', 'shard')), as said below
- moment2: float32 [768, 9216], P(('dp', 'shard')), as said below
- vectors: float32 [12, 768], replicated, as said below
- vec_moment1: float32 [12, 768], replicated, as said below
- vec_moment2: float32 [12, 768], replicated, as said below
Outputs:
- output: float32 [36864, 768], P(('dp', 'shard'))
- input_grad: float32 [36864, 768], P(('dp', 'shard'))
- new_moment1: float32 [768, 9216], P(('dp', 'shard'))
- new_moment2: float32 [768, 9216], P(('dp', 'shard'))
- new_weights: float32 [768, 9216], P(('dp', 'shard'))
- new_vec_moment1: float32 [12, 768], replicated
- new_vec_moment2: float32 [12, 768], replicated
- new_vectors: float32 [12, 768], replicated
- norm_pairs: float32 [4, 2], replicated
- trust: float32 [4], replicated
The draws below stay inside these ranges and needn't reach their ends.
Inputs may be any that keep to these rules, and one draw needn't show every extreme that they name: `lengths`: valid tokens of a slot, its query included. `null_flags`: 1 marks a null document, of which only the first 64 tokens count. float32 master weights. `moment1`: first moments. `moment2`: positive second moments. `vectors`: gains near one, small biases. `vec_moment1`: first moments. `vec_moment2`: positive second moments.
All inputs are finite; a program needn't handle non-finite values. No bound on the sum of `null_flags` on one device may be relied on, other than what follows from the above.
Results may differ from the reference program's by a relative error of at most 0.013.
The reference program's roundings to bfloat16 on the way count: a program that leaves them out, or rounds other values in their place, can miss the bound.
Values may be sent and summed in bfloat16 or wider, within the bound.
A program may use at most 192 MiB of HBM per device.

```python
import math
import jax
import jax.numpy as jnp
from jax import lax

D = 768
HEADS = 12
FF = 3072
SLOT = 288
QLEN = 64
STEP = 5
SLOTS_DEV = 4
SLOTS = 128
TOKENS = 36864
N_DP = 8
N_SHARD = 4


def owner_rise(row_total, strength):
    per_device = row_total // (N_DP * N_SHARD)
    owner_index = jnp.arange(row_total) // per_device
    outer_part = (owner_index // N_SHARD).astype(jnp.float32) / max(N_DP - 1, 1)
    inner_part = (owner_index % N_SHARD).astype(jnp.float32) / max(N_SHARD - 1, 1)
    return jnp.exp(strength * (outer_part + inner_part - 1.0))


def column_values(first, second, third, fourth):
    columns = jnp.arange(12 * D)
    return jnp.where(columns < 3 * D, first, jnp.where(columns < 4 * D, second, jnp.where(columns < 8 * D, third, fourth))).astype(jnp.float32)


def gradient_scale():
    return column_values(0.5, 0.3, 0.2, 0.4) * math.sqrt(0.6 * TOKENS)


def signed_noise(key, shape):
    return jax.random.normal(key, shape, jnp.float32)


def draw_weights(key, part):
    key = jax.random.fold_in(key, 11)
    key_entries, key_columns = jax.random.split(key)
    entries = signed_noise(key_entries, (D, 12 * D))
    strength = 0.55
    column_scale = jnp.exp(jax.random.uniform(key_columns, (12 * D,), jnp.float32, math.log(0.7), math.log(1.4)))
    fan_in = column_values(D, D / 16, D, FF)
    return entries * owner_rise(D, strength)[:, None] * column_scale / jnp.sqrt(fan_in)


def draw_moment1(key, part):
    key = jax.random.fold_in(key, 12)
    noise_part = signed_noise(key, (D, 12 * D))
    strength = 0.55
    return gradient_scale() * owner_rise(D, strength)[:, None] * noise_part


def draw_moment2(key, part):
    key = jax.random.fold_in(key, 13)
    factor = jnp.exp(jax.random.uniform(key, (D, 12 * D), jnp.float32, 0.0, math.log(4.0)))
    scale_row = gradient_scale()
    return scale_row * scale_row * factor


def draw_vectors(key, part):
    key = jax.random.fold_in(key, 14)
    noise_part = signed_noise(key, (12, D))
    row_index = jnp.arange(12)[:, None]
    base_value = jnp.where((row_index == 3) | (row_index == 6), 1.0, 0.0).astype(jnp.float32)
    return base_value + 0.1 * noise_part


def draw_vec_moment1(key, part):
    key = jax.random.fold_in(key, 15)
    noise_part = signed_noise(key, (12, D))
    return 0.5 * math.sqrt(0.6 * TOKENS) * noise_part


def draw_vec_moment2(key, part):
    key = jax.random.fold_in(key, 16)
    factor = jnp.exp(jax.random.uniform(key, (12, D), jnp.float32, 0.0, math.log(4.0)))
    return 0.25 * 0.6 * TOKENS * factor


def draw_lengths(key, part):
    key = jax.random.fold_in(key, 17)
    slot_index = jnp.arange(SLOTS, dtype=jnp.int32)
    owner_index = slot_index // SLOTS_DEV
    outer_part = owner_index // N_SHARD
    inner_part = owner_index % N_SHARD
    outer_span = max(N_DP - 1, 1)
    inner_span = max(N_SHARD - 1, 1)
    reach_len = QLEN + (SLOT - QLEN) * (outer_span + outer_part) * (inner_span + inner_part) // (4 * outer_span * inner_span)
    shortfall = jax.random.randint(key, (SLOTS,), 0, (reach_len - QLEN) // 4 + 1)
    lengths_out = reach_len - shortfall
    return lengths_out.at[SLOTS - 1].set(SLOT).astype(jnp.int32)


def place_ends(values, rng, least, top_value):
    extent = values.shape
    place = [jax.random.randint(jax.random.fold_in(rng, axis), (), 0, extent[axis]) for axis in range(len(extent))]
    values = values.at[tuple(place)].set(least)
    longest = extent.index(max(extent))
    place[longest] = (place[longest] + 1) % extent[longest]
    return values.at[tuple(place)].set(top_value)


def steps_of(own_key, dims, cuts, low, top_value):
    level, own = 1.0, jax.random.fold_in(own_key, 6)
    for position, blocks in cuts:
        draws = jnp.exp(jax.random.uniform(jax.random.fold_in(own, position), (blocks,), jnp.float32, low / len(cuts), top_value / len(cuts)))
        level = level * jnp.repeat(draws, dims[position] // blocks).reshape([-1 if axis == position else 1 for axis in range(len(dims))])
    return level


def scatter_about(rng, extent, deviation, most, cuts=(), kind=jnp.bfloat16):
    drawn = deviation * jax.random.normal(rng, extent, jnp.float32)
    if cuts:
        drawn = drawn * steps_of(rng, extent, cuts, -0.22, 0.18)
    return jnp.clip(drawn, -most, most).astype(kind)


def setup_inputs(seed: int = 0) -> dict:
    seeds = jax.random.split(jax.random.key(seed), 11)
    return {
        "tokens": scatter_about(seeds[0], (TOKENS, D), 1.0, 6.0, ((0, 32),), jnp.float32),
        "cotangent": scatter_about(seeds[1], (TOKENS, D), 1.0, 6.0, ((0, 32),), jnp.float32),
        "lengths": draw_lengths(jax.random.fold_in(seeds[10], 71), 0),
        "null_flags": place_ends((jax.random.randint(seeds[3], (SLOTS,), 0, 8) < 1).astype(jnp.int32), jax.random.fold_in(seeds[3], 1), 0, 1),
        "weights": draw_weights(jax.random.fold_in(seeds[10], 71), 0),
        "moment1": draw_moment1(jax.random.fold_in(seeds[10], 71), 0),
        "moment2": draw_moment2(jax.random.fold_in(seeds[10], 71), 0),
        "vectors": draw_vectors(jax.random.fold_in(seeds[10], 71), 0),
        "vec_moment1": draw_vec_moment1(jax.random.fold_in(seeds[10], 71), 0),
        "vec_moment2": draw_vec_moment2(jax.random.fold_in(seeds[10], 71), 0),
    }


@jax.custom_vjp
def low(v):
    return lax.optimization_barrier(v.astype(jnp.bfloat16)).astype(jnp.float32)

@jax.custom_vjp
def low_back(v):
    return v

def low_keep(v):
    return (low(v), None)

def low_pass(kept, grad):
    return (grad,)

def back_keep(v):
    return (v, None)

def back_low(kept, grad):
    return (low(grad),)
low.defvjp(low_keep, low_pass)
low_back.defvjp(back_keep, back_low)

def norm_apply(values, gain, shift):
    centred = values - lax.optimization_barrier(jnp.mean(values, axis=-1, keepdims=True))
    inverse = lax.rsqrt(lax.optimization_barrier(jnp.mean(centred * centred, axis=-1, keepdims=True)) + 1e-05)
    return centred * inverse * gain + shift

def reference(tokens, cotangent, lengths, null_flags, weights, moment1, moment2, vectors, vec_moment1, vec_moment2):
    highest = lax.Precision.HIGHEST
    head_size = D // HEADS
    score_scale = head_size ** (-0.5)
    valid_len = jnp.where(null_flags == 1, QLEN, lengths).astype(jnp.int32)
    rows_valid = jnp.arange(SLOT, dtype=jnp.int32)[None, :] < valid_len[:, None]
    groups = SLOTS // 8

    def forward(token_f, weight_f, vector_f):
        rounded = low(weight_f)
        w_qkv = rounded[:, :3 * D]
        w_out = rounded[:, 3 * D:4 * D]
        w_in = rounded[:, 4 * D:8 * D]
        w_down = rounded[:, 8 * D:].reshape(FF, D)
        qkv_bias = jnp.concatenate([vector_f[0], jnp.zeros((D,), jnp.float32), vector_f[1]])
        ffn_bias = vector_f[8:12].reshape(FF)

        def group_fn(packed):
            block_tokens, block_valid = packed
            token_low = low(block_tokens)
            qkv = low(low_back(jnp.dot(token_low, w_qkv, precision=highest) + qkv_bias))
            shaped = qkv.reshape(8, SLOT, 3, HEADS, head_size)
            query_part = shaped[:, :, 0]
            key_part = shaped[:, :, 1]
            value_part = shaped[:, :, 2]
            scores = jnp.einsum('bqhd,bkhd->bhqk', query_part, key_part, precision=highest) * score_scale
            scores = low_back(jnp.where(block_valid[:, None, None, :], scores, -1000000000.0))
            row_top = lax.optimization_barrier(jnp.max(scores, axis=-1, keepdims=True))
            exponent = jnp.exp(scores - row_top)
            softmax_out = low(exponent / lax.optimization_barrier(jnp.sum(exponent, axis=-1, keepdims=True)))
            context = jnp.einsum('bhqk,bkhd->bqhd', softmax_out, value_part, precision=highest)
            context = low(low_back(context.reshape(8 * SLOT, D)))
            attention = low_back(jnp.dot(context, w_out, precision=highest) + vector_f[2])
            hidden_one = norm_apply(block_tokens + attention, vector_f[3], vector_f[4])
            hidden_low = low(hidden_one)
            pre_act = low_back(jnp.dot(hidden_low, w_in, precision=highest) + ffn_bias)
            act_low = low(jax.nn.gelu(pre_act, approximate=False))
            ffn_out = low_back(jnp.dot(act_low, w_down, precision=highest) + vector_f[5])
            return norm_apply(hidden_one + ffn_out, vector_f[6], vector_f[7])
        result = lax.map(jax.checkpoint(group_fn), (token_f.reshape(groups, 8 * SLOT, D), rows_valid.reshape(groups, 8, SLOT)))
        return result.reshape(SLOTS * SLOT, D)
    output, pullback = jax.vjp(forward, tokens, weights, vectors)
    masked_cotangent = cotangent * rows_valid.reshape(SLOTS * SLOT, 1).astype(jnp.float32)
    grad_tokens, grad_weights, grad_vectors = pullback(masked_cotangent)
    correction = 1.0 - 0.5 ** STEP
    new_first = 0.5 * moment1 + 0.5 * grad_weights
    new_second = 0.5 * moment2 + 0.5 * grad_weights * grad_weights
    update = new_first / correction / (jnp.sqrt(new_second / correction) + 1e-06) + 0.01 * weights
    column_edges = (0, 3 * D, 4 * D, 8 * D, 12 * D)
    pair_rows = []
    for group_index in range(4):
        start_col = column_edges[group_index]
        stop_col = column_edges[group_index + 1]
        weight_part = weights[:, start_col:stop_col]
        update_part = update[:, start_col:stop_col]
        pair_rows.append(jnp.stack([jnp.sqrt(jnp.sum(weight_part * weight_part)), jnp.sqrt(jnp.sum(update_part * update_part))]))
    norm_pairs = jnp.stack(pair_rows)
    trust_ratio = norm_pairs[:, 0] / (norm_pairs[:, 1] + 1e-06)
    column_trust = jnp.concatenate([jnp.ones((column_edges[group_index + 1] - column_edges[group_index],), jnp.float32) * trust_ratio[group_index] for group_index in range(4)])
    new_weights = weights - 0.3 * column_trust * update
    vec_first = 0.5 * vec_moment1 + 0.5 * grad_vectors
    vec_second = 0.5 * vec_moment2 + 0.5 * grad_vectors * grad_vectors
    new_vectors = vectors - 0.3 * (vec_first / correction) / (jnp.sqrt(vec_second / correction) + 1e-06)
    return (output, grad_tokens, new_first, new_second, new_weights, vec_first, vec_second, new_vectors, norm_pairs, trust_ratio)
```

```python
import jax
import jax.numpy as jnp
from jax import lax
from jax.experimental import pallas as pl
from jax.experimental.pallas import tpu as pltpu
from jax.sharding import PartitionSpec as P

HEADS = 12
SLOT = 288
QLEN = 64
STEP = 5


def norm_forward(values, gain, shift):
    centred = values - jnp.mean(values, axis=-1, keepdims=True)
    inverse = lax.rsqrt(jnp.mean(centred * centred, axis=-1, keepdims=True) + 1e-05)
    normed = centred * inverse
    return (normed * gain + shift, normed, inverse)


def norm_backward(grad_result, normed, inverse, gain):
    scaled = grad_result * gain
    grad_gain = jnp.sum(grad_result * normed, axis=0)
    grad_shift = jnp.sum(grad_result, axis=0)
    centred = scaled - jnp.mean(scaled, axis=-1, keepdims=True)
    grad_input = inverse * (centred - normed * jnp.mean(scaled * normed, axis=-1, keepdims=True))
    return (grad_input, grad_gain, grad_shift)


def gelu_slope(values):
    return (
        0.5 * (1.0 + jax.scipy.special.erf(values * 0.7071067811865476))
        + values * jnp.exp(-0.5 * values * values) * 0.3989422804014327
    )


def plain(
    tokens,
    cotangent,
    lengths,
    null_flags,
    weights,
    moment1,
    moment2,
    vectors,
    vec_moment1,
    vec_moment2,
):
    model_width = tokens.shape[1]
    row_count = tokens.shape[0]
    slot_count = lengths.shape[0]
    head_size = model_width // HEADS
    score_scale = head_size ** (-0.5)
    block_slots = min(2, slot_count)
    block_count = slot_count // block_slots
    valid_len = jnp.where(null_flags == 1, QLEN, lengths)
    key_valid = jnp.arange(SLOT, dtype=jnp.int32)[None, :] < valid_len[:, None]
    key_blocks = key_valid.reshape(block_count, block_slots, SLOT)
    row_weight = key_valid.reshape(row_count, 1).astype(jnp.float32)
    qkv_bias = jnp.concatenate([vectors[0], jnp.zeros((model_width,), jnp.float32), vectors[1]])
    ffn_bias = vectors[8:12].reshape(4 * model_width)
    token_low = tokens.astype(jnp.bfloat16)

    def block_scores(qkv_block, valid_keys):
        scores = (
            jnp.einsum(
                "bqhd,bkhd->bhqk",
                qkv_block[:, :, 0],
                qkv_block[:, :, 1],
                preferred_element_type=jnp.float32,
            )
            * score_scale
        )
        return jnp.where(valid_keys[:, None, None, :], scores, -1000000000.0)

    def attend_block(packed):
        qkv_block, valid_keys = packed
        scores = block_scores(qkv_block, valid_keys)
        row_top = jnp.max(scores, axis=-1, keepdims=True)
        exponent = jnp.exp(scores - row_top)
        row_total = jnp.sum(exponent, axis=-1, keepdims=True)
        softmax_out = (exponent / row_total).astype(jnp.bfloat16)
        context = jnp.einsum(
            "bhqk,bkhd->bqhd", softmax_out, qkv_block[:, :, 2], preferred_element_type=jnp.float32
        )
        return (context.astype(jnp.bfloat16), (row_top + jnp.log(row_total))[..., 0])

    def attend_back(packed):
        qkv_block, valid_keys, log_block, grad_block = packed
        scores = block_scores(qkv_block, valid_keys)
        softmax_out = jnp.exp(scores - log_block[..., None])
        grad_values = jnp.einsum(
            "bhqk,bqhd->bkhd",
            softmax_out.astype(jnp.bfloat16),
            grad_block,
            preferred_element_type=jnp.float32,
        )
        grad_soft = jnp.einsum(
            "bqhd,bkhd->bhqk", grad_block, qkv_block[:, :, 2], preferred_element_type=jnp.float32
        )
        grad_scores = softmax_out * (
            grad_soft - jnp.sum(grad_soft * softmax_out, axis=-1, keepdims=True)
        )
        scores_low = grad_scores.astype(jnp.bfloat16)
        grad_query = (
            jnp.einsum(
                "bhqk,bkhd->bqhd",
                scores_low,
                qkv_block[:, :, 1],
                preferred_element_type=jnp.float32,
            )
            * score_scale
        )
        grad_keys = (
            jnp.einsum(
                "bhqk,bqhd->bkhd",
                scores_low,
                qkv_block[:, :, 0],
                preferred_element_type=jnp.float32,
            )
            * score_scale
        )
        return jnp.stack([grad_query, grad_keys, grad_values], axis=2).astype(jnp.bfloat16)

    gathered = lax.all_gather(weights.astype(jnp.bfloat16), ("dp", "shard"), axis=0, tiled=True)
    first_mats = (
        gathered[:, : 3 * model_width],
        gathered[:, 3 * model_width : 4 * model_width],
        gathered[:, 4 * model_width : 8 * model_width],
        gathered[:, 8 * model_width :].reshape(4 * model_width, model_width),
    )
    w_qkv, w_out, w_in, w_down = first_mats
    qkv_low = (jnp.dot(token_low, w_qkv, preferred_element_type=jnp.float32) + qkv_bias).astype(
        jnp.bfloat16
    )
    qkv_blocks = qkv_low.reshape(block_count, block_slots, SLOT, 3, HEADS, head_size)
    contexts, log_total = lax.map(attend_block, (qkv_blocks, key_blocks))
    context_low = contexts.reshape(row_count, model_width)
    attention = jnp.dot(context_low, w_out, preferred_element_type=jnp.float32) + vectors[2]
    hidden_one, normed_one, inverse_one = norm_forward(tokens + attention, vectors[3], vectors[4])
    hidden_low = hidden_one.astype(jnp.bfloat16)
    pre_act = jnp.dot(hidden_low, w_in, preferred_element_type=jnp.float32) + ffn_bias
    act_low = jax.nn.gelu(pre_act, approximate=False).astype(jnp.bfloat16)
    ffn_out = jnp.dot(act_low, w_down, preferred_element_type=jnp.float32) + vectors[5]
    result, normed_two, inverse_two = norm_forward(hidden_one + ffn_out, vectors[6], vectors[7])
    first_kept = (
        qkv_blocks,
        log_total,
        context_low,
        normed_one,
        inverse_one,
        hidden_low,
        pre_act,
        act_low,
        normed_two,
        inverse_two,
        result,
    )
    output = first_kept[10]
    w_qkv, w_out, w_in, w_down = first_mats
    (
        qkv_blocks,
        log_total,
        context_low,
        normed_one,
        inverse_one,
        hidden_low,
        pre_act,
        act_low,
        normed_two,
        inverse_two,
    ) = first_kept[:10]
    grad_result = cotangent * row_weight
    grad_two, grad_gain_two, grad_shift_two = norm_backward(
        grad_result, normed_two, inverse_two, vectors[6]
    )
    grad_ffn_low = grad_two.astype(jnp.bfloat16)
    grad_bias_down = jnp.sum(grad_ffn_low, axis=0, dtype=jnp.float32)
    grad_down = jnp.einsum("tf,td->fd", act_low, grad_ffn_low, preferred_element_type=jnp.float32)
    grad_act = jnp.einsum("td,fd->tf", grad_ffn_low, w_down, preferred_element_type=jnp.float32)
    grad_pre_low = (grad_act * gelu_slope(pre_act)).astype(jnp.bfloat16)
    grad_bias_in = jnp.sum(grad_pre_low, axis=0, dtype=jnp.float32)
    grad_in = jnp.einsum("td,tf->df", hidden_low, grad_pre_low, preferred_element_type=jnp.float32)
    grad_hidden = grad_two + jnp.einsum(
        "tf,df->td", grad_pre_low, w_in, preferred_element_type=jnp.float32
    )
    grad_residual, grad_gain_one, grad_shift_one = norm_backward(
        grad_hidden, normed_one, inverse_one, vectors[3]
    )
    grad_attn_low = grad_residual.astype(jnp.bfloat16)
    grad_bias_out = jnp.sum(grad_attn_low, axis=0, dtype=jnp.float32)
    grad_out = jnp.einsum(
        "tc,td->cd", context_low, grad_attn_low, preferred_element_type=jnp.float32
    )
    grad_context = jnp.einsum(
        "td,cd->tc", grad_attn_low, w_out, preferred_element_type=jnp.float32
    ).astype(jnp.bfloat16)
    grad_blocks = grad_context.reshape(block_count, block_slots, SLOT, HEADS, head_size)
    grad_qkv_low = lax.map(attend_back, (qkv_blocks, key_blocks, log_total, grad_blocks)).reshape(
        row_count, 3 * model_width
    )
    grad_bias_qkv = jnp.sum(grad_qkv_low, axis=0, dtype=jnp.float32)
    grad_qkv = jnp.einsum("td,te->de", token_low, grad_qkv_low, preferred_element_type=jnp.float32)
    input_grad = grad_residual + jnp.einsum(
        "te,de->td", grad_qkv_low, w_qkv, preferred_element_type=jnp.float32
    )
    vector_grad = jnp.concatenate(
        [
            jnp.stack(
                [
                    grad_bias_qkv[:model_width],
                    grad_bias_qkv[2 * model_width :],
                    grad_bias_out,
                    grad_gain_one,
                    grad_shift_one,
                    grad_bias_down,
                    grad_gain_two,
                    grad_shift_two,
                ]
            ),
            grad_bias_in.reshape(4, model_width),
        ],
        axis=0,
    )
    qkv_shard, out_shard, in_shard, down_shard = (
        lax.psum_scatter(grad_qkv, ("dp", "shard"), scatter_dimension=0, tiled=True),
        lax.psum_scatter(grad_out, ("dp", "shard"), scatter_dimension=0, tiled=True),
        lax.psum_scatter(grad_in, ("dp", "shard"), scatter_dimension=0, tiled=True),
        lax.psum_scatter(
            grad_down.reshape(model_width, 4 * model_width),
            ("dp", "shard"),
            scatter_dimension=0,
            tiled=True,
        ),
    )
    vector_total = lax.psum(vector_grad, ("dp", "shard"))
    grad_shard = jnp.concatenate([qkv_shard, out_shard, in_shard, down_shard], axis=1)
    correction = 1.0 - 0.5**STEP
    new_first = 0.5 * moment1 + 0.5 * grad_shard
    new_second = 0.5 * moment2 + 0.5 * grad_shard * grad_shard
    update = new_first / correction / (jnp.sqrt(new_second / correction) + 1e-06) + 0.01 * weights
    column_edges = (0, 3 * model_width, 4 * model_width, 8 * model_width, 12 * model_width)
    pair_rows = []
    for group_index in range(4):
        weight_part = weights[:, column_edges[group_index] : column_edges[group_index + 1]]
        update_part = update[:, column_edges[group_index] : column_edges[group_index + 1]]
        pair_rows.append(
            jnp.stack([jnp.sum(weight_part * weight_part), jnp.sum(update_part * update_part)])
        )
    pair_squares = jnp.stack(pair_rows)
    pair_total = lax.psum(pair_squares, ("dp", "shard"))
    norm_pairs = jnp.sqrt(pair_total)
    trust_ratio = norm_pairs[:, 0] / (norm_pairs[:, 1] + 1e-06)
    column_trust = jnp.concatenate(
        [
            jnp.ones((column_edges[group_index + 1] - column_edges[group_index],), jnp.float32)
            * trust_ratio[group_index]
            for group_index in range(4)
        ]
    )
    new_weights = weights - 0.3 * column_trust * update
    vec_first = 0.5 * vec_moment1 + 0.5 * vector_total
    vec_second = 0.5 * vec_moment2 + 0.5 * vector_total * vector_total
    new_vectors = vectors - 0.3 * (vec_first / correction) / (
        jnp.sqrt(vec_second / correction) + 1e-06
    )
    return (
        output,
        input_grad,
        new_first,
        new_second,
        new_weights,
        vec_first,
        vec_second,
        new_vectors,
        norm_pairs,
        trust_ratio,
    )


SUM = jnp.float32
LOW = jnp.bfloat16
PIECES = 12
TILE = 768
HALF = 384
NEG = -1e9


def dot(left, right, left_dim, right_dim):
    return lax.dot_general(
        left, right, (((left_dim,), (right_dim,)), ((), ())), preferred_element_type=SUM
    )


def slot_rows(slot):
    return pl.ds(pl.multiple_of(slot * SLOT, SLOT), SLOT)


def each(count, body):
    def step(index, carry):
        body(index)
        return carry

    lax.fori_loop(0, count, step, 0)


def mean_lanes(values):
    return jnp.mean(values, axis=-1, keepdims=True)


def sum_rows(values):
    return jnp.sum(values, axis=0, keepdims=True)


def head_operands(query, key, valid):
    lane = lax.broadcasted_iota(jnp.int32, query.shape, 1)
    row = lax.broadcasted_iota(jnp.int32, query.shape, 0)
    low_head = lane < 64
    bias = jnp.where(row < valid, 0.0, NEG).astype(LOW)
    scaled = query * jnp.asarray(0.125, LOW)
    one, zero = jnp.ones_like(query), jnp.zeros_like(query)
    queries = (
        jnp.where(low_head, scaled, jnp.where(lane == 64, one, zero)),
        jnp.where(low_head, jnp.where(lane == 0, one, zero), scaled),
    )
    keys = (
        jnp.where(low_head, key, jnp.where(lane == 64, bias, zero)),
        jnp.where(low_head, jnp.where(lane == 0, bias, zero), key),
    )
    return queries, keys, low_head


def attend(unit, slot, valid, qkv, context, log_total):
    rows = slot_rows(slot)
    items = []
    for half in range(2):
        query, key, value = (
            qkv[unit, rows, (3 * half + part) * 128 : (3 * half + part + 1) * 128]
            for part in range(3)
        )
        queries, keys, low_head = head_operands(query, key, valid)
        items += [(queries[head], keys[head], value) for head in range(2)]
    scores = [dot(key, query, 1, 1) for query, key, _ in items]
    results = []
    for index, values in enumerate(scores):
        top = jnp.max(values, axis=0, keepdims=True)
        exponent = jnp.exp(values - top)
        total = sum_rows(exponent)
        log_total[unit, slot, index : index + 1, :] = top + jnp.log(total)
        results.append((exponent * (1.0 / total)).astype(LOW))
    results = [dot(probs, item[2], 0, 0) for probs, item in zip(results, items)]
    for half in range(2):
        lanes = pl.ds(pl.multiple_of((unit + 3 * half) * 128, 128), 128)
        joined = jnp.where(low_head, results[2 * half], results[2 * half + 1])
        context[rows, lanes] = joined.astype(LOW)


def attend_back(unit, slot, valid, qkv, grad_context, log_total, vec_grad):
    rows = slot_rows(slot)
    items = []
    for half in range(2):
        query, key, value = (
            qkv[unit, rows, (3 * half + part) * 128 : (3 * half + part + 1) * 128]
            for part in range(3)
        )
        lanes = pl.ds(pl.multiple_of((unit + 3 * half) * 128, 128), 128)
        grad = grad_context[rows, lanes]
        queries, keys, low_head = head_operands(query, key, valid)
        zero = jnp.zeros_like(grad)
        grads = (jnp.where(low_head, grad, zero), jnp.where(low_head, zero, grad))
        items += [
            (queries[head], keys[head], grads[head], query, key, value, grad) for head in range(2)
        ]
    scores = [dot(item[1], item[0], 1, 1) for item in items]
    grad_probs = [dot(item[5], item[2], 1, 1) for item in items]
    probs, grad_value = [], []
    for index, item in enumerate(items):
        probs.append(jnp.exp(scores[index] - log_total[unit, slot, index : index + 1, :]))
        grad_value.append(dot(probs[index].astype(LOW), item[6], 1, 0))
    grad_key, grad_query = [], []
    for index, item in enumerate(items):
        inner = sum_rows(grad_probs[index] * probs[index])
        low = (probs[index] * (grad_probs[index] - inner)).astype(LOW)
        grad_key.append(dot(low, item[3], 1, 0))
        grad_query.append(dot(low, item[4], 0, 0))
    for half in range(2):
        first, second = 2 * half, 2 * half + 1
        lanes = pl.ds(pl.multiple_of((unit + 3 * half) * 128, 128), 128)
        for part, parts, scale in (
            (0, grad_query, 0.125),
            (1, grad_key, 0.125),
            (2, grad_value, 1.0),
        ):
            joined = (jnp.where(low_head, parts[first], parts[second]) * scale).astype(LOW)
            qkv[unit, rows, (3 * half + part) * 128 : (3 * half + part + 1) * 128] = joined
            if part != 1:
                row = part // 2
                vec_grad[row : row + 1, lanes] += sum_rows(joined.astype(SUM))


def layer(
    valid, tokens, cotangent, walls, vectors, qkv_bias, ffn_bias,
    output, input_grad, pieces, vec_grad,
    normed, token_low, qkv, context, hidden_low, act, slope, grad, grad_low, side, inverse,
    log_total, mat, mat_low, in_sem, out_sem, mat_sem,
):
    def weight(piece):
        return walls[piece]

    cot_copy = pltpu.make_async_copy(cotangent, side, in_sem.at[0])
    cot_copy.start()
    tok_copy = pltpu.make_async_copy(tokens, normed, in_sem.at[1])
    tok_copy.start()
    tok_copy.wait()
    vec_grad[...] = jnp.zeros_like(vec_grad)

    def cast_slot(slot):
        rows = slot_rows(slot)
        token_low[rows, :] = normed[rows, :].astype(LOW)

    each(4, cast_slot)

    def project(unit):
        def project_slot(slot):
            rows = slot_rows(slot)
            values = dot(token_low[rows, :], weight(unit), 1, 0) + qkv_bias[unit]
            qkv[unit, rows, :] = values.astype(LOW)

        each(4, project_slot)
        each(4, lambda slot: attend(unit, slot, valid[slot], qkv, context, log_total))

    each(3, project)

    def attend_out(slot):
        rows = slot_rows(slot)
        values = normed[rows, :] + (dot(context[rows, :], weight(3), 1, 0) + vectors[2:3, :])
        centred = values - mean_lanes(values)
        inv = lax.rsqrt(mean_lanes(centred * centred) + 1e-05)
        unit_values = centred * inv
        normed[rows, :] = unit_values
        inverse[rows, :] = jnp.broadcast_to(inv, (SLOT, 128))
        hidden_low[rows, :] = (unit_values * vectors[3:4, :] + vectors[4:5, :]).astype(LOW)

    each(4, attend_out)

    def widen(chunk):
        def widen_slot(slot):
            rows = slot_rows(slot)
            pre = dot(hidden_low[rows, :], weight(4 + chunk), 1, 0) + ffn_bias[chunk]
            phi = 0.5 + 0.5 * lax.erf(pre * 0.7071067811865476)
            act[chunk, rows, :] = (pre * phi).astype(LOW)
            bell = jnp.exp(pre * pre * -0.5) * 0.3989422804014327
            slope[chunk, rows, :] = (phi + pre * bell).astype(LOW)

        each(4, widen_slot)

    each(4, widen)
    cot_copy.wait()

    def narrow(slot):
        rows = slot_rows(slot)
        ffn = dot(act[0, rows, :], weight(8), 1, 0)
        for chunk in range(1, 4):
            ffn += dot(act[chunk, rows, :], weight(8 + chunk), 1, 0)
        hidden = normed[rows, :] * vectors[3:4, :] + vectors[4:5, :]
        values = hidden + (ffn + vectors[5:6, :])
        centred = values - mean_lanes(values)
        inv = lax.rsqrt(mean_lanes(centred * centred) + 1e-05)
        unit_values = centred * inv
        kept = lax.broadcasted_iota(jnp.int32, (SLOT, 1), 0) < valid[slot]
        grad_out = jnp.where(kept, side[rows, :], 0.0)
        side[rows, :] = unit_values * vectors[6:7, :] + vectors[7:8, :]
        pltpu.make_async_copy(side.at[rows, :], output.at[rows, :], out_sem.at[slot]).start()
        vec_grad[6:7, :] += sum_rows(grad_out * unit_values)
        vec_grad[7:8, :] += sum_rows(grad_out)
        scaled = grad_out * vectors[6:7, :]
        result = inv * (
            scaled - mean_lanes(scaled) - unit_values * mean_lanes(scaled * unit_values)
        )
        grad[rows, :] = result
        low = result.astype(LOW)
        grad_low[rows, :] = low
        vec_grad[5:6, :] += sum_rows(low.astype(SUM))

    each(4, narrow)

    def piece_copy(index, piece):
        slot = lax.rem(index, 2)
        return pltpu.make_async_copy(mat_low.at[slot], pieces.at[piece], mat_sem.at[slot])

    def emit(index, piece, left, right):
        values = dot(left, right, 0, 0)

        @pl.when(index >= 2)
        def _():
            piece_copy(index, piece).wait()

        mat_low[lax.rem(index, 2)] = values.astype(LOW)
        piece_copy(index, piece).start()

    def back_chunk(chunk):
        emit(2 * chunk, 8 + chunk, act[chunk], grad_low[...])

        def back_slot(slot):
            rows = slot_rows(slot)
            values = dot(grad_low[rows, :], weight(8 + chunk), 1, 1)
            low = (values * slope[chunk, rows, :].astype(SUM)).astype(LOW)
            slope[chunk, rows, :] = low
            row = pl.ds(8 + chunk, 1)
            vec_grad[row, :] += sum_rows(low.astype(SUM))

        each(4, back_slot)
        emit(2 * chunk + 1, 4 + chunk, hidden_low[...], slope[chunk])

    each(4, back_chunk)

    def back_norm(slot):
        rows = slot_rows(slot)
        total = grad[rows, :]
        for chunk in range(4):
            total += dot(slope[chunk, rows, :], weight(4 + chunk), 1, 1)
        unit_values = normed[rows, :]
        vec_grad[3:4, :] += sum_rows(total * unit_values)
        vec_grad[4:5, :] += sum_rows(total)
        scaled = total * vectors[3:4, :]
        inv = inverse[rows, 0:1]
        result = inv * (
            scaled - mean_lanes(scaled) - unit_values * mean_lanes(scaled * unit_values)
        )
        grad[rows, :] = result
        low = result.astype(LOW)
        grad_low[rows, :] = low
        vec_grad[2:3, :] += sum_rows(low.astype(SUM))

    each(4, back_norm)
    emit(8, 3, context[...], grad_low[...])

    def back_context(slot):
        rows = slot_rows(slot)
        context[rows, :] = dot(grad_low[rows, :], weight(3), 1, 1).astype(LOW)

    each(4, back_context)

    def back_unit(unit):
        each(
            4,
            lambda slot: attend_back(unit, slot, valid[slot], qkv, context, log_total, vec_grad),
        )
        emit(9 + unit, unit, token_low[...], qkv[unit])

    each(3, back_unit)

    def back_tokens(slot):
        rows = slot_rows(slot)
        pltpu.make_async_copy(side.at[rows, :], output.at[rows, :], out_sem.at[slot]).wait()
        total = grad[rows, :]
        for unit in range(3):
            total += dot(qkv[unit, rows, :], weight(unit), 1, 1)
        side[rows, :] = total
        pltpu.make_async_copy(side.at[rows, :], input_grad.at[rows, :], out_sem.at[slot]).start()

    each(4, back_tokens)
    for slot in range(4):
        rows = slot_rows(slot)
        pltpu.make_async_copy(side.at[rows, :], input_grad.at[rows, :], out_sem.at[slot]).wait()
    piece_copy(10, 0).wait()
    piece_copy(11, 0).wait()


def permute_columns(shard):
    rows = shard.shape[0]
    first = shard[:, :2304].reshape(rows, 3, 2, 3, 128).transpose(3, 0, 2, 1, 4)
    second = shard[:, 2304:3072].reshape(1, rows, TILE)
    third = shard[:, 3072:6144].reshape(rows, TILE, 4).transpose(2, 0, 1)
    fourth = shard[:, 6144:].reshape(rows, 4, TILE).transpose(1, 0, 2)
    return jnp.concatenate([first.reshape(3, rows, TILE), second, third, fourth], axis=0)


def restore_columns(pieces):
    rows = pieces.shape[1]
    first = pieces[:3].reshape(3, rows, 2, 3, 128).transpose(1, 3, 2, 0, 4)
    third = pieces[4:8].transpose(1, 2, 0)
    fourth = pieces[8:].transpose(1, 0, 2)
    return jnp.concatenate(
        [
            first.reshape(rows, 2304),
            pieces[3],
            third.reshape(rows, 3072),
            fourth.reshape(rows, 3072),
        ],
        axis=1,
    )


def run_layer(tokens, cotangent, valid, walls, vectors):
    rows = tokens.shape[0]
    zero = jnp.zeros((TILE,), SUM)
    qkv_bias = jnp.stack([vectors[0], zero, vectors[1]]).reshape(3, 2, 3, 128)
    qkv_bias = qkv_bias.transpose(2, 1, 0, 3).reshape(3, 1, TILE)
    ffn_bias = vectors[8:12].reshape(TILE, 4).T.reshape(4, 1, TILE)
    vmem = pl.BlockSpec(memory_space=pltpu.VMEM)
    smem = pl.BlockSpec(memory_space=pltpu.SMEM)
    hbm = pl.BlockSpec(memory_space=pl.ANY)
    full = lambda *shape: pltpu.VMEM(shape, SUM)
    low = lambda *shape: pltpu.VMEM(shape, LOW)
    return pl.pallas_call(
        layer,
        out_shape=[
            jax.ShapeDtypeStruct((rows, TILE), SUM),
            jax.ShapeDtypeStruct((rows, TILE), SUM),
            jax.ShapeDtypeStruct((PIECES, TILE, TILE), LOW),
            jax.ShapeDtypeStruct((16, TILE), SUM),
        ],
        in_specs=[smem, hbm, hbm, vmem, vmem, vmem, vmem],
        out_specs=[hbm, hbm, hbm, vmem],
        scratch_shapes=[
            full(rows, TILE),
            low(rows, TILE),
            low(3, rows, TILE),
            low(rows, TILE),
            low(rows, TILE),
            low(4, rows, TILE),
            low(4, rows, TILE),
            full(rows, TILE),
            low(rows, TILE),
            full(rows, TILE),
            full(rows, 128),
            full(3, 4, 4, SLOT),
            full(8, 128),
            low(2, TILE, TILE),
            pltpu.SemaphoreType.DMA((2,)),
            pltpu.SemaphoreType.DMA((4,)),
            pltpu.SemaphoreType.DMA((2,)),
        ],
        compiler_params=pltpu.CompilerParams(vmem_limit_bytes=63 * 2**20),
        cost_estimate=pl.CostEstimate(
            flops=60 * 10**9, bytes_accessed=60 * 10**6, transcendentals=10**7
        ),
    )(valid, tokens, cotangent, walls, vectors, qkv_bias, ffn_bias)


def fused(
    tokens,
    cotangent,
    lengths,
    null_flags,
    weights,
    moment1,
    moment2,
    vectors,
    vec_moment1,
    vec_moment2,
):
    axes = ("dp", "shard")
    valid = jnp.where(null_flags == 1, QLEN, lengths).astype(jnp.int32)
    low = permute_columns(weights.astype(LOW))
    walls = lax.all_gather(low, axes, axis=1, tiled=True)
    output, input_grad, pieces, vec_grad = run_layer(tokens, cotangent, valid, walls, vectors)
    shard = lax.psum_scatter(pieces, axes, scatter_dimension=1, tiled=True)
    grad_shard = restore_columns(shard.astype(SUM))
    vec_total = lax.psum(vec_grad, axes)
    ffn_rows = vec_total[8:12].T.reshape(4, TILE)
    vec_total = jnp.concatenate([vec_total[:8], ffn_rows], axis=0)
    return (output, input_grad) + optimize(
        grad_shard, vec_total, weights, moment1, moment2, vectors, vec_moment1, vec_moment2
    )


def optimize(
    grad_shard, vec_total, weights, moment1, moment2, vectors, vec_moment1, vec_moment2
):
    correction = 1.0 - 0.5**STEP
    new_first = 0.5 * moment1 + 0.5 * grad_shard
    new_second = 0.5 * moment2 + 0.5 * grad_shard * grad_shard
    update = new_first / correction / (jnp.sqrt(new_second / correction) + 1e-06) + 0.01 * weights
    edges = (0, 2304, 3072, 6144, 9216)
    squares = jnp.stack(
        [
            jnp.stack(
                [
                    jnp.sum(jnp.square(values[:, edges[index] : edges[index + 1]]))
                    for values in (weights, update)
                ]
            )
            for index in range(4)
        ]
    )
    norm_pairs = jnp.sqrt(lax.psum(squares, ("dp", "shard")))
    trust = norm_pairs[:, 0] / (norm_pairs[:, 1] + 1e-06)
    column = jnp.arange(weights.shape[1])
    column_trust = jnp.where(
        column < edges[1],
        trust[0],
        jnp.where(column < edges[2], trust[1], jnp.where(column < edges[3], trust[2], trust[3])),
    )
    new_weights = weights - 0.3 * column_trust * update
    vec_first = 0.5 * vec_moment1 + 0.5 * vec_total
    vec_second = 0.5 * vec_moment2 + 0.5 * vec_total * vec_total
    new_vectors = vectors - 0.3 * (vec_first / correction) / (
        jnp.sqrt(vec_second / correction) + 1e-06
    )
    return (
        new_first,
        new_second,
        new_weights,
        vec_first,
        vec_second,
        new_vectors,
        norm_pairs,
        trust,
    )


def solution(mesh):
    split = P(("dp", "shard"), None)
    flat = P(("dp", "shard"))
    in_specs = (split, split, flat, flat, split, split, split, P(), P(), P())
    out_specs = (split,) * 5 + (P(),) * 5
    body = fused if mesh.shape["dp"] == 8 and mesh.shape["shard"] == 4 else plain
    return jax.shard_map(body, mesh=mesh, in_specs=in_specs, out_specs=out_specs, check_vma=False)
```

```python
import jax
import jax.numpy as jnp
from jax import lax
from jax.experimental import pallas as pl
from jax.experimental.pallas import tpu as pltpu
from jax.sharding import PartitionSpec as P

HEADS = 12
SLOT = 288
QLEN = 64
STEP = 5


def norm_forward(values, gain, shift):
    centred = values - jnp.mean(values, axis=-1, keepdims=True)
    inverse = lax.rsqrt(jnp.mean(centred * centred, axis=-1, keepdims=True) + 1e-05)
    normed = centred * inverse
    return (normed * gain + shift, normed, inverse)


def norm_backward(grad_result, normed, inverse, gain):
    scaled = grad_result * gain
    grad_gain = jnp.sum(grad_result * normed, axis=0)
    grad_shift = jnp.sum(grad_result, axis=0)
    centred = scaled - jnp.mean(scaled, axis=-1, keepdims=True)
    grad_input = inverse * (centred - normed * jnp.mean(scaled * normed, axis=-1, keepdims=True))
    return (grad_input, grad_gain, grad_shift)


def gelu_slope(values):
    return (
        0.5 * (1.0 + jax.scipy.special.erf(values * 0.7071067811865476))
        + values * jnp.exp(-0.5 * values * values) * 0.3989422804014327
    )


def plain(
    tokens,
    cotangent,
    lengths,
    null_flags,
    weights,
    moment1,
    moment2,
    vectors,
    vec_moment1,
    vec_moment2,
):
    model_width = tokens.shape[1]
    row_count = tokens.shape[0]
    slot_count = lengths.shape[0]
    head_size = model_width // HEADS
    score_scale = head_size ** (-0.5)
    block_slots = min(2, slot_count)
    block_count = slot_count // block_slots
    valid_len = jnp.where(null_flags == 1, QLEN, lengths)
    key_valid = jnp.arange(SLOT, dtype=jnp.int32)[None, :] < valid_len[:, None]
    key_blocks = key_valid.reshape(block_count, block_slots, SLOT)
    row_weight = key_valid.reshape(row_count, 1).astype(jnp.float32)
    qkv_bias = jnp.concatenate([vectors[0], jnp.zeros((model_width,), jnp.float32), vectors[1]])
    ffn_bias = vectors[8:12].reshape(4 * model_width)
    token_low = tokens.astype(jnp.bfloat16)

    def block_scores(qkv_block, valid_keys):
        scores = (
            jnp.einsum(
                "bqhd,bkhd->bhqk",
                qkv_block[:, :, 0],
                qkv_block[:, :, 1],
                preferred_element_type=jnp.float32,
            )
            * score_scale
        )
        return jnp.where(valid_keys[:, None, None, :], scores, -1000000000.0)

    def attend_block(packed):
        qkv_block, valid_keys = packed
        scores = block_scores(qkv_block, valid_keys)
        row_top = jnp.max(scores, axis=-1, keepdims=True)
        exponent = jnp.exp(scores - row_top)
        row_total = jnp.sum(exponent, axis=-1, keepdims=True)
        softmax_out = (exponent / row_total).astype(jnp.bfloat16)
        context = jnp.einsum(
            "bhqk,bkhd->bqhd", softmax_out, qkv_block[:, :, 2], preferred_element_type=jnp.float32
        )
        return (context.astype(jnp.bfloat16), (row_top + jnp.log(row_total))[..., 0])

    def attend_back(packed):
        qkv_block, valid_keys, log_block, grad_block = packed
        scores = block_scores(qkv_block, valid_keys)
        softmax_out = jnp.exp(scores - log_block[..., None])
        grad_values = jnp.einsum(
            "bhqk,bqhd->bkhd",
            softmax_out.astype(jnp.bfloat16),
            grad_block,
            preferred_element_type=jnp.float32,
        )
        grad_soft = jnp.einsum(
            "bqhd,bkhd->bhqk", grad_block, qkv_block[:, :, 2], preferred_element_type=jnp.float32
        )
        grad_scores = softmax_out * (
            grad_soft - jnp.sum(grad_soft * softmax_out, axis=-1, keepdims=True)
        )
        scores_low = grad_scores.astype(jnp.bfloat16)
        grad_query = (
            jnp.einsum(
                "bhqk,bkhd->bqhd",
                scores_low,
                qkv_block[:, :, 1],
                preferred_element_type=jnp.float32,
            )
            * score_scale
        )
        grad_keys = (
            jnp.einsum(
                "bhqk,bqhd->bkhd",
                scores_low,
                qkv_block[:, :, 0],
                preferred_element_type=jnp.float32,
            )
            * score_scale
        )
        return jnp.stack([grad_query, grad_keys, grad_values], axis=2).astype(jnp.bfloat16)

    gathered = lax.all_gather(weights.astype(jnp.bfloat16), ("dp", "shard"), axis=0, tiled=True)
    first_mats = (
        gathered[:, : 3 * model_width],
        gathered[:, 3 * model_width : 4 * model_width],
        gathered[:, 4 * model_width : 8 * model_width],
        gathered[:, 8 * model_width :].reshape(4 * model_width, model_width),
    )
    w_qkv, w_out, w_in, w_down = first_mats
    qkv_low = (jnp.dot(token_low, w_qkv, preferred_element_type=jnp.float32) + qkv_bias).astype(
        jnp.bfloat16
    )
    qkv_blocks = qkv_low.reshape(block_count, block_slots, SLOT, 3, HEADS, head_size)
    contexts, log_total = lax.map(attend_block, (qkv_blocks, key_blocks))
    context_low = contexts.reshape(row_count, model_width)
    attention = jnp.dot(context_low, w_out, preferred_element_type=jnp.float32) + vectors[2]
    hidden_one, normed_one, inverse_one = norm_forward(tokens + attention, vectors[3], vectors[4])
    hidden_low = hidden_one.astype(jnp.bfloat16)
    pre_act = jnp.dot(hidden_low, w_in, preferred_element_type=jnp.float32) + ffn_bias
    act_low = jax.nn.gelu(pre_act, approximate=False).astype(jnp.bfloat16)
    ffn_out = jnp.dot(act_low, w_down, preferred_element_type=jnp.float32) + vectors[5]
    result, normed_two, inverse_two = norm_forward(hidden_one + ffn_out, vectors[6], vectors[7])
    first_kept = (
        qkv_blocks,
        log_total,
        context_low,
        normed_one,
        inverse_one,
        hidden_low,
        pre_act,
        act_low,
        normed_two,
        inverse_two,
        result,
    )
    output = first_kept[10]
    w_qkv, w_out, w_in, w_down = first_mats
    (
        qkv_blocks,
        log_total,
        context_low,
        normed_one,
        inverse_one,
        hidden_low,
        pre_act,
        act_low,
        normed_two,
        inverse_two,
    ) = first_kept[:10]
    grad_result = cotangent * row_weight
    grad_two, grad_gain_two, grad_shift_two = norm_backward(
        grad_result, normed_two, inverse_two, vectors[6]
    )
    grad_ffn_low = grad_two.astype(jnp.bfloat16)
    grad_bias_down = jnp.sum(grad_ffn_low, axis=0, dtype=jnp.float32)
    grad_down = jnp.einsum("tf,td->fd", act_low, grad_ffn_low, preferred_element_type=jnp.float32)
    grad_act = jnp.einsum("td,fd->tf", grad_ffn_low, w_down, preferred_element_type=jnp.float32)
    grad_pre_low = (grad_act * gelu_slope(pre_act)).astype(jnp.bfloat16)
    grad_bias_in = jnp.sum(grad_pre_low, axis=0, dtype=jnp.float32)
    grad_in = jnp.einsum("td,tf->df", hidden_low, grad_pre_low, preferred_element_type=jnp.float32)
    grad_hidden = grad_two + jnp.einsum(
        "tf,df->td", grad_pre_low, w_in, preferred_element_type=jnp.float32
    )
    grad_residual, grad_gain_one, grad_shift_one = norm_backward(
        grad_hidden, normed_one, inverse_one, vectors[3]
    )
    grad_attn_low = grad_residual.astype(jnp.bfloat16)
    grad_bias_out = jnp.sum(grad_attn_low, axis=0, dtype=jnp.float32)
    grad_out = jnp.einsum(
        "tc,td->cd", context_low, grad_attn_low, preferred_element_type=jnp.float32
    )
    grad_context = jnp.einsum(
        "td,cd->tc", grad_attn_low, w_out, preferred_element_type=jnp.float32
    ).astype(jnp.bfloat16)
    grad_blocks = grad_context.reshape(block_count, block_slots, SLOT, HEADS, head_size)
    grad_qkv_low = lax.map(attend_back, (qkv_blocks, key_blocks, log_total, grad_blocks)).reshape(
        row_count, 3 * model_width
    )
    grad_bias_qkv = jnp.sum(grad_qkv_low, axis=0, dtype=jnp.float32)
    grad_qkv = jnp.einsum("td,te->de", token_low, grad_qkv_low, preferred_element_type=jnp.float32)
    input_grad = grad_residual + jnp.einsum(
        "te,de->td", grad_qkv_low, w_qkv, preferred_element_type=jnp.float32
    )
    vector_grad = jnp.concatenate(
        [
            jnp.stack(
                [
                    grad_bias_qkv[:model_width],
                    grad_bias_qkv[2 * model_width :],
                    grad_bias_out,
                    grad_gain_one,
                    grad_shift_one,
                    grad_bias_down,
                    grad_gain_two,
                    grad_shift_two,
                ]
            ),
            grad_bias_in.reshape(4, model_width),
        ],
        axis=0,
    )
    qkv_shard, out_shard, in_shard, down_shard = (
        lax.psum_scatter(grad_qkv, ("dp", "shard"), scatter_dimension=0, tiled=True),
        lax.psum_scatter(grad_out, ("dp", "shard"), scatter_dimension=0, tiled=True),
        lax.psum_scatter(grad_in, ("dp", "shard"), scatter_dimension=0, tiled=True),
        lax.psum_scatter(
            grad_down.reshape(model_width, 4 * model_width),
            ("dp", "shard"),
            scatter_dimension=0,
            tiled=True,
        ),
    )
    vector_total = lax.psum(vector_grad, ("dp", "shard"))
    grad_shard = jnp.concatenate([qkv_shard, out_shard, in_shard, down_shard], axis=1)
    correction = 1.0 - 0.5**STEP
    new_first = 0.5 * moment1 + 0.5 * grad_shard
    new_second = 0.5 * moment2 + 0.5 * grad_shard * grad_shard
    update = new_first / correction / (jnp.sqrt(new_second / correction) + 1e-06) + 0.01 * weights
    column_edges = (0, 3 * model_width, 4 * model_width, 8 * model_width, 12 * model_width)
    pair_rows = []
    for group_index in range(4):
        weight_part = weights[:, column_edges[group_index] : column_edges[group_index + 1]]
        update_part = update[:, column_edges[group_index] : column_edges[group_index + 1]]
        pair_rows.append(
            jnp.stack([jnp.sum(weight_part * weight_part), jnp.sum(update_part * update_part)])
        )
    pair_squares = jnp.stack(pair_rows)
    pair_total = lax.psum(pair_squares, ("dp", "shard"))
    norm_pairs = jnp.sqrt(pair_total)
    trust_ratio = norm_pairs[:, 0] / (norm_pairs[:, 1] + 1e-06)
    column_trust = jnp.concatenate(
        [
            jnp.ones((column_edges[group_index + 1] - column_edges[group_index],), jnp.float32)
            * trust_ratio[group_index]
            for group_index in range(4)
        ]
    )
    new_weights = weights - 0.3 * column_trust * update
    vec_first = 0.5 * vec_moment1 + 0.5 * vector_total
    vec_second = 0.5 * vec_moment2 + 0.5 * vector_total * vector_total
    new_vectors = vectors - 0.3 * (vec_first / correction) / (
        jnp.sqrt(vec_second / correction) + 1e-06
    )
    return (
        output,
        input_grad,
        new_first,
        new_second,
        new_weights,
        vec_first,
        vec_second,
        new_vectors,
        norm_pairs,
        trust_ratio,
    )


SUM = jnp.float32
LOW = jnp.bfloat16
PIECES = 12
TILE = 768
HALF = 384
NEG = -1e9


def dot(left, right, left_dim, right_dim):
    return lax.dot_general(
        left, right, (((left_dim,), (right_dim,)), ((), ())), preferred_element_type=SUM
    )


def slot_rows(slot):
    return pl.ds(pl.multiple_of(slot * SLOT, SLOT), SLOT)


def each(count, body):
    def step(index, carry):
        body(index)
        return carry

    lax.fori_loop(0, count, step, 0)


def mean_lanes(values):
    return jnp.mean(values, axis=-1, keepdims=True)


def sum_rows(values):
    return jnp.sum(values, axis=0, keepdims=True)


def head_operands(query, key, valid):
    lane = lax.broadcasted_iota(jnp.int32, query.shape, 1)
    row = lax.broadcasted_iota(jnp.int32, query.shape, 0)
    low_head = lane < 64
    bias = jnp.where(row < valid, 0.0, NEG).astype(LOW)
    scaled = query * jnp.asarray(0.125, LOW)
    one, zero = jnp.ones_like(query), jnp.zeros_like(query)
    queries = (
        jnp.where(low_head, scaled, jnp.where(lane == 64, one, zero)),
        jnp.where(low_head, jnp.where(lane == 0, one, zero), scaled),
    )
    keys = (
        jnp.where(low_head, key, jnp.where(lane == 64, bias, zero)),
        jnp.where(low_head, jnp.where(lane == 0, bias, zero), key),
    )
    return queries, keys, low_head


def attend(unit, slot, valid, qkv, context, log_total):
    rows = slot_rows(slot)
    items = []
    for half in range(2):
        query, key, value = (
            qkv[unit, rows, (3 * half + part) * 128 : (3 * half + part + 1) * 128]
            for part in range(3)
        )
        queries, keys, low_head = head_operands(query, key, valid)
        items += [(queries[head], keys[head], value) for head in range(2)]
    scores = [dot(key, query, 1, 1) for query, key, _ in items]
    results = []
    for index, values in enumerate(scores):
        top = jnp.max(values, axis=0, keepdims=True)
        exponent = jnp.exp(values - top)
        total = sum_rows(exponent)
        log_total[unit, slot, index : index + 1, :] = top + jnp.log(total)
        results.append((exponent * (1.0 / total)).astype(LOW))
    results = [dot(probs, item[2], 0, 0) for probs, item in zip(results, items)]
    for half in range(2):
        lanes = pl.ds(pl.multiple_of((unit + 3 * half) * 128, 128), 128)
        joined = jnp.where(low_head, results[2 * half], results[2 * half + 1])
        context[rows, lanes] = joined.astype(LOW)


def attend_back(unit, slot, valid, qkv, grad_context, log_total, vec_grad):
    rows = slot_rows(slot)
    for half in range(2):
        query, key, value = (
            qkv[unit, rows, (3 * half + part) * 128 : (3 * half + part + 1) * 128]
            for part in range(3)
        )
        lanes = pl.ds(pl.multiple_of((unit + 3 * half) * 128, 128), 128)
        grad = grad_context[rows, lanes]
        queries, keys, low_head = head_operands(query, key, valid)
        zero = jnp.zeros_like(grad)
        grads = (jnp.where(low_head, grad, zero), jnp.where(low_head, zero, grad))
        scores = [dot(keys[head], queries[head], 1, 1) for head in range(2)]
        grad_probs = [dot(value, grads[head], 1, 1) for head in range(2)]
        probs, grad_value = [], []
        for head in range(2):
            index = 2 * half + head
            probs.append(jnp.exp(scores[head] - log_total[unit, slot, index : index + 1, :]))
            grad_value.append(dot(probs[head].astype(LOW), grad, 1, 0))
        grad_key, grad_query = [], []
        for head in range(2):
            inner = sum_rows(grad_probs[head] * probs[head])
            low = (probs[head] * (grad_probs[head] - inner)).astype(LOW)
            grad_key.append(dot(low, query, 1, 0))
            grad_query.append(dot(low, key, 0, 0))
        for part, parts, scale in (
            (0, grad_query, 0.125),
            (1, grad_key, 0.125),
            (2, grad_value, 1.0),
        ):
            joined = (jnp.where(low_head, parts[0], parts[1]) * scale).astype(LOW)
            qkv[unit, rows, (3 * half + part) * 128 : (3 * half + part + 1) * 128] = joined
            if part != 1:
                row = part // 2
                vec_grad[row : row + 1, lanes] += sum_rows(joined.astype(SUM))


def place():
    outer, inner = lax.axis_index("dp"), lax.axis_index("shard")
    z, y, x, core = outer // 2, outer % 2, inner // 2, inner % 2
    here = dict(z=z, y=y, x=x, core=core, high=z // 2, low=z % 2)
    here["y1"], here["x1"] = y + core * (1 - 2 * y), x + (1 - core) * (1 - 2 * x)
    here["y2"], here["x2"] = y + (1 - core) * (1 - 2 * y), x + core * (1 - 2 * x)
    device = lambda z, y, x, core: (z * 2 + y, x * 2 + core)
    here["twin"] = device(z, y, x, 1 - core)
    here["near_z"] = device(z + 1 - 2 * (z % 2), y, x, core)
    here["far_z"] = device((z + 2) % 4, y, x, core)
    here["first"] = device(z, here["y1"], here["x1"], core)
    here["second"] = device(z, here["y2"], here["x2"], core)
    here["along_x"] = device(z, y, 1 - x, core)
    here["along_y"] = device(z, 1 - y, x, core)
    here["mine"] = pl.ds(pl.multiple_of(core * HALF, 128), HALF)
    here["other"] = pl.ds(pl.multiple_of((1 - core) * HALF, 128), HALF)
    return here


def send(source, target, sent, arrived, device):
    return pltpu.make_async_remote_copy(
        src_ref=source,
        dst_ref=target,
        send_sem=sent,
        recv_sem=arrived,
        device_id=device,
        device_id_type=pl.DeviceIdType.MESH,
    )


def inside(index):
    if isinstance(index, int):
        return 0 <= index < PIECES
    return jnp.logical_and(index >= 0, index < PIECES)


def guarded(index, body):
    if isinstance(index, int):
        if inside(index):
            body(index)
    else:
        pl.when(inside(index))(lambda: body(index))


def layer(
    valid, tokens, cotangent, shard, vectors, qkv_bias, ffn_bias,
    output, input_grad, grad_shard, vec_total,
    walls, normed, token_low, qkv, context, hidden_low, act, slope, grad, grad_low, side, inverse,
    log_total, vec_grad, mat, mat_send, mat_got, pair_keep, pair_send, pair_got,
    line_keep, line_send, line_got, two_keep, two_send, two_got, one_keep, one_send, one_got, rows48,
    shares, vec_got, in_sem, out_sem, twin_sem, gather_sent, gather_got, reduce_sent, reduce_got,
    share_sem, vec_sent, vec_arrived,
):
    here = place()
    z, y, x, core, high, low = (here[name] for name in ("z", "y", "x", "core", "high", "low"))
    y1, x1, y2, x2 = (here[name] for name in ("y1", "x1", "y2", "x2"))
    mine, other = here["mine"], here["other"]

    cot_copy = pltpu.make_async_copy(cotangent, side, in_sem.at[0])
    cot_copy.start()
    tok_copy = pltpu.make_async_copy(tokens, normed, in_sem.at[1])
    tok_copy.start()

    barrier = pltpu.get_barrier_semaphore()
    peers = ("twin", "near_z", "far_z", "along_x", "along_y")
    for name in peers:
        pl.semaphore_signal(
            barrier, inc=1, device_id=here[name], device_id_type=pl.DeviceIdType.MESH
        )
    pl.semaphore_wait(barrier, len(peers))

    swap = send(
        shard.at[:, :, other], shares.at[:, :, other], twin_sem.at[0], twin_sem.at[1], here["twin"]
    )
    swap.start()
    vec_grad[...] = jnp.zeros_like(vec_grad)
    swap.wait()

    def fill(piece):
        own, twin = shard[piece, :, mine], shares[piece, :, mine]
        upper = jnp.where(core == 0, own, twin)
        lower = jnp.where(core == 0, twin, own)
        joined = jnp.concatenate([upper, lower], axis=0)
        walls[piece, high, low, y, x, :, mine] = joined.astype(LOW)

    each(PIECES, fill)

    def gather_copy(piece, stage):
        if stage == 0:
            part, device = walls.at[piece, high, low, y, x, :, mine], here["far_z"]
        elif stage == 1:
            part, device = walls.at[piece, :, low, y, x, :, mine], here["near_z"]
        elif stage == 2:
            part, device = walls.at[piece, :, :, y, x, :, mine], here["first"]
        elif stage == 3:
            part, device = walls.at[piece, :, :, y, x, :, mine], here["second"]
        elif stage == 4:
            part, device = walls.at[piece, :, :, y1, x1, :, mine], here["second"]
        else:
            part, device = walls.at[piece, :, :, :, :, :, mine], here["twin"]
        return send(part, part, gather_sent.at[piece, stage], gather_got.at[piece, stage], device)

    def gather(notch):
        def begin(piece):
            gather_copy(piece, 0).start()

        def spread_line(piece):
            gather_copy(piece, 0).wait_recv()
            gather_copy(piece, 1).start()

        def spread_plane(piece):
            gather_copy(piece, 1).wait_recv()
            gather_copy(piece, 2).start()
            gather_copy(piece, 3).start()

        def pass_on(piece):
            gather_copy(piece, 2).wait_recv()
            gather_copy(piece, 4).start()

        def share(piece):
            gather_copy(piece, 3).wait_recv()
            gather_copy(piece, 4).wait_recv()
            gather_copy(piece, 5).start()

        def finish(piece):
            gather_copy(piece, 5).wait_recv()
            for stage in range(6):
                gather_copy(piece, stage).wait_send()

        for age, body in enumerate((begin, spread_line, spread_plane, pass_on, share, finish)):
            guarded(notch - age, body)

    def weight(piece):
        return walls[piece].reshape(TILE, TILE)

    for notch in range(3):
        gather(notch)
    tok_copy.wait()

    def cast_slot(slot):
        rows = slot_rows(slot)
        token_low[rows, :] = normed[rows, :].astype(LOW)

    each(4, cast_slot)
    for notch in range(3, 6):
        gather(notch)

    def project(unit):
        def project_slot(slot):
            rows = slot_rows(slot)
            values = dot(token_low[rows, :], weight(unit), 1, 0) + qkv_bias[unit]
            qkv[unit, rows, :] = values.astype(LOW)

        each(4, project_slot)
        gather(6 + unit)
        each(4, lambda slot: attend(unit, slot, valid[slot], qkv, context, log_total))

    each(3, project)

    def attend_out(slot):
        rows = slot_rows(slot)
        values = normed[rows, :] + (dot(context[rows, :], weight(3), 1, 0) + vectors[2:3, :])
        centred = values - mean_lanes(values)
        inv = lax.rsqrt(mean_lanes(centred * centred) + 1e-05)
        unit_values = centred * inv
        normed[rows, :] = unit_values
        inverse[rows, :] = jnp.broadcast_to(inv, (SLOT, 128))
        hidden_low[rows, :] = (unit_values * vectors[3:4, :] + vectors[4:5, :]).astype(LOW)

    each(4, attend_out)

    def widen(chunk):
        gather(9 + chunk)

        def widen_slot(slot):
            rows = slot_rows(slot)
            pre = dot(hidden_low[rows, :], weight(4 + chunk), 1, 0) + ffn_bias[chunk]
            phi = 0.5 + 0.5 * lax.erf(pre * 0.7071067811865476)
            act[chunk, rows, :] = (pre * phi).astype(LOW)
            bell = jnp.exp(pre * pre * -0.5) * 0.3989422804014327
            slope[chunk, rows, :] = (phi + pre * bell).astype(LOW)

        each(4, widen_slot)

    each(4, widen)
    cot_copy.wait()

    def clear_slot(slot):
        rows = slot_rows(slot)
        grad[rows, :] = normed[rows, :] * vectors[3:4, :] + (vectors[4:5, :] + vectors[5:6, :])

    each(4, clear_slot)

    def narrow(chunk):
        gather(13 + chunk)

        def narrow_slot(slot):
            rows = slot_rows(slot)
            grad[rows, :] += dot(act[chunk, rows, :], weight(8 + chunk), 1, 0)

        each(4, narrow_slot)

    each(3, narrow)
    gather(16)

    def finish_slot(slot):
        rows = slot_rows(slot)
        values = grad[rows, :] + dot(act[3, rows, :], weight(11), 1, 0)
        centred = values - mean_lanes(values)
        inv = lax.rsqrt(mean_lanes(centred * centred) + 1e-05)
        unit_values = centred * inv
        kept = lax.broadcasted_iota(jnp.int32, (SLOT, 1), 0) < valid[slot]
        grad_out = jnp.where(kept, side[rows, :], 0.0)
        side[rows, :] = unit_values * vectors[6:7, :] + vectors[7:8, :]
        pltpu.make_async_copy(side.at[rows, :], output.at[rows, :], out_sem.at[slot]).start()
        vec_grad[6:7, :] += sum_rows(grad_out * unit_values)
        vec_grad[7:8, :] += sum_rows(grad_out)
        scaled = grad_out * vectors[6:7, :]
        result = inv * (
            scaled - mean_lanes(scaled) - unit_values * mean_lanes(scaled * unit_values)
        )
        grad[rows, :] = result
        rounded = result.astype(LOW)
        grad_low[rows, :] = rounded
        vec_grad[5:6, :] += sum_rows(rounded.astype(SUM))

    each(4, finish_slot)

    def reduce_copy(index, stage):
        turn = index % 2 if isinstance(index, int) else lax.rem(index, 2)
        source, target, device = (
            (mat_send, mat_got.at[turn], here["twin"]),
            (pair_send, pair_got.at[turn], here["second"]),
            (line_send, line_got.at[turn], here["first"]),
            (two_send, two_got.at[turn], here["near_z"]),
            (one_send, one_got.at[turn], here["far_z"]),
        )[stage]
        return send(source, target, reduce_sent.at[stage], reduce_got.at[stage, turn], device)

    def share_copy(index):
        part = shares.at[index, :, mine]
        source = rows48.at[pl.ds(pl.multiple_of((1 - core) * 24, 8), 24), :]
        return send(source, part, share_sem.at[0, index], share_sem.at[1, index], here["twin"])

    def reduce(notch):
        def turn_of(index):
            return index % 2 if isinstance(index, int) else lax.rem(index, 2)

        def shared(index):
            share_copy(index).wait()

        def last(index):
            reduce_copy(index, 4).wait()
            rows48[...] = one_keep[...] + one_got[turn_of(index)].astype(SUM)
            shares[index, :, mine] = rows48[pl.ds(pl.multiple_of(core * 24, 8), 24), :]
            share_copy(index).start()

        def fourth(index):
            reduce_copy(index, 3).wait()
            turn = turn_of(index)
            one_keep[...] = two_keep[high] + two_got[turn, high].astype(SUM)
            one_send[...] = (two_keep[1 - high] + two_got[turn, 1 - high].astype(SUM)).astype(LOW)
            reduce_copy(index, 4).start()

        def third(index):
            reduce_copy(index, 2).wait()
            turn = turn_of(index)
            two_send[...] = (
                line_keep[:, 1 - low] + line_got[turn, :, 1 - low].astype(SUM)
            ).astype(LOW)
            reduce_copy(index, 3).start()
            two_keep[...] = line_keep[:, low] + line_got[turn, :, low].astype(SUM)

        def second(index):
            reduce_copy(index, 1).wait()
            turn = turn_of(index)
            line_send[...] = (pair_keep[1] + pair_got[turn, 1].astype(SUM)).astype(LOW)
            reduce_copy(index, 2).start()
            line_keep[...] = pair_keep[0] + pair_got[turn, 0].astype(SUM)

        def first(index):
            reduce_copy(index, 0).wait()
            turn = turn_of(index)

            def column(row, col):
                return mat[:, :, row, col, :, mine] + mat_got[turn, :, :, row, col].astype(SUM)

            pair_send[0] = column(y2, x2).astype(LOW)
            pair_send[1] = column(1 - y, 1 - x).astype(LOW)
            reduce_copy(index, 1).start()
            pair_keep[0] = column(y, x)
            pair_keep[1] = column(y1, x1)

        for age, body in ((6, shared), (5, last), (4, fourth), (3, third), (2, second), (1, first)):
            guarded(notch - age, body)

    def emit(index, left, right):
        reduce(index)
        for part in range(2):
            values = dot(left[:, part * HALF : (part + 1) * HALF], right[...], 0, 0)
            mat[part] = values.reshape(mat.shape[1:])
        mat_send[...] = mat[:, :, :, :, :, other].astype(LOW)
        reduce_copy(index, 0).start()

    def back_chunk(chunk):
        emit(2 * chunk, act.at[chunk], grad_low)

        def back_slot(slot):
            rows = slot_rows(slot)
            values = dot(grad_low[rows, :], weight(8 + chunk), 1, 1)
            rounded = (values * slope[chunk, rows, :].astype(SUM)).astype(LOW)
            slope[chunk, rows, :] = rounded
            row = pl.ds(8 + chunk, 1)
            vec_grad[row, :] += sum_rows(rounded.astype(SUM))

        each(4, back_slot)
        emit(2 * chunk + 1, hidden_low, slope.at[chunk])

        def back_hidden(slot):
            rows = slot_rows(slot)
            grad[rows, :] += dot(slope[chunk, rows, :], weight(4 + chunk), 1, 1)

        each(4, back_hidden)

    each(4, back_chunk)

    def back_norm(slot):
        rows = slot_rows(slot)
        total = grad[rows, :]
        unit_values = normed[rows, :]
        vec_grad[3:4, :] += sum_rows(total * unit_values)
        vec_grad[4:5, :] += sum_rows(total)
        scaled = total * vectors[3:4, :]
        inv = inverse[rows, 0:1]
        result = inv * (
            scaled - mean_lanes(scaled) - unit_values * mean_lanes(scaled * unit_values)
        )
        grad[rows, :] = result
        rounded = result.astype(LOW)
        grad_low[rows, :] = rounded
        vec_grad[2:3, :] += sum_rows(rounded.astype(SUM))

    each(4, back_norm)
    emit(8, context, grad_low)

    def back_context(slot):
        rows = slot_rows(slot)
        context[rows, :] = dot(grad_low[rows, :], weight(3), 1, 1).astype(LOW)

    each(4, back_context)

    def back_unit(unit):
        each(
            4,
            lambda slot: attend_back(unit, slot, valid[slot], qkv, context, log_total, vec_grad),
        )
        emit(9 + unit, token_low, qkv.at[unit])

    each(3, back_unit)

    order = ("twin", "along_x", "along_y", "near_z", "far_z")

    def vec_copy(stage):
        return send(
            vec_grad, vec_got.at[stage], vec_sent.at[stage], vec_arrived.at[stage], here[order[stage]]
        )

    def back_tokens(slot):
        rows = slot_rows(slot)
        pltpu.make_async_copy(side.at[rows, :], output.at[rows, :], out_sem.at[slot]).wait()
        total = grad[rows, :]
        for unit in range(3):
            total += dot(qkv[unit, rows, :], weight(unit), 1, 1)
        side[rows, :] = total
        pltpu.make_async_copy(side.at[rows, :], input_grad.at[rows, :], out_sem.at[slot]).start()

    for step in range(6):
        if step > 0:
            vec_copy(step - 1).wait()
            vec_grad[...] += vec_got[step - 1]
        if step < 5:
            vec_copy(step).start()
        reduce(12 + step)
        if step < 4:
            back_tokens(step)
    vec_total[...] = vec_grad[...]
    out_copy = pltpu.make_async_copy(shares, grad_shard, in_sem.at[0])
    out_copy.start()
    out_copy.wait()
    for slot in range(4):
        rows = slot_rows(slot)
        pltpu.make_async_copy(side.at[rows, :], input_grad.at[rows, :], out_sem.at[slot]).wait()


def permute_columns(shard):
    rows = shard.shape[0]
    first = shard[:, :2304].reshape(rows, 3, 2, 3, 128).transpose(3, 0, 2, 1, 4)
    second = shard[:, 2304:3072].reshape(1, rows, TILE)
    third = shard[:, 3072:6144].reshape(rows, TILE, 4).transpose(2, 0, 1)
    fourth = shard[:, 6144:].reshape(rows, 4, TILE).transpose(1, 0, 2)
    return jnp.concatenate([first.reshape(3, rows, TILE), second, third, fourth], axis=0)


def restore_columns(pieces):
    rows = pieces.shape[1]
    first = pieces[:3].reshape(3, rows, 2, 3, 128).transpose(1, 3, 2, 0, 4)
    third = pieces[4:8].transpose(1, 2, 0)
    fourth = pieces[8:].transpose(1, 0, 2)
    return jnp.concatenate(
        [
            first.reshape(rows, 2304),
            pieces[3],
            third.reshape(rows, 3072),
            fourth.reshape(rows, 3072),
        ],
        axis=1,
    )


def run_layer(tokens, cotangent, valid, shard, vectors):
    rows = tokens.shape[0]
    zero = jnp.zeros((TILE,), SUM)
    qkv_bias = jnp.stack([vectors[0], zero, vectors[1]]).reshape(3, 2, 3, 128)
    qkv_bias = qkv_bias.transpose(2, 1, 0, 3).reshape(3, 1, TILE)
    ffn_bias = vectors[8:12].reshape(TILE, 4).T.reshape(4, 1, TILE)
    vmem = pl.BlockSpec(memory_space=pltpu.VMEM)
    smem = pl.BlockSpec(memory_space=pltpu.SMEM)
    hbm = pl.BlockSpec(memory_space=pl.ANY)
    full = lambda *shape: pltpu.VMEM(shape, SUM)
    low = lambda *shape: pltpu.VMEM(shape, LOW)
    copies = lambda *shape: pltpu.SemaphoreType.DMA(shape)
    return pl.pallas_call(
        layer,
        out_shape=[
            jax.ShapeDtypeStruct((rows, TILE), SUM),
            jax.ShapeDtypeStruct((rows, TILE), SUM),
            jax.ShapeDtypeStruct((PIECES, 24, TILE), SUM),
            jax.ShapeDtypeStruct((16, TILE), SUM),
        ],
        in_specs=[smem, hbm, hbm, vmem, vmem, vmem, vmem],
        out_specs=[hbm, hbm, hbm, vmem],
        scratch_shapes=[
            low(PIECES, 2, 2, 2, 2, 48, TILE),
            full(rows, TILE),
            low(rows, TILE),
            low(3, rows, TILE),
            low(rows, TILE),
            low(rows, TILE),
            low(4, rows, TILE),
            low(4, rows, TILE),
            full(rows, TILE),
            low(rows, TILE),
            full(rows, TILE),
            full(rows, 128),
            full(3, 4, 4, SLOT),
            full(16, TILE),
            full(2, 2, 2, 2, 48, TILE),
            low(2, 2, 2, 2, 48, HALF),
            low(2, 2, 2, 2, 2, 48, HALF),
            full(2, 2, 2, 48, HALF),
            low(2, 2, 2, 48, HALF),
            low(2, 2, 2, 2, 48, HALF),
            full(2, 2, 48, HALF),
            low(2, 2, 48, HALF),
            low(2, 2, 2, 48, HALF),
            full(2, 48, HALF),
            low(2, 48, HALF),
            low(2, 2, 48, HALF),
            full(48, HALF),
            low(48, HALF),
            low(2, 48, HALF),
            full(48, HALF),
            full(PIECES, 24, TILE),
            full(5, 16, TILE),
            copies(2),
            copies(4),
            copies(2),
            copies(PIECES, 6),
            copies(PIECES, 6),
            copies(5),
            copies(5, 2),
            copies(2, PIECES),
            copies(5),
            copies(5),
        ],
        compiler_params=pltpu.CompilerParams(
            collective_id=0, has_side_effects=True, vmem_limit_bytes=64 * 2**20
        ),
        cost_estimate=pl.CostEstimate(
            flops=60 * 10**9, bytes_accessed=60 * 10**6, transcendentals=10**7
        ),
    )(valid, tokens, cotangent, shard, vectors, qkv_bias, ffn_bias)


def fused(
    tokens,
    cotangent,
    lengths,
    null_flags,
    weights,
    moment1,
    moment2,
    vectors,
    vec_moment1,
    vec_moment2,
):
    valid = jnp.where(null_flags == 1, QLEN, lengths).astype(jnp.int32)
    shard = permute_columns(weights)
    output, input_grad, grad_pieces, vec_total = run_layer(
        tokens, cotangent, valid, shard, vectors
    )
    order = (9, 10, 11, 8, 1, 3, 5, 7, 0, 2, 4, 6)
    grad_shard = restore_columns(jnp.stack([grad_pieces[index] for index in order]))
    ffn_rows = vec_total[8:12].T.reshape(4, TILE)
    vec_total = jnp.concatenate([vec_total[:8], ffn_rows], axis=0)
    return (output, input_grad) + optimize(
        grad_shard, vec_total, weights, moment1, moment2, vectors, vec_moment1, vec_moment2
    )


def optimize(
    grad_shard, vec_total, weights, moment1, moment2, vectors, vec_moment1, vec_moment2
):
    correction = 1.0 - 0.5**STEP
    new_first = 0.5 * moment1 + 0.5 * grad_shard
    new_second = 0.5 * moment2 + 0.5 * grad_shard * grad_shard
    update = new_first / correction / (jnp.sqrt(new_second / correction) + 1e-06) + 0.01 * weights
    edges = (0, 2304, 3072, 6144, 9216)
    squares = jnp.stack(
        [
            jnp.stack(
                [
                    jnp.sum(jnp.square(values[:, edges[index] : edges[index + 1]]))
                    for values in (weights, update)
                ]
            )
            for index in range(4)
        ]
    )
    norm_pairs = jnp.sqrt(lax.psum(squares, ("dp", "shard")))
    trust = norm_pairs[:, 0] / (norm_pairs[:, 1] + 1e-06)
    column = jnp.arange(weights.shape[1])
    column_trust = jnp.where(
        column < edges[1],
        trust[0],
        jnp.where(column < edges[2], trust[1], jnp.where(column < edges[3], trust[2], trust[3])),
    )
    new_weights = weights - 0.3 * column_trust * update
    vec_first = 0.5 * vec_moment1 + 0.5 * vec_total
    vec_second = 0.5 * vec_moment2 + 0.5 * vec_total * vec_total
    new_vectors = vectors - 0.3 * (vec_first / correction) / (
        jnp.sqrt(vec_second / correction) + 1e-06
    )
    return (
        new_first,
        new_second,
        new_weights,
        vec_first,
        vec_second,
        new_vectors,
        norm_pairs,
        trust,
    )


def solution(mesh):
    split = P(("dp", "shard"), None)
    flat = P(("dp", "shard"))
    in_specs = (split, split, flat, flat, split, split, split, P(), P(), P())
    out_specs = (split,) * 5 + (P(),) * 5
    body = fused if mesh.shape["dp"] == 8 and mesh.shape["shard"] == 4 else plain
    return jax.shard_map(body, mesh=mesh, in_specs=in_specs, out_specs=out_specs, check_vma=False)
```

```python
import jax
import jax.numpy as jnp
from jax import lax
from jax.experimental import pallas as pl
from jax.experimental.pallas import tpu as pltpu
from jax.sharding import PartitionSpec as P

HEADS = 12
SLOT = 288
QLEN = 64
STEP = 5


def norm_forward(values, gain, shift):
    centred = values - jnp.mean(values, axis=-1, keepdims=True)
    inverse = lax.rsqrt(jnp.mean(centred * centred, axis=-1, keepdims=True) + 1e-05)
    normed = centred * inverse
    return (normed * gain + shift, normed, inverse)


def norm_backward(grad_result, normed, inverse, gain):
    scaled = grad_result * gain
    grad_gain = jnp.sum(grad_result * normed, axis=0)
    grad_shift = jnp.sum(grad_result, axis=0)
    centred = scaled - jnp.mean(scaled, axis=-1, keepdims=True)
    grad_input = inverse * (centred - normed * jnp.mean(scaled * normed, axis=-1, keepdims=True))
    return (grad_input, grad_gain, grad_shift)


def gelu_slope(values):
    return (
        0.5 * (1.0 + jax.scipy.special.erf(values * 0.7071067811865476))
        + values * jnp.exp(-0.5 * values * values) * 0.3989422804014327
    )


def plain(
    tokens,
    cotangent,
    lengths,
    null_flags,
    weights,
    moment1,
    moment2,
    vectors,
    vec_moment1,
    vec_moment2,
):
    model_width = tokens.shape[1]
    row_count = tokens.shape[0]
    slot_count = lengths.shape[0]
    head_size = model_width // HEADS
    score_scale = head_size ** (-0.5)
    block_slots = min(2, slot_count)
    block_count = slot_count // block_slots
    valid_len = jnp.where(null_flags == 1, QLEN, lengths)
    key_valid = jnp.arange(SLOT, dtype=jnp.int32)[None, :] < valid_len[:, None]
    key_blocks = key_valid.reshape(block_count, block_slots, SLOT)
    row_weight = key_valid.reshape(row_count, 1).astype(jnp.float32)
    qkv_bias = jnp.concatenate([vectors[0], jnp.zeros((model_width,), jnp.float32), vectors[1]])
    ffn_bias = vectors[8:12].reshape(4 * model_width)
    token_low = tokens.astype(jnp.bfloat16)

    def block_scores(qkv_block, valid_keys):
        scores = (
            jnp.einsum(
                "bqhd,bkhd->bhqk",
                qkv_block[:, :, 0],
                qkv_block[:, :, 1],
                preferred_element_type=jnp.float32,
            )
            * score_scale
        )
        return jnp.where(valid_keys[:, None, None, :], scores, -1000000000.0)

    def attend_block(packed):
        qkv_block, valid_keys = packed
        scores = block_scores(qkv_block, valid_keys)
        row_top = jnp.max(scores, axis=-1, keepdims=True)
        exponent = jnp.exp(scores - row_top)
        row_total = jnp.sum(exponent, axis=-1, keepdims=True)
        softmax_out = (exponent / row_total).astype(jnp.bfloat16)
        context = jnp.einsum(
            "bhqk,bkhd->bqhd", softmax_out, qkv_block[:, :, 2], preferred_element_type=jnp.float32
        )
        return (context.astype(jnp.bfloat16), (row_top + jnp.log(row_total))[..., 0])

    def attend_back(packed):
        qkv_block, valid_keys, log_block, grad_block = packed
        scores = block_scores(qkv_block, valid_keys)
        softmax_out = jnp.exp(scores - log_block[..., None])
        grad_values = jnp.einsum(
            "bhqk,bqhd->bkhd",
            softmax_out.astype(jnp.bfloat16),
            grad_block,
            preferred_element_type=jnp.float32,
        )
        grad_soft = jnp.einsum(
            "bqhd,bkhd->bhqk", grad_block, qkv_block[:, :, 2], preferred_element_type=jnp.float32
        )
        grad_scores = softmax_out * (
            grad_soft - jnp.sum(grad_soft * softmax_out, axis=-1, keepdims=True)
        )
        scores_low = grad_scores.astype(jnp.bfloat16)
        grad_query = (
            jnp.einsum(
                "bhqk,bkhd->bqhd",
                scores_low,
                qkv_block[:, :, 1],
                preferred_element_type=jnp.float32,
            )
            * score_scale
        )
        grad_keys = (
            jnp.einsum(
                "bhqk,bqhd->bkhd",
                scores_low,
                qkv_block[:, :, 0],
                preferred_element_type=jnp.float32,
            )
            * score_scale
        )
        return jnp.stack([grad_query, grad_keys, grad_values], axis=2).astype(jnp.bfloat16)

    gathered = lax.all_gather(weights.astype(jnp.bfloat16), ("dp", "shard"), axis=0, tiled=True)
    first_mats = (
        gathered[:, : 3 * model_width],
        gathered[:, 3 * model_width : 4 * model_width],
        gathered[:, 4 * model_width : 8 * model_width],
        gathered[:, 8 * model_width :].reshape(4 * model_width, model_width),
    )
    w_qkv, w_out, w_in, w_down = first_mats
    qkv_low = (jnp.dot(token_low, w_qkv, preferred_element_type=jnp.float32) + qkv_bias).astype(
        jnp.bfloat16
    )
    qkv_blocks = qkv_low.reshape(block_count, block_slots, SLOT, 3, HEADS, head_size)
    contexts, log_total = lax.map(attend_block, (qkv_blocks, key_blocks))
    context_low = contexts.reshape(row_count, model_width)
    attention = jnp.dot(context_low, w_out, preferred_element_type=jnp.float32) + vectors[2]
    hidden_one, normed_one, inverse_one = norm_forward(tokens + attention, vectors[3], vectors[4])
    hidden_low = hidden_one.astype(jnp.bfloat16)
    pre_act = jnp.dot(hidden_low, w_in, preferred_element_type=jnp.float32) + ffn_bias
    act_low = jax.nn.gelu(pre_act, approximate=False).astype(jnp.bfloat16)
    ffn_out = jnp.dot(act_low, w_down, preferred_element_type=jnp.float32) + vectors[5]
    result, normed_two, inverse_two = norm_forward(hidden_one + ffn_out, vectors[6], vectors[7])
    first_kept = (
        qkv_blocks,
        log_total,
        context_low,
        normed_one,
        inverse_one,
        hidden_low,
        pre_act,
        act_low,
        normed_two,
        inverse_two,
        result,
    )
    output = first_kept[10]
    w_qkv, w_out, w_in, w_down = first_mats
    (
        qkv_blocks,
        log_total,
        context_low,
        normed_one,
        inverse_one,
        hidden_low,
        pre_act,
        act_low,
        normed_two,
        inverse_two,
    ) = first_kept[:10]
    grad_result = cotangent * row_weight
    grad_two, grad_gain_two, grad_shift_two = norm_backward(
        grad_result, normed_two, inverse_two, vectors[6]
    )
    grad_ffn_low = grad_two.astype(jnp.bfloat16)
    grad_bias_down = jnp.sum(grad_ffn_low, axis=0, dtype=jnp.float32)
    grad_down = jnp.einsum("tf,td->fd", act_low, grad_ffn_low, preferred_element_type=jnp.float32)
    grad_act = jnp.einsum("td,fd->tf", grad_ffn_low, w_down, preferred_element_type=jnp.float32)
    grad_pre_low = (grad_act * gelu_slope(pre_act)).astype(jnp.bfloat16)
    grad_bias_in = jnp.sum(grad_pre_low, axis=0, dtype=jnp.float32)
    grad_in = jnp.einsum("td,tf->df", hidden_low, grad_pre_low, preferred_element_type=jnp.float32)
    grad_hidden = grad_two + jnp.einsum(
        "tf,df->td", grad_pre_low, w_in, preferred_element_type=jnp.float32
    )
    grad_residual, grad_gain_one, grad_shift_one = norm_backward(
        grad_hidden, normed_one, inverse_one, vectors[3]
    )
    grad_attn_low = grad_residual.astype(jnp.bfloat16)
    grad_bias_out = jnp.sum(grad_attn_low, axis=0, dtype=jnp.float32)
    grad_out = jnp.einsum(
        "tc,td->cd", context_low, grad_attn_low, preferred_element_type=jnp.float32
    )
    grad_context = jnp.einsum(
        "td,cd->tc", grad_attn_low, w_out, preferred_element_type=jnp.float32
    ).astype(jnp.bfloat16)
    grad_blocks = grad_context.reshape(block_count, block_slots, SLOT, HEADS, head_size)
    grad_qkv_low = lax.map(attend_back, (qkv_blocks, key_blocks, log_total, grad_blocks)).reshape(
        row_count, 3 * model_width
    )
    grad_bias_qkv = jnp.sum(grad_qkv_low, axis=0, dtype=jnp.float32)
    grad_qkv = jnp.einsum("td,te->de", token_low, grad_qkv_low, preferred_element_type=jnp.float32)
    input_grad = grad_residual + jnp.einsum(
        "te,de->td", grad_qkv_low, w_qkv, preferred_element_type=jnp.float32
    )
    vector_grad = jnp.concatenate(
        [
            jnp.stack(
                [
                    grad_bias_qkv[:model_width],
                    grad_bias_qkv[2 * model_width :],
                    grad_bias_out,
                    grad_gain_one,
                    grad_shift_one,
                    grad_bias_down,
                    grad_gain_two,
                    grad_shift_two,
                ]
            ),
            grad_bias_in.reshape(4, model_width),
        ],
        axis=0,
    )
    qkv_shard, out_shard, in_shard, down_shard = (
        lax.psum_scatter(grad_qkv, ("dp", "shard"), scatter_dimension=0, tiled=True),
        lax.psum_scatter(grad_out, ("dp", "shard"), scatter_dimension=0, tiled=True),
        lax.psum_scatter(grad_in, ("dp", "shard"), scatter_dimension=0, tiled=True),
        lax.psum_scatter(
            grad_down.reshape(model_width, 4 * model_width),
            ("dp", "shard"),
            scatter_dimension=0,
            tiled=True,
        ),
    )
    vector_total = lax.psum(vector_grad, ("dp", "shard"))
    grad_shard = jnp.concatenate([qkv_shard, out_shard, in_shard, down_shard], axis=1)
    correction = 1.0 - 0.5**STEP
    new_first = 0.5 * moment1 + 0.5 * grad_shard
    new_second = 0.5 * moment2 + 0.5 * grad_shard * grad_shard
    update = new_first / correction / (jnp.sqrt(new_second / correction) + 1e-06) + 0.01 * weights
    column_edges = (0, 3 * model_width, 4 * model_width, 8 * model_width, 12 * model_width)
    pair_rows = []
    for group_index in range(4):
        weight_part = weights[:, column_edges[group_index] : column_edges[group_index + 1]]
        update_part = update[:, column_edges[group_index] : column_edges[group_index + 1]]
        pair_rows.append(
            jnp.stack([jnp.sum(weight_part * weight_part), jnp.sum(update_part * update_part)])
        )
    pair_squares = jnp.stack(pair_rows)
    pair_total = lax.psum(pair_squares, ("dp", "shard"))
    norm_pairs = jnp.sqrt(pair_total)
    trust_ratio = norm_pairs[:, 0] / (norm_pairs[:, 1] + 1e-06)
    column_trust = jnp.concatenate(
        [
            jnp.ones((column_edges[group_index + 1] - column_edges[group_index],), jnp.float32)
            * trust_ratio[group_index]
            for group_index in range(4)
        ]
    )
    new_weights = weights - 0.3 * column_trust * update
    vec_first = 0.5 * vec_moment1 + 0.5 * vector_total
    vec_second = 0.5 * vec_moment2 + 0.5 * vector_total * vector_total
    new_vectors = vectors - 0.3 * (vec_first / correction) / (
        jnp.sqrt(vec_second / correction) + 1e-06
    )
    return (
        output,
        input_grad,
        new_first,
        new_second,
        new_weights,
        vec_first,
        vec_second,
        new_vectors,
        norm_pairs,
        trust_ratio,
    )


SUM = jnp.float32
LOW = jnp.bfloat16
PIECES = 12
TILE = 768
HALF = 384
NEG = -1e9
CORRECTION = 1.0 - 0.5**STEP


def dot(left, right, left_dim, right_dim):
    return lax.dot_general(
        left, right, (((left_dim,), (right_dim,)), ((), ())), preferred_element_type=SUM
    )


def slot_rows(slot):
    return pl.ds(pl.multiple_of(slot * SLOT, SLOT), SLOT)


def each(count, body):
    def step(index, carry):
        body(index)
        return carry

    lax.fori_loop(0, count, step, 0)


def mean_lanes(values):
    return jnp.mean(values, axis=-1, keepdims=True)


def sum_rows(values):
    return jnp.sum(values, axis=0, keepdims=True)


def head_operands(query, key, valid):
    lane = lax.broadcasted_iota(jnp.int32, query.shape, 1)
    row = lax.broadcasted_iota(jnp.int32, query.shape, 0)
    low_head = lane < 64
    bias = jnp.where(row < valid, 0.0, NEG).astype(LOW)
    scaled = query * jnp.asarray(0.125, LOW)
    one, zero = jnp.ones_like(query), jnp.zeros_like(query)
    queries = (
        jnp.where(low_head, scaled, jnp.where(lane == 64, one, zero)),
        jnp.where(low_head, jnp.where(lane == 0, one, zero), scaled),
    )
    keys = (
        jnp.where(low_head, key, jnp.where(lane == 64, bias, zero)),
        jnp.where(low_head, jnp.where(lane == 0, bias, zero), key),
    )
    return queries, keys, low_head


def attend(unit, slot, valid, qkv, context, log_total):
    rows = slot_rows(slot)
    items = []
    for half in range(2):
        query, key, value = (
            qkv[unit, rows, (3 * half + part) * 128 : (3 * half + part + 1) * 128]
            for part in range(3)
        )
        queries, keys, low_head = head_operands(query, key, valid)
        items += [(queries[head], keys[head], value) for head in range(2)]
    scores = [dot(key, query, 1, 1) for query, key, _ in items]
    results = []
    for index, values in enumerate(scores):
        top = jnp.max(values, axis=0, keepdims=True)
        exponent = jnp.exp(values - top)
        total = sum_rows(exponent)
        log_total[unit, slot, index : index + 1, :] = top + jnp.log(total)
        results.append((exponent * (1.0 / total)).astype(LOW))
    results = [dot(probs, item[2], 0, 0) for probs, item in zip(results, items)]
    for half in range(2):
        lanes = pl.ds(pl.multiple_of((unit + 3 * half) * 128, 128), 128)
        joined = jnp.where(low_head, results[2 * half], results[2 * half + 1])
        context[rows, lanes] = joined.astype(LOW)


def attend_back(unit, slot, valid, qkv, grad_context, log_total, vec_grad):
    rows = slot_rows(slot)
    for half in range(2):
        query, key, value = (
            qkv[unit, rows, (3 * half + part) * 128 : (3 * half + part + 1) * 128]
            for part in range(3)
        )
        lanes = pl.ds(pl.multiple_of((unit + 3 * half) * 128, 128), 128)
        grad = grad_context[rows, lanes]
        queries, keys, low_head = head_operands(query, key, valid)
        zero = jnp.zeros_like(grad)
        grads = (jnp.where(low_head, grad, zero), jnp.where(low_head, zero, grad))
        scores = [dot(keys[head], queries[head], 1, 1) for head in range(2)]
        grad_probs = [dot(value, grads[head], 1, 1) for head in range(2)]
        probs, grad_value = [], []
        for head in range(2):
            index = 2 * half + head
            probs.append(jnp.exp(scores[head] - log_total[unit, slot, index : index + 1, :]))
            grad_value.append(dot(probs[head].astype(LOW), grad, 1, 0))
        grad_key, grad_query = [], []
        for head in range(2):
            inner = sum_rows(grad_probs[head] * probs[head])
            low = (probs[head] * (grad_probs[head] - inner)).astype(LOW)
            grad_key.append(dot(low, query, 1, 0))
            grad_query.append(dot(low, key, 0, 0))
        for part, parts, scale in (
            (0, grad_query, 0.125),
            (1, grad_key, 0.125),
            (2, grad_value, 1.0),
        ):
            joined = (jnp.where(low_head, parts[0], parts[1]) * scale).astype(LOW)
            qkv[unit, rows, (3 * half + part) * 128 : (3 * half + part + 1) * 128] = joined
            if part != 1:
                row = part // 2
                vec_grad[row : row + 1, lanes] += sum_rows(joined.astype(SUM))


def make_order(buffer):
    row = lax.broadcasted_iota(jnp.int32, (512, 512), 0)
    column = lax.broadcasted_iota(jnp.int32, (512, 512), 1)
    chosen = column == 4 * (row % 128) + row // 128
    buffer[0, 0:512, 0:512] = jnp.where(chosen, 1.0, 0.0).astype(LOW)


def reorder(values, buffer, side):
    first = values.astype(LOW)
    rest = values - first.astype(SUM)
    second = rest.astype(LOW)
    third = (rest - second.astype(SUM)).astype(LOW)
    order = buffer[0, 0:512, 0:512]
    return (dot(first, order, 1, side) + dot(second, order, 1, side)) + dot(third, order, 1, side)


def place():
    outer, inner = lax.axis_index("dp"), lax.axis_index("shard")
    z, y, x, core = outer // 2, outer % 2, inner // 2, inner % 2
    here = dict(z=z, y=y, x=x, core=core, high=z // 2, low=z % 2)
    here["y1"], here["x1"] = y + core * (1 - 2 * y), x + (1 - core) * (1 - 2 * x)
    here["y2"], here["x2"] = y + (1 - core) * (1 - 2 * y), x + core * (1 - 2 * x)
    device = lambda z, y, x, core: (z * 2 + y, x * 2 + core)
    here["twin"] = device(z, y, x, 1 - core)
    here["near_z"] = device(z + 1 - 2 * (z % 2), y, x, core)
    here["far_z"] = device((z + 2) % 4, y, x, core)
    here["first"] = device(z, here["y1"], here["x1"], core)
    here["second"] = device(z, here["y2"], here["x2"], core)
    here["along_x"] = device(z, y, 1 - x, core)
    here["along_y"] = device(z, 1 - y, x, core)
    here["mine"] = pl.ds(pl.multiple_of(core * HALF, 128), HALF)
    here["other"] = pl.ds(pl.multiple_of((1 - core) * HALF, 128), HALF)
    return here


def send(source, target, sent, arrived, device):
    return pltpu.make_async_remote_copy(
        src_ref=source,
        dst_ref=target,
        send_sem=sent,
        recv_sem=arrived,
        device_id=device,
        device_id_type=pl.DeviceIdType.MESH,
    )


def inside(index):
    if isinstance(index, int):
        return 0 <= index < PIECES
    return jnp.logical_and(index >= 0, index < PIECES)


def guarded(index, body):
    if isinstance(index, int):
        if inside(index):
            body(index)
    else:
        pl.when(inside(index))(lambda: body(index))


def layer(
    lengths, null_flags, tokens, cotangent, weights, moment1, moment2, vectors, vec_moment1,
    vec_moment2,
    output, input_grad, new_moment1, new_moment2, new_weights, new_vec_moment1, new_vec_moment2,
    new_vectors, norm_pairs, trust,
    walls, normed, token_low, qkv, context, hidden_low, act, slope, grad, grad_low, side, inverse,
    log_total, vec_grad, mat, mat_send, mat_got, pair_keep, pair_send, pair_got,
    line_keep, line_send, line_got, two_keep, two_send, two_got, one_keep, one_send, one_got, rows48,
    shares, vec_got, qkv_bias, ffn_bias, squares, squares_got,
    in_sem, out_sem, twin_sem, gather_sent, gather_got, reduce_sent, reduce_got,
    share_sem, vec_sent, vec_arrived, state_sem, square_sem,
):
    here = place()
    z, y, x, core, high, low = (here[name] for name in ("z", "y", "x", "core", "high", "low"))
    y1, x1, y2, x2 = (here[name] for name in ("y1", "x1", "y2", "x2"))
    mine, other = here["mine"], here["other"]

    def valid(slot):
        return jnp.where(null_flags[slot] == 1, QLEN, lengths[slot])

    def state_rows(quarter, chunk):
        return pl.ds(quarter * SLOT + 24 * chunk, 24)

    def state_copy(array, buffer, quarter, chunk):
        return pltpu.make_async_copy(
            array.at[:, pl.ds(TILE * chunk, TILE)],
            buffer.at[state_rows(quarter, chunk), :],
            state_sem.at[quarter, chunk],
        )

    def result_copy(array, quarter, chunk):
        return pltpu.make_async_copy(
            normed.at[state_rows(quarter, chunk), :],
            array.at[:, pl.ds(TILE * chunk, TILE)],
            state_sem.at[quarter, chunk],
        )

    for chunk in range(PIECES):
        state_copy(weights, grad, 0, chunk).start()
    cot_copy = pltpu.make_async_copy(cotangent, side, in_sem.at[0])
    cot_copy.start()
    tok_copy = pltpu.make_async_copy(tokens, normed, in_sem.at[1])
    tok_copy.start()

    barrier = pltpu.get_barrier_semaphore()
    peers = ("twin", "near_z", "far_z", "along_x", "along_y")
    for name in peers:
        pl.semaphore_signal(
            barrier, inc=1, device_id=here[name], device_id_type=pl.DeviceIdType.MESH
        )
    pl.semaphore_wait(barrier, len(peers))

    for chunk in range(PIECES):
        state_copy(weights, grad, 0, chunk).wait()
    for unit in range(3):
        for half in range(2):
            for part in range(3):
                lanes = slice((unit + 3 * half) * 128, (unit + 3 * half + 1) * 128)
                place_lanes = slice((3 * half + part) * 128, (3 * half + part + 1) * 128)
                grad[state_rows(1, unit), place_lanes] = grad[state_rows(0, part), lanes]

    def swap(first, count):
        rows = pl.ds(24 * first, 24 * count)
        return send(
            grad.at[pl.ds(SLOT + 24 * first, 24 * count), other],
            shares.at[rows, other],
            twin_sem.at[0, first],
            twin_sem.at[1, first],
            here["twin"],
        )

    swap(0, 3).start()
    make_order(act)
    for block in range(6):
        values = jnp.concatenate(
            [
                grad[state_rows(0, 4 + part // 3), part % 3 * 256 : part % 3 * 256 + 256]
                for part in (2 * block, 2 * block + 1)
            ],
            axis=1,
        )
        ordered = dot(values.astype(LOW), act[0, 0:512, 0:512], 1, 1)
        for chunk in range(4):
            grad[state_rows(1, 4 + chunk), block * 128 : block * 128 + 128] = ordered[
                :, chunk * 128 : chunk * 128 + 128
            ]
    for chunk in (3, 8, 9, 10, 11):
        grad[state_rows(1, chunk), :] = grad[state_rows(0, chunk), :]
    swap(3, 9).start()
    vec_grad[...] = jnp.zeros_like(vec_grad)
    for unit in range(3):
        for half in range(2):
            lanes = slice((unit + 3 * half) * 128, (unit + 3 * half + 1) * 128)
            for part, row in ((0, 0), (2, 1)):
                target = slice((3 * half + part) * 128, (3 * half + part + 1) * 128)
                qkv_bias[unit, :, target] = vectors[row : row + 1, lanes]
            target = slice((3 * half + 1) * 128, (3 * half + 2) * 128)
            qkv_bias[unit, :, target] = jnp.zeros((1, 128), SUM)
    for block in range(6):
        values = jnp.concatenate(
            [
                vectors[8 + part // 3 : 9 + part // 3, part % 3 * 256 : part % 3 * 256 + 256]
                for part in (2 * block, 2 * block + 1)
            ],
            axis=1,
        )
        ordered = reorder(values, act, 1)
        for chunk in range(4):
            ffn_bias[chunk, :, block * 128 : block * 128 + 128] = ordered[
                :, chunk * 128 : chunk * 128 + 128
            ]

    def fill(piece):
        rows = pl.ds(pl.multiple_of(24 * piece, 8), 24)
        own, twin = grad[pl.ds(pl.multiple_of(SLOT + 24 * piece, 8), 24), mine], shares[rows, mine]
        upper = jnp.where(core == 0, own, twin)
        lower = jnp.where(core == 0, twin, own)
        joined = jnp.concatenate([upper, lower], axis=0)
        walls[piece, high, low, y, x, :, mine] = joined.astype(LOW)

    swap(0, 3).wait()
    each(3, fill)

    def gather_copy(piece, stage):
        if stage == 0:
            part, device = walls.at[piece, high, low, y, x, :, mine], here["far_z"]
        elif stage == 1:
            part, device = walls.at[piece, :, low, y, x, :, mine], here["near_z"]
        elif stage == 2:
            part, device = walls.at[piece, :, :, y, x, :, mine], here["first"]
        elif stage == 3:
            part, device = walls.at[piece, :, :, y, x, :, mine], here["second"]
        elif stage == 4:
            part, device = walls.at[piece, :, :, y1, x1, :, mine], here["second"]
        else:
            part, device = walls.at[piece, :, :, :, :, :, mine], here["twin"]
        return send(part, part, gather_sent.at[piece, stage], gather_got.at[piece, stage], device)

    def gather(notch):
        def begin(piece):
            gather_copy(piece, 0).start()

        def spread_line(piece):
            gather_copy(piece, 0).wait_recv()
            gather_copy(piece, 1).start()

        def spread_plane(piece):
            gather_copy(piece, 1).wait_recv()
            gather_copy(piece, 2).start()
            gather_copy(piece, 3).start()

        def pass_on(piece):
            gather_copy(piece, 2).wait_recv()
            gather_copy(piece, 4).start()

        def share(piece):
            gather_copy(piece, 3).wait_recv()
            gather_copy(piece, 4).wait_recv()
            gather_copy(piece, 5).start()

        def finish(piece):
            gather_copy(piece, 5).wait_recv()
            for stage in range(6):
                gather_copy(piece, stage).wait_send()

        for age, body in enumerate((begin, spread_line, spread_plane, pass_on, share, finish)):
            guarded(notch - age, body)

    def weight(piece):
        return walls[piece].reshape(TILE, TILE)

    gather(0)
    swap(3, 9).wait()
    each(9, lambda piece: fill(3 + piece))
    gather(1)
    gather(2)
    tok_copy.wait()

    def cast_slot(slot):
        rows = slot_rows(slot)
        token_low[rows, :] = normed[rows, :].astype(LOW)

    each(4, cast_slot)
    for notch in range(3, 6):
        gather(notch)

    def project(unit):
        def project_slot(slot):
            rows = slot_rows(slot)
            values = dot(token_low[rows, :], weight(unit), 1, 0) + qkv_bias[unit]
            qkv[unit, rows, :] = values.astype(LOW)

        each(4, project_slot)
        gather(6 + unit)
        each(4, lambda slot: attend(unit, slot, valid(slot), qkv, context, log_total))

    each(3, project)

    def attend_out(slot):
        rows = slot_rows(slot)
        values = normed[rows, :] + (dot(context[rows, :], weight(3), 1, 0) + vectors[2:3, :])
        centred = values - mean_lanes(values)
        inv = lax.rsqrt(mean_lanes(centred * centred) + 1e-05)
        unit_values = centred * inv
        normed[rows, :] = unit_values
        inverse[rows, :] = jnp.broadcast_to(inv, (SLOT, 128))
        hidden_low[rows, :] = (unit_values * vectors[3:4, :] + vectors[4:5, :]).astype(LOW)

    each(4, attend_out)

    def widen(chunk):
        gather(9 + chunk)

        def widen_slot(slot):
            rows = slot_rows(slot)
            pre = dot(hidden_low[rows, :], weight(4 + chunk), 1, 0) + ffn_bias[chunk]
            phi = 0.5 + 0.5 * lax.erf(pre * 0.7071067811865476)
            act[chunk, rows, :] = (pre * phi).astype(LOW)
            bell = jnp.exp(pre * pre * -0.5) * 0.3989422804014327
            slope[chunk, rows, :] = (phi + pre * bell).astype(LOW)

        each(4, widen_slot)

    each(4, widen)
    cot_copy.wait()

    def narrow_first(slot):
        rows = slot_rows(slot)
        start = normed[rows, :] * vectors[3:4, :] + (vectors[4:5, :] + vectors[5:6, :])
        grad[rows, :] = start + dot(act[0, rows, :], weight(8), 1, 0)

    gather(13)
    each(4, narrow_first)

    def narrow(chunk):
        gather(14 + chunk)

        def narrow_slot(slot):
            rows = slot_rows(slot)
            grad[rows, :] += dot(act[1 + chunk, rows, :], weight(9 + chunk), 1, 0)

        each(4, narrow_slot)

    each(2, narrow)
    gather(16)

    def finish_slot(slot):
        rows = slot_rows(slot)
        values = grad[rows, :] + dot(act[3, rows, :], weight(11), 1, 0)
        centred = values - mean_lanes(values)
        inv = lax.rsqrt(mean_lanes(centred * centred) + 1e-05)
        unit_values = centred * inv
        kept = lax.broadcasted_iota(jnp.int32, (SLOT, 1), 0) < valid(slot)
        grad_out = jnp.where(kept, side[rows, :], 0.0)
        side[rows, :] = unit_values * vectors[6:7, :] + vectors[7:8, :]
        pltpu.make_async_copy(side.at[rows, :], output.at[rows, :], out_sem.at[slot]).start()
        vec_grad[6:7, :] += sum_rows(grad_out * unit_values)
        vec_grad[7:8, :] += sum_rows(grad_out)
        scaled = grad_out * vectors[6:7, :]
        result = inv * (
            scaled - mean_lanes(scaled) - unit_values * mean_lanes(scaled * unit_values)
        )
        grad[rows, :] = result
        rounded = result.astype(LOW)
        grad_low[rows, :] = rounded
        vec_grad[5:6, :] += sum_rows(rounded.astype(SUM))

    each(4, finish_slot)

    def reduce_copy(index, stage):
        turn = index % 2 if isinstance(index, int) else lax.rem(index, 2)
        source, target, device = (
            (mat_send, mat_got.at[turn], here["twin"]),
            (pair_send, pair_got.at[turn], here["second"]),
            (line_send, line_got.at[turn], here["first"]),
            (two_send, two_got.at[turn], here["near_z"]),
            (one_send, one_got.at[turn], here["far_z"]),
        )[stage]
        return send(source, target, reduce_sent.at[stage], reduce_got.at[stage, turn], device)

    def share_copy(index):
        part = shares.at[pl.ds(pl.multiple_of(24 * index, 8), 24), mine]
        source = rows48.at[pl.ds(pl.multiple_of((1 - core) * 24, 8), 24), :]
        return send(source, part, share_sem.at[0, index], share_sem.at[1, index], here["twin"])

    def reduce(notch):
        def turn_of(index):
            return index % 2 if isinstance(index, int) else lax.rem(index, 2)

        def shared(index):
            share_copy(index).wait()

        def last(index):
            reduce_copy(index, 4).wait()
            rows48[...] = one_keep[...] + one_got[turn_of(index)].astype(SUM)
            shares[pl.ds(pl.multiple_of(24 * index, 8), 24), mine] = rows48[
                pl.ds(pl.multiple_of(core * 24, 8), 24), :
            ]
            share_copy(index).start()

        def fourth(index):
            reduce_copy(index, 3).wait()
            turn = turn_of(index)
            one_keep[...] = two_keep[high] + two_got[turn, high].astype(SUM)
            one_send[...] = (two_keep[1 - high] + two_got[turn, 1 - high].astype(SUM)).astype(LOW)
            reduce_copy(index, 4).start()

        def third(index):
            reduce_copy(index, 2).wait()
            turn = turn_of(index)
            two_send[...] = (
                line_keep[:, 1 - low] + line_got[turn, :, 1 - low].astype(SUM)
            ).astype(LOW)
            reduce_copy(index, 3).start()
            two_keep[...] = line_keep[:, low] + line_got[turn, :, low].astype(SUM)

        def second(index):
            reduce_copy(index, 1).wait()
            turn = turn_of(index)
            line_send[...] = (pair_keep[1] + pair_got[turn, 1].astype(SUM)).astype(LOW)
            reduce_copy(index, 2).start()
            line_keep[...] = pair_keep[0] + pair_got[turn, 0].astype(SUM)

        def first(index):
            reduce_copy(index, 0).wait()
            turn = turn_of(index)

            def column(row, col):
                return mat[:, :, row, col, :, mine] + mat_got[turn, :, :, row, col].astype(SUM)

            pair_send[0] = column(y2, x2).astype(LOW)
            pair_send[1] = column(1 - y, 1 - x).astype(LOW)
            reduce_copy(index, 1).start()
            pair_keep[0] = column(y, x)
            pair_keep[1] = column(y1, x1)

        for age, body in ((6, shared), (5, last), (4, fourth), (3, third), (2, second), (1, first)):
            guarded(notch - age, body)

    def emit(index, left, right):
        reduce(index)
        for part in range(2):
            values = dot(left[:, part * HALF : (part + 1) * HALF], right[...], 0, 0)
            mat[part] = values.reshape(mat.shape[1:])
        mat_send[...] = mat[:, :, :, :, :, other].astype(LOW)
        reduce_copy(index, 0).start()

    def back_chunk(chunk):
        emit(2 * chunk, act.at[chunk], grad_low)

        def back_slot(slot):
            rows = slot_rows(slot)
            values = dot(grad_low[rows, :], weight(8 + chunk), 1, 1)
            rounded = (values * slope[chunk, rows, :].astype(SUM)).astype(LOW)
            slope[chunk, rows, :] = rounded
            row = pl.ds(8 + chunk, 1)
            vec_grad[row, :] += sum_rows(rounded.astype(SUM))

        each(4, back_slot)
        emit(2 * chunk + 1, hidden_low, slope.at[chunk])

        def back_hidden(slot):
            rows = slot_rows(slot)
            grad[rows, :] += dot(slope[chunk, rows, :], weight(4 + chunk), 1, 1)

        each(4, back_hidden)

    each(4, back_chunk)

    def back_norm(slot):
        rows = slot_rows(slot)
        total = grad[rows, :]
        unit_values = normed[rows, :]
        vec_grad[3:4, :] += sum_rows(total * unit_values)
        vec_grad[4:5, :] += sum_rows(total)
        scaled = total * vectors[3:4, :]
        inv = inverse[rows, 0:1]
        result = inv * (
            scaled - mean_lanes(scaled) - unit_values * mean_lanes(scaled * unit_values)
        )
        grad[rows, :] = result
        rounded = result.astype(LOW)
        grad_low[rows, :] = rounded
        vec_grad[2:3, :] += sum_rows(rounded.astype(SUM))

    each(4, back_norm)
    emit(8, context, grad_low)
    states = (moment1, moment2, weights)
    for quarter, array in enumerate(states):
        for chunk in range(PIECES):
            state_copy(array, normed, quarter, chunk).start()

    def back_context(slot):
        rows = slot_rows(slot)
        context[rows, :] = dot(grad_low[rows, :], weight(3), 1, 1).astype(LOW)

    each(4, back_context)

    def back_unit(unit):
        each(
            4,
            lambda slot: attend_back(unit, slot, valid(slot), qkv, context, log_total, vec_grad),
        )
        emit(9 + unit, token_low, qkv.at[unit])

    each(3, back_unit)

    order = ("twin", "along_x", "along_y", "near_z", "far_z")

    def vec_copy(stage):
        return send(
            vec_grad, vec_got.at[stage], vec_sent.at[stage], vec_arrived.at[stage], here[order[stage]]
        )

    def back_tokens(slot):
        rows = slot_rows(slot)
        pltpu.make_async_copy(side.at[rows, :], output.at[rows, :], out_sem.at[slot]).wait()
        total = grad[rows, :]
        for unit in range(3):
            total += dot(qkv[unit, rows, :], weight(unit), 1, 1)
        side[rows, :] = total
        pltpu.make_async_copy(side.at[rows, :], input_grad.at[rows, :], out_sem.at[slot]).start()

    def adapt(first, second, value, held):
        new_first = 0.5 * first + 0.5 * value
        new_second = 0.5 * second + 0.5 * value * value
        step = (new_first / CORRECTION) / (jnp.sqrt(new_second / CORRECTION) + 1e-06)
        if held is not None:
            step = step + 0.01 * held
        return new_first, new_second, step

    def lane_sums(values):
        total = sum_rows(values)
        return sum(total[:, 128 * index : 128 * index + 128] for index in range(6))

    def group_of(chunk):
        return 0 if chunk < 3 else 1 if chunk == 3 else 2 if chunk < 8 else 3

    def adapt_chunk(chunk):
        row = 4 + group_of(chunk)
        first, second, step = adapt(
            *(normed[state_rows(quarter, chunk), :] for quarter in (0, 1, 3, 2))
        )
        normed[state_rows(0, chunk), :] = first
        normed[state_rows(1, chunk), :] = second
        normed[state_rows(3, chunk), :] = step
        result_copy(new_moment1, 0, chunk).start()
        result_copy(new_moment2, 1, chunk).start()
        squares[row : row + 1, :] += lane_sums(step * step)

    def weight_squares():
        squares[...] = jnp.zeros_like(squares)
        for quarter, array in enumerate(states):
            for chunk in range(PIECES):
                state_copy(array, normed, quarter, chunk).wait()
        for chunk in range(PIECES):
            held = normed[state_rows(2, chunk), :]
            row = group_of(chunk)
            squares[row : row + 1, :] += lane_sums(held * held)

    def adapt_early():
        make_order(act)
        normed[state_rows(3, 3), :] = shares[pl.ds(24 * 8, 24), :]
        for chunk in range(4):
            normed[state_rows(3, 8 + chunk), :] = shares[pl.ds(24 * 2 * chunk, 24), :]
        for block in range(6):
            values = jnp.concatenate(
                [
                    shares[pl.ds(24 * (2 * chunk + 1), 24), block * 128 : block * 128 + 128]
                    for chunk in range(4)
                ],
                axis=1,
            )
            ordered = reorder(values, act, 0)
            for half in range(2):
                part = 2 * block + half
                lanes = slice(part % 3 * 256, part % 3 * 256 + 256)
                normed[state_rows(3, 4 + part // 3), lanes] = ordered[
                    :, half * 256 : half * 256 + 256
                ]
        for chunk in range(3, PIECES):
            adapt_chunk(chunk)

    def adapt_late():
        for unit in range(3):
            for half in range(2):
                for part in range(3):
                    lanes = slice((unit + 3 * half) * 128, (unit + 3 * half + 1) * 128)
                    source = slice((3 * half + part) * 128, (3 * half + part + 1) * 128)
                    normed[state_rows(3, part), lanes] = shares[pl.ds(24 * (9 + unit), 24), source]
        for chunk in range(3):
            adapt_chunk(chunk)

    def adapt_vectors():
        for block in range(6):
            values = jnp.concatenate(
                [
                    vec_grad[8 + chunk : 9 + chunk, block * 128 : block * 128 + 128]
                    for chunk in range(4)
                ],
                axis=1,
            )
            ordered = reorder(values, act, 0)
            for half in range(2):
                part = 2 * block + half
                lanes = slice(part % 3 * 256, part % 3 * 256 + 256)
                row = 8 + part // 3
                vec_got[0, row : row + 1, lanes] = ordered[:, half * 256 : half * 256 + 256]
        vec_got[0, 0:8, :] = vec_grad[0:8, :]
        first, second, step = adapt(
            vec_moment1[...], vec_moment2[...], vec_got[0, 0:12, :], None
        )
        new_vec_moment1[...] = first
        new_vec_moment2[...] = second
        new_vectors[...] = vectors[...] - 0.3 * step

    def square_copy(stage):
        return send(
            squares,
            squares_got.at[stage],
            square_sem.at[0, stage],
            square_sem.at[1, stage],
            here[order[stage]],
        )

    for step in range(6):
        if step > 0:
            vec_copy(step - 1).wait()
            vec_grad[...] += vec_got[step - 1]
        if step < 5:
            vec_copy(step).start()
        reduce(12 + step)
        if step < 4:
            back_tokens(step)
        if step == 0:
            weight_squares()
        if step == 3:
            adapt_early()
    adapt_late()
    for stage in range(5):
        square_copy(stage).start()
        if stage == 0:
            adapt_vectors()
        square_copy(stage).wait()
        squares[...] += squares_got[stage]
    norms = jnp.sqrt(jnp.sum(squares[...], axis=1, keepdims=True))
    ratio = norms[0:4] / (norms[4:8] + 1e-06)
    norm_pairs[:, 0:1] = norms[0:4]
    norm_pairs[:, 1:2] = norms[4:8]
    for group in range(4):
        trust[group] = ratio[group, 0]
    for chunk in range(PIECES):
        group = group_of(chunk)
        rows = state_rows(2, chunk)
        factor = 0.3 * ratio[group : group + 1, :]
        normed[rows, :] = normed[rows, :] - factor * normed[state_rows(3, chunk), :]
        result_copy(new_weights, 2, chunk).start()
    for quarter, array in enumerate((new_moment1, new_moment2, new_weights)):
        for chunk in range(PIECES):
            result_copy(array, quarter, chunk).wait()
    for slot in range(4):
        rows = slot_rows(slot)
        pltpu.make_async_copy(side.at[rows, :], input_grad.at[rows, :], out_sem.at[slot]).wait()


def fused(
    tokens,
    cotangent,
    lengths,
    null_flags,
    weights,
    moment1,
    moment2,
    vectors,
    vec_moment1,
    vec_moment2,
):
    rows = tokens.shape[0]
    vmem = pl.BlockSpec(memory_space=pltpu.VMEM)
    smem = pl.BlockSpec(memory_space=pltpu.SMEM)
    hbm = pl.BlockSpec(memory_space=pl.ANY)
    full = lambda *shape: pltpu.VMEM(shape, SUM)
    low = lambda *shape: pltpu.VMEM(shape, LOW)
    copies = lambda *shape: pltpu.SemaphoreType.DMA(shape)
    like = lambda array: jax.ShapeDtypeStruct(array.shape, array.dtype)
    return pl.pallas_call(
        layer,
        out_shape=[
            like(tokens),
            like(tokens),
            like(weights),
            like(weights),
            like(weights),
            like(vectors),
            like(vectors),
            like(vectors),
            jax.ShapeDtypeStruct((4, 2), SUM),
            jax.ShapeDtypeStruct((4,), SUM),
        ],
        in_specs=[smem, smem] + [hbm] * 5 + [vmem] * 3,
        out_specs=[hbm] * 5 + [vmem] * 4 + [smem],
        scratch_shapes=[
            low(PIECES, 2, 2, 2, 2, 48, TILE),
            full(rows, TILE),
            low(rows, TILE),
            low(3, rows, TILE),
            low(rows, TILE),
            low(rows, TILE),
            low(4, rows, TILE),
            low(4, rows, TILE),
            full(rows, TILE),
            low(rows, TILE),
            full(rows, TILE),
            full(rows, 128),
            full(3, 4, 4, SLOT),
            full(16, TILE),
            full(2, 2, 2, 2, 48, TILE),
            low(2, 2, 2, 2, 48, HALF),
            low(2, 2, 2, 2, 2, 48, HALF),
            full(2, 2, 2, 48, HALF),
            low(2, 2, 2, 48, HALF),
            low(2, 2, 2, 2, 48, HALF),
            full(2, 2, 48, HALF),
            low(2, 2, 48, HALF),
            low(2, 2, 2, 48, HALF),
            full(2, 48, HALF),
            low(2, 48, HALF),
            low(2, 2, 48, HALF),
            full(48, HALF),
            low(48, HALF),
            low(2, 48, HALF),
            full(48, HALF),
            full(SLOT, TILE),
            full(5, 16, TILE),
            full(3, 1, TILE),
            full(4, 1, TILE),
            full(8, 128),
            full(5, 8, 128),
            copies(2),
            copies(4),
            copies(2, 4),
            copies(PIECES, 6),
            copies(PIECES, 6),
            copies(5),
            copies(5, 2),
            copies(2, PIECES),
            copies(5),
            copies(5),
            copies(3, PIECES),
            copies(2, 5),
        ],
        compiler_params=pltpu.CompilerParams(
            collective_id=0, has_side_effects=True, vmem_limit_bytes=64 * 2**20
        ),
        cost_estimate=pl.CostEstimate(
            flops=60 * 10**9, bytes_accessed=60 * 10**6, transcendentals=10**7
        ),
    )(
        lengths,
        null_flags,
        tokens,
        cotangent,
        weights,
        moment1,
        moment2,
        vectors,
        vec_moment1,
        vec_moment2,
    )


def solution(mesh):
    split = P(("dp", "shard"), None)
    flat = P(("dp", "shard"))
    in_specs = (split, split, flat, flat, split, split, split, P(), P(), P())
    out_specs = (split,) * 5 + (P(),) * 5
    body = fused if mesh.shape["dp"] == 8 and mesh.shape["shard"] == 4 else plain
    return jax.shard_map(body, mesh=mesh, in_specs=in_specs, out_specs=out_specs, check_vma=False)
```

```python
import jax
import jax.numpy as jnp
from jax import lax
from jax.experimental import pallas as pl
from jax.experimental.pallas import tpu as pltpu
from jax.sharding import PartitionSpec as P

HEADS = 12
SLOT = 288
QLEN = 64
STEP = 5


def norm_forward(values, gain, shift):
    centred = values - jnp.mean(values, axis=-1, keepdims=True)
    inverse = lax.rsqrt(jnp.mean(centred * centred, axis=-1, keepdims=True) + 1e-05)
    normed = centred * inverse
    return (normed * gain + shift, normed, inverse)


def norm_backward(grad_result, normed, inverse, gain):
    scaled = grad_result * gain
    grad_gain = jnp.sum(grad_result * normed, axis=0)
    grad_shift = jnp.sum(grad_result, axis=0)
    centred = scaled - jnp.mean(scaled, axis=-1, keepdims=True)
    grad_input = inverse * (centred - normed * jnp.mean(scaled * normed, axis=-1, keepdims=True))
    return (grad_input, grad_gain, grad_shift)


def gelu_slope(values):
    return (
        0.5 * (1.0 + jax.scipy.special.erf(values * 0.7071067811865476))
        + values * jnp.exp(-0.5 * values * values) * 0.3989422804014327
    )


def plain(
    tokens,
    cotangent,
    lengths,
    null_flags,
    weights,
    moment1,
    moment2,
    vectors,
    vec_moment1,
    vec_moment2,
):
    model_width = tokens.shape[1]
    row_count = tokens.shape[0]
    slot_count = lengths.shape[0]
    head_size = model_width // HEADS
    score_scale = head_size ** (-0.5)
    block_slots = min(2, slot_count)
    block_count = slot_count // block_slots
    valid_len = jnp.where(null_flags == 1, QLEN, lengths)
    key_valid = jnp.arange(SLOT, dtype=jnp.int32)[None, :] < valid_len[:, None]
    key_blocks = key_valid.reshape(block_count, block_slots, SLOT)
    row_weight = key_valid.reshape(row_count, 1).astype(jnp.float32)
    qkv_bias = jnp.concatenate([vectors[0], jnp.zeros((model_width,), jnp.float32), vectors[1]])
    ffn_bias = vectors[8:12].reshape(4 * model_width)
    token_low = tokens.astype(jnp.bfloat16)

    def block_scores(qkv_block, valid_keys):
        scores = (
            jnp.einsum(
                "bqhd,bkhd->bhqk",
                qkv_block[:, :, 0],
                qkv_block[:, :, 1],
                preferred_element_type=jnp.float32,
            )
            * score_scale
        )
        return jnp.where(valid_keys[:, None, None, :], scores, -1000000000.0)

    def attend_block(packed):
        qkv_block, valid_keys = packed
        scores = block_scores(qkv_block, valid_keys)
        row_top = jnp.max(scores, axis=-1, keepdims=True)
        exponent = jnp.exp(scores - row_top)
        row_total = jnp.sum(exponent, axis=-1, keepdims=True)
        softmax_out = (exponent / row_total).astype(jnp.bfloat16)
        context = jnp.einsum(
            "bhqk,bkhd->bqhd", softmax_out, qkv_block[:, :, 2], preferred_element_type=jnp.float32
        )
        return (context.astype(jnp.bfloat16), (row_top + jnp.log(row_total))[..., 0])

    def attend_back(packed):
        qkv_block, valid_keys, log_block, grad_block = packed
        scores = block_scores(qkv_block, valid_keys)
        softmax_out = jnp.exp(scores - log_block[..., None])
        grad_values = jnp.einsum(
            "bhqk,bqhd->bkhd",
            softmax_out.astype(jnp.bfloat16),
            grad_block,
            preferred_element_type=jnp.float32,
        )
        grad_soft = jnp.einsum(
            "bqhd,bkhd->bhqk", grad_block, qkv_block[:, :, 2], preferred_element_type=jnp.float32
        )
        grad_scores = softmax_out * (
            grad_soft - jnp.sum(grad_soft * softmax_out, axis=-1, keepdims=True)
        )
        scores_low = grad_scores.astype(jnp.bfloat16)
        grad_query = (
            jnp.einsum(
                "bhqk,bkhd->bqhd",
                scores_low,
                qkv_block[:, :, 1],
                preferred_element_type=jnp.float32,
            )
            * score_scale
        )
        grad_keys = (
            jnp.einsum(
                "bhqk,bqhd->bkhd",
                scores_low,
                qkv_block[:, :, 0],
                preferred_element_type=jnp.float32,
            )
            * score_scale
        )
        return jnp.stack([grad_query, grad_keys, grad_values], axis=2).astype(jnp.bfloat16)

    gathered = lax.all_gather(weights.astype(jnp.bfloat16), ("dp", "shard"), axis=0, tiled=True)
    first_mats = (
        gathered[:, : 3 * model_width],
        gathered[:, 3 * model_width : 4 * model_width],
        gathered[:, 4 * model_width : 8 * model_width],
        gathered[:, 8 * model_width :].reshape(4 * model_width, model_width),
    )
    w_qkv, w_out, w_in, w_down = first_mats
    qkv_low = (jnp.dot(token_low, w_qkv, preferred_element_type=jnp.float32) + qkv_bias).astype(
        jnp.bfloat16
    )
    qkv_blocks = qkv_low.reshape(block_count, block_slots, SLOT, 3, HEADS, head_size)
    contexts, log_total = lax.map(attend_block, (qkv_blocks, key_blocks))
    context_low = contexts.reshape(row_count, model_width)
    attention = jnp.dot(context_low, w_out, preferred_element_type=jnp.float32) + vectors[2]
    hidden_one, normed_one, inverse_one = norm_forward(tokens + attention, vectors[3], vectors[4])
    hidden_low = hidden_one.astype(jnp.bfloat16)
    pre_act = jnp.dot(hidden_low, w_in, preferred_element_type=jnp.float32) + ffn_bias
    act_low = jax.nn.gelu(pre_act, approximate=False).astype(jnp.bfloat16)
    ffn_out = jnp.dot(act_low, w_down, preferred_element_type=jnp.float32) + vectors[5]
    result, normed_two, inverse_two = norm_forward(hidden_one + ffn_out, vectors[6], vectors[7])
    first_kept = (
        qkv_blocks,
        log_total,
        context_low,
        normed_one,
        inverse_one,
        hidden_low,
        pre_act,
        act_low,
        normed_two,
        inverse_two,
        result,
    )
    output = first_kept[10]
    w_qkv, w_out, w_in, w_down = first_mats
    (
        qkv_blocks,
        log_total,
        context_low,
        normed_one,
        inverse_one,
        hidden_low,
        pre_act,
        act_low,
        normed_two,
        inverse_two,
    ) = first_kept[:10]
    grad_result = cotangent * row_weight
    grad_two, grad_gain_two, grad_shift_two = norm_backward(
        grad_result, normed_two, inverse_two, vectors[6]
    )
    grad_ffn_low = grad_two.astype(jnp.bfloat16)
    grad_bias_down = jnp.sum(grad_ffn_low, axis=0, dtype=jnp.float32)
    grad_down = jnp.einsum("tf,td->fd", act_low, grad_ffn_low, preferred_element_type=jnp.float32)
    grad_act = jnp.einsum("td,fd->tf", grad_ffn_low, w_down, preferred_element_type=jnp.float32)
    grad_pre_low = (grad_act * gelu_slope(pre_act)).astype(jnp.bfloat16)
    grad_bias_in = jnp.sum(grad_pre_low, axis=0, dtype=jnp.float32)
    grad_in = jnp.einsum("td,tf->df", hidden_low, grad_pre_low, preferred_element_type=jnp.float32)
    grad_hidden = grad_two + jnp.einsum(
        "tf,df->td", grad_pre_low, w_in, preferred_element_type=jnp.float32
    )
    grad_residual, grad_gain_one, grad_shift_one = norm_backward(
        grad_hidden, normed_one, inverse_one, vectors[3]
    )
    grad_attn_low = grad_residual.astype(jnp.bfloat16)
    grad_bias_out = jnp.sum(grad_attn_low, axis=0, dtype=jnp.float32)
    grad_out = jnp.einsum(
        "tc,td->cd", context_low, grad_attn_low, preferred_element_type=jnp.float32
    )
    grad_context = jnp.einsum(
        "td,cd->tc", grad_attn_low, w_out, preferred_element_type=jnp.float32
    ).astype(jnp.bfloat16)
    grad_blocks = grad_context.reshape(block_count, block_slots, SLOT, HEADS, head_size)
    grad_qkv_low = lax.map(attend_back, (qkv_blocks, key_blocks, log_total, grad_blocks)).reshape(
        row_count, 3 * model_width
    )
    grad_bias_qkv = jnp.sum(grad_qkv_low, axis=0, dtype=jnp.float32)
    grad_qkv = jnp.einsum("td,te->de", token_low, grad_qkv_low, preferred_element_type=jnp.float32)
    input_grad = grad_residual + jnp.einsum(
        "te,de->td", grad_qkv_low, w_qkv, preferred_element_type=jnp.float32
    )
    vector_grad = jnp.concatenate(
        [
            jnp.stack(
                [
                    grad_bias_qkv[:model_width],
                    grad_bias_qkv[2 * model_width :],
                    grad_bias_out,
                    grad_gain_one,
                    grad_shift_one,
                    grad_bias_down,
                    grad_gain_two,
                    grad_shift_two,
                ]
            ),
            grad_bias_in.reshape(4, model_width),
        ],
        axis=0,
    )
    qkv_shard, out_shard, in_shard, down_shard = (
        lax.psum_scatter(grad_qkv, ("dp", "shard"), scatter_dimension=0, tiled=True),
        lax.psum_scatter(grad_out, ("dp", "shard"), scatter_dimension=0, tiled=True),
        lax.psum_scatter(grad_in, ("dp", "shard"), scatter_dimension=0, tiled=True),
        lax.psum_scatter(
            grad_down.reshape(model_width, 4 * model_width),
            ("dp", "shard"),
            scatter_dimension=0,
            tiled=True,
        ),
    )
    vector_total = lax.psum(vector_grad, ("dp", "shard"))
    grad_shard = jnp.concatenate([qkv_shard, out_shard, in_shard, down_shard], axis=1)
    correction = 1.0 - 0.5**STEP
    new_first = 0.5 * moment1 + 0.5 * grad_shard
    new_second = 0.5 * moment2 + 0.5 * grad_shard * grad_shard
    update = new_first / correction / (jnp.sqrt(new_second / correction) + 1e-06) + 0.01 * weights
    column_edges = (0, 3 * model_width, 4 * model_width, 8 * model_width, 12 * model_width)
    pair_rows = []
    for group_index in range(4):
        weight_part = weights[:, column_edges[group_index] : column_edges[group_index + 1]]
        update_part = update[:, column_edges[group_index] : column_edges[group_index + 1]]
        pair_rows.append(
            jnp.stack([jnp.sum(weight_part * weight_part), jnp.sum(update_part * update_part)])
        )
    pair_squares = jnp.stack(pair_rows)
    pair_total = lax.psum(pair_squares, ("dp", "shard"))
    norm_pairs = jnp.sqrt(pair_total)
    trust_ratio = norm_pairs[:, 0] / (norm_pairs[:, 1] + 1e-06)
    column_trust = jnp.concatenate(
        [
            jnp.ones((column_edges[group_index + 1] - column_edges[group_index],), jnp.float32)
            * trust_ratio[group_index]
            for group_index in range(4)
        ]
    )
    new_weights = weights - 0.3 * column_trust * update
    vec_first = 0.5 * vec_moment1 + 0.5 * vector_total
    vec_second = 0.5 * vec_moment2 + 0.5 * vector_total * vector_total
    new_vectors = vectors - 0.3 * (vec_first / correction) / (
        jnp.sqrt(vec_second / correction) + 1e-06
    )
    return (
        output,
        input_grad,
        new_first,
        new_second,
        new_weights,
        vec_first,
        vec_second,
        new_vectors,
        norm_pairs,
        trust_ratio,
    )


SUM = jnp.float32
LOW = jnp.bfloat16
PIECES = 12
TILE = 768
HALF = 384
NEG = -1e9
CORRECTION = 1.0 - 0.5**STEP


def dot(left, right, left_dim, right_dim):
    return lax.dot_general(
        left, right, (((left_dim,), (right_dim,)), ((), ())), preferred_element_type=SUM
    )


def slot_rows(slot):
    return pl.ds(pl.multiple_of(slot * SLOT, SLOT), SLOT)


def each(count, body, unroll=1):
    def step(index, carry):
        body(index)
        return carry

    lax.fori_loop(0, count, step, 0, unroll=unroll)


def mean_lanes(values):
    return jnp.mean(values, axis=-1, keepdims=True)


def sum_rows(values):
    return jnp.sum(values, axis=0, keepdims=True)


def head_operands(query, key, valid):
    lane = lax.broadcasted_iota(jnp.int32, query.shape, 1)
    row = lax.broadcasted_iota(jnp.int32, query.shape, 0)
    low_head = lane < 64
    bias = jnp.where(row < valid, 0.0, NEG).astype(LOW)
    scaled = query * jnp.asarray(0.125, LOW)
    one, zero = jnp.ones_like(query), jnp.zeros_like(query)
    queries = (
        jnp.where(low_head, scaled, jnp.where(lane == 64, one, zero)),
        jnp.where(low_head, jnp.where(lane == 0, one, zero), scaled),
    )
    keys = (
        jnp.where(low_head, key, jnp.where(lane == 64, bias, zero)),
        jnp.where(low_head, jnp.where(lane == 0, bias, zero), key),
    )
    return queries, keys, low_head


def attend(unit, slot, valid, qkv, context, log_total):
    rows = slot_rows(slot)
    items = []
    for half in range(2):
        query, key, value = (
            qkv[unit, rows, (3 * half + part) * 128 : (3 * half + part + 1) * 128]
            for part in range(3)
        )
        queries, keys, low_head = head_operands(query, key, valid)
        items += [(queries[head], keys[head], value) for head in range(2)]
    scores = [dot(key, query, 1, 1) for query, key, _ in items]
    results = []
    for index, values in enumerate(scores):
        top = jnp.max(values, axis=0, keepdims=True)
        exponent = jnp.exp(values - top)
        total = sum_rows(exponent)
        log_total[unit, slot, index : index + 1, :] = top + jnp.log(total)
        results.append((exponent * (1.0 / total)).astype(LOW))
    results = [dot(probs, item[2], 0, 0) for probs, item in zip(results, items)]
    for half in range(2):
        lanes = pl.ds(pl.multiple_of((unit + 3 * half) * 128, 128), 128)
        joined = jnp.where(low_head, results[2 * half], results[2 * half + 1])
        context[rows, lanes] = joined.astype(LOW)


def attend_back(unit, slot, valid, qkv, grad_context, log_total, vec_grad):
    rows = slot_rows(slot)
    for half in range(2):
        query, key, value = (
            qkv[unit, rows, (3 * half + part) * 128 : (3 * half + part + 1) * 128]
            for part in range(3)
        )
        lanes = pl.ds(pl.multiple_of((unit + 3 * half) * 128, 128), 128)
        grad = grad_context[rows, lanes]
        queries, keys, low_head = head_operands(query, key, valid)
        zero = jnp.zeros_like(grad)
        grads = (jnp.where(low_head, grad, zero), jnp.where(low_head, zero, grad))
        scores = [dot(keys[head], queries[head], 1, 1) for head in range(2)]
        grad_probs = [dot(value, grads[head], 1, 1) for head in range(2)]
        probs, grad_value = [], []
        for head in range(2):
            index = 2 * half + head
            probs.append(jnp.exp(scores[head] - log_total[unit, slot, index : index + 1, :]))
            grad_value.append(dot(probs[head].astype(LOW), grad, 1, 0))
        grad_key, grad_query = [], []
        for head in range(2):
            inner = sum_rows(grad_probs[head] * probs[head])
            low = (probs[head] * (grad_probs[head] - inner)).astype(LOW)
            grad_key.append(dot(low, query, 1, 0))
            grad_query.append(dot(low, key, 0, 0))
        for part, parts, scale in (
            (0, grad_query, 0.125),
            (1, grad_key, 0.125),
            (2, grad_value, 1.0),
        ):
            joined = (jnp.where(low_head, parts[0], parts[1]) * scale).astype(LOW)
            qkv[unit, rows, (3 * half + part) * 128 : (3 * half + part + 1) * 128] = joined
            if part != 1:
                row = part // 2
                vec_grad[row : row + 1, lanes] += sum_rows(joined.astype(SUM))


def make_order(buffer):
    row = lax.broadcasted_iota(jnp.int32, (512, 512), 0)
    column = lax.broadcasted_iota(jnp.int32, (512, 512), 1)
    chosen = column == 4 * (row % 128) + row // 128
    buffer[0, 0:512, 0:512] = jnp.where(chosen, 1.0, 0.0).astype(LOW)


def reorder(values, buffer, side):
    first = values.astype(LOW)
    rest = values - first.astype(SUM)
    second = rest.astype(LOW)
    third = (rest - second.astype(SUM)).astype(LOW)
    order = buffer[0, 0:512, 0:512]
    return (dot(first, order, 1, side) + dot(second, order, 1, side)) + dot(third, order, 1, side)


def place():
    outer, inner = lax.axis_index("dp"), lax.axis_index("shard")
    z, y, x, core = outer // 2, outer % 2, inner // 2, inner % 2
    here = dict(z=z, y=y, x=x, core=core, high=z // 2, low=z % 2)
    here["y1"], here["x1"] = y + core * (1 - 2 * y), x + (1 - core) * (1 - 2 * x)
    here["y2"], here["x2"] = y + (1 - core) * (1 - 2 * y), x + core * (1 - 2 * x)
    device = lambda z, y, x, core: (z * 2 + y, x * 2 + core)
    here["twin"] = device(z, y, x, 1 - core)
    here["near_z"] = device(z + 1 - 2 * (z % 2), y, x, core)
    here["far_z"] = device((z + 2) % 4, y, x, core)
    here["first"] = device(z, here["y1"], here["x1"], core)
    here["second"] = device(z, here["y2"], here["x2"], core)
    here["along_x"] = device(z, y, 1 - x, core)
    here["along_y"] = device(z, 1 - y, x, core)
    here["line_group"] = (
        z * 2 + core, 8, lambda index: device(index // 2, y, x, index % 2)
    )
    here["plane_group"] = (
        y * 2 + x, 4, lambda index: device(z, index // 2, index % 2, core)
    )
    here["mine"] = pl.ds(pl.multiple_of(core * HALF, 128), HALF)
    here["other"] = pl.ds(pl.multiple_of((1 - core) * HALF, 128), HALF)
    return here


def send(source, target, sent, arrived, device):
    return pltpu.make_async_remote_copy(
        src_ref=source,
        dst_ref=target,
        send_sem=sent,
        recv_sem=arrived,
        device_id=device,
        device_id_type=pl.DeviceIdType.MESH,
    )


def inside(index):
    if isinstance(index, int):
        return 0 <= index < PIECES
    return jnp.logical_and(index >= 0, index < PIECES)


def guarded(index, body):
    if isinstance(index, int):
        if inside(index):
            body(index)
    else:
        pl.when(inside(index))(lambda: body(index))


def layer(
    lengths, null_flags, tokens, cotangent, weights, moment1, moment2, vectors, vec_moment1,
    vec_moment2,
    output, input_grad, new_moment1, new_moment2, update, new_vec_moment1, new_vec_moment2,
    new_vectors, norm_pairs, trust,
    walls, normed, token_low, qkv, context, hidden_low, act, slope, grad, grad_low, side, inverse,
    log_total, vec_grad, mat, mat_send, mat_got, pair_keep, pair_send, pair_got,
    line_keep, line_send, line_got, z_keep, z_send, z_got,
    shares, qkv_bias, ffn_bias, squares, squares_got,
    in_sem, out_sem, twin_sem, gather_sent, gather_got, reduce_sent, reduce_got,
    vec_sem, state_sem, square_sem, cot_sem,
):
    here = place()
    z, y, x, core, high, low = (here[name] for name in ("z", "y", "x", "core", "high", "low"))
    y1, x1, y2, x2 = (here[name] for name in ("y1", "x1", "y2", "x2"))
    mine, other = here["mine"], here["other"]

    def valid(slot):
        return jnp.where(null_flags[slot] == 1, QLEN, lengths[slot])

    def state_rows(quarter, chunk):
        return pl.ds(quarter * SLOT + 24 * chunk, 24)

    def state_copy(array, buffer, quarter, chunk):
        return pltpu.make_async_copy(
            array.at[:, pl.ds(TILE * chunk, TILE)],
            buffer.at[state_rows(quarter, chunk), :],
            state_sem.at[quarter, chunk],
        )

    def result_copy(array, quarter, chunk):
        return pltpu.make_async_copy(
            normed.at[state_rows(quarter, chunk), :],
            array.at[:, pl.ds(TILE * chunk, TILE)],
            state_sem.at[quarter, chunk],
        )

    for chunk in range(PIECES):
        state_copy(weights, grad, 0, chunk).start()
    def cot_copy(slot):
        return pltpu.make_async_copy(
            cotangent.at[slot_rows(slot), :], side.at[slot % 2], cot_sem.at[slot]
        )

    def output_copy(slot):
        return pltpu.make_async_copy(
            side.at[slot % 2], output.at[slot_rows(slot), :], out_sem.at[slot]
        )

    def grad_copy(slot):
        rows = slot_rows(slot)
        return pltpu.make_async_copy(grad.at[rows, :], input_grad.at[rows, :], out_sem.at[slot])

    for slot in range(2):
        cot_copy(slot).start()
    tok_copy = pltpu.make_async_copy(tokens, normed, in_sem.at[1])
    tok_copy.start()

    barrier = pltpu.get_barrier_semaphore()
    peers = []
    for group in ("line_group", "plane_group"):
        index, size, device_of = here[group]
        peers += [device_of((index + step) % size) for step in range(1, size)]
    for peer in peers:
        pl.semaphore_signal(barrier, inc=1, device_id=peer, device_id_type=pl.DeviceIdType.MESH)
    pl.semaphore_wait(barrier, len(peers))

    for chunk in range(PIECES):
        state_copy(weights, grad, 0, chunk).wait()
    for unit in range(3):
        for half in range(2):
            for part in range(3):
                lanes = slice((unit + 3 * half) * 128, (unit + 3 * half + 1) * 128)
                place_lanes = slice((3 * half + part) * 128, (3 * half + part + 1) * 128)
                grad[state_rows(1, unit), place_lanes] = grad[state_rows(0, part), lanes]

    def swap(first, count):
        rows = pl.ds(24 * first, 24 * count)
        return send(
            grad.at[pl.ds(SLOT + 24 * first, 24 * count), other],
            shares.at[rows, other],
            twin_sem.at[0, first],
            twin_sem.at[1, first],
            here["twin"],
        )

    swap(0, 3).start()
    def fill(piece):
        rows = pl.ds(pl.multiple_of(24 * piece, 8), 24)
        own, twin = grad[pl.ds(pl.multiple_of(SLOT + 24 * piece, 8), 24), mine], shares[rows, mine]
        upper = jnp.where(core == 0, own, twin)
        lower = jnp.where(core == 0, twin, own)
        joined = jnp.concatenate([upper, lower], axis=0)
        walls[piece, high, low, y, x, :, mine] = joined.astype(LOW)

    swap(0, 3).wait()
    each(3, fill)

    own, line = (high, low, y, x), (slice(None), low, y, x)
    column, next_column = (slice(None), slice(None), y, x), (slice(None), slice(None), y1, x1)
    everything = (slice(None),) * 4
    paths = (
        (
            ((own, "far_z"),),
            ((line, "near_z"),),
            ((column, "first"), (column, "second")),
            ((next_column, "second"),),
            ((everything, "twin"),),
        ),
        (
            ((own, "first"), (own, "far_z")),
            (((high, low, y1, x1), "far_z"), (line, "near_z")),
            (((slice(None), low, y1, x1), "near_z"), (column, "second")),
            ((next_column, "second"),),
            ((everything, "twin"),),
        ),
    )

    def gather_copies(piece, path, stage):
        first = sum(len(copies) for copies in paths[path][:stage])
        copies = []
        for index, (blocks, device) in enumerate(paths[path][stage]):
            part = walls.at[(piece,) + blocks + (slice(None), mine)]
            sent, got = (
                array.at[piece, first + index] for array in (gather_sent, gather_got)
            )
            copies.append(send(part, part, sent, got, here[device]))
        return copies

    def gather(notch):
        def advance(piece, path, stage):
            if stage > 0:
                for copy in gather_copies(piece, path, stage - 1):
                    copy.wait_recv()
            if stage < 5:
                for copy in gather_copies(piece, path, stage):
                    copy.start()
            else:
                for done in range(5):
                    for copy in gather_copies(piece, path, done):
                        copy.wait_send()

        for stage in range(6):

            def step(piece, stage=stage):
                if isinstance(piece, int):
                    advance(piece, min(piece % 3, 1), stage)
                else:
                    turn = lax.rem(piece, 3)
                    pl.when(turn == 0)(lambda: advance(piece, 0, stage))
                    pl.when(turn != 0)(lambda: advance(piece, 1, stage))

            guarded(notch - 2 * stage, step)

    def weight(piece):
        return walls[piece].reshape(TILE, TILE)

    gather(0)
    make_order(act)
    for block in range(6):
        values = jnp.concatenate(
            [
                grad[state_rows(0, 4 + part // 3), part % 3 * 256 : part % 3 * 256 + 256]
                for part in (2 * block, 2 * block + 1)
            ],
            axis=1,
        )
        ordered = dot(values.astype(LOW), act[0, 0:512, 0:512], 1, 1)
        for chunk in range(4):
            grad[state_rows(1, 4 + chunk), block * 128 : block * 128 + 128] = ordered[
                :, chunk * 128 : chunk * 128 + 128
            ]
    for chunk in (3, 8, 9, 10, 11):
        grad[state_rows(1, chunk), :] = grad[state_rows(0, chunk), :]
    swap(3, 9).start()
    gather(1)
    vec_grad[...] = jnp.zeros_like(vec_grad)
    for unit in range(3):
        for half in range(2):
            lanes = slice((unit + 3 * half) * 128, (unit + 3 * half + 1) * 128)
            for part, row in ((0, 0), (2, 1)):
                target = slice((3 * half + part) * 128, (3 * half + part + 1) * 128)
                qkv_bias[unit, :, target] = vectors[row : row + 1, lanes]
            target = slice((3 * half + 1) * 128, (3 * half + 2) * 128)
            qkv_bias[unit, :, target] = jnp.zeros((1, 128), SUM)
    for block in range(6):
        values = jnp.concatenate(
            [
                vectors[8 + part // 3 : 9 + part // 3, part % 3 * 256 : part % 3 * 256 + 256]
                for part in (2 * block, 2 * block + 1)
            ],
            axis=1,
        )
        ordered = reorder(values, act, 1)
        for chunk in range(4):
            ffn_bias[chunk, :, block * 128 : block * 128 + 128] = ordered[
                :, chunk * 128 : chunk * 128 + 128
            ]

    gather(2)
    swap(3, 9).wait()
    each(9, lambda piece: fill(3 + piece))
    gather(3)
    tok_copy.wait()

    def cast_slot(slot):
        rows = slot_rows(slot)
        token_low[rows, :] = normed[rows, :].astype(LOW)

    each(4, cast_slot, 4)
    for notch in range(4, 11):
        gather(notch)

    def project(unit):
        def project_slot(slot):
            rows = slot_rows(slot)
            values = dot(token_low[rows, :], weight(unit), 1, 0) + qkv_bias[unit]
            qkv[unit, rows, :] = values.astype(LOW)

        each(4, project_slot, 4)

        def attend_slots(pair):
            for slot in range(2):
                index = 2 * pair + slot
                attend(unit, index, valid(index), qkv, context, log_total)
            pl.when(pair == 0)(lambda: gather(11 + unit))

        each(2, attend_slots)

    each(3, project)

    def attend_out(slot):
        rows = slot_rows(slot)
        values = normed[rows, :] + (dot(context[rows, :], weight(3), 1, 0) + vectors[2:3, :])
        centred = values - mean_lanes(values)
        inv = lax.rsqrt(mean_lanes(centred * centred) + 1e-05)
        unit_values = centred * inv
        normed[rows, :] = unit_values
        inverse[rows, :] = jnp.broadcast_to(inv, (SLOT, 128))
        hidden_low[rows, :] = (unit_values * vectors[3:4, :] + vectors[4:5, :]).astype(LOW)

    gather(14)
    each(4, attend_out, 2)

    def widen(chunk):
        gather(15 + chunk)

        def widen_slot(slot):
            rows = slot_rows(slot)
            pre = dot(hidden_low[rows, :], weight(4 + chunk), 1, 0) + ffn_bias[chunk]
            phi = 0.5 + 0.5 * lax.erf(pre * 0.7071067811865476)
            act[chunk, rows, :] = (pre * phi).astype(LOW)
            bell = jnp.exp(pre * pre * -0.5) * 0.3989422804014327
            slope[chunk, rows, :] = (phi + pre * bell).astype(LOW)

        each(4, widen_slot, 4)

    each(4, widen, 4)
    def narrow_first(slot):
        rows = slot_rows(slot)
        start = normed[rows, :] * vectors[3:4, :] + (vectors[4:5, :] + vectors[5:6, :])
        grad[rows, :] = start + dot(act[0, rows, :], weight(8), 1, 0)

    gather(19)
    each(4, narrow_first, 4)

    def narrow(chunk):
        def narrow_slot(slot):
            rows = slot_rows(slot)
            grad[rows, :] += dot(act[1 + chunk, rows, :], weight(9 + chunk), 1, 0)

        each(4, narrow_slot, 4)

    gather(20)
    each(2, narrow)
    gather(21)

    def finish_slot(slot):
        rows = slot_rows(slot)
        if 1 <= slot < 3:
            output_copy(slot - 1).wait()
            cot_copy(slot + 1).start()
        values = grad[rows, :] + dot(act[3, rows, :], weight(11), 1, 0)
        centred = values - mean_lanes(values)
        inv = lax.rsqrt(mean_lanes(centred * centred) + 1e-05)
        unit_values = centred * inv
        kept = lax.broadcasted_iota(jnp.int32, (SLOT, 1), 0) < valid(slot)
        cot_copy(slot).wait()
        grad_out = jnp.where(kept, side[slot % 2], 0.0)
        side[slot % 2] = unit_values * vectors[6:7, :] + vectors[7:8, :]
        output_copy(slot).start()
        vec_grad[6:7, :] += sum_rows(grad_out * unit_values)
        vec_grad[7:8, :] += sum_rows(grad_out)
        scaled = grad_out * vectors[6:7, :]
        result = inv * (
            scaled - mean_lanes(scaled) - unit_values * mean_lanes(scaled * unit_values)
        )
        grad[rows, :] = result
        rounded = result.astype(LOW)
        grad_low[rows, :] = rounded
        vec_grad[5:6, :] += sum_rows(rounded.astype(SUM))

    for slot in range(4):
        finish_slot(slot)
    output_copy(2).wait()
    output_copy(3).wait()

    def turn_of(index, count):
        return index % count if isinstance(index, int) else lax.rem(index, count)

    def reduce_copies(index, stage):
        two, four = turn_of(index, 2), turn_of(index, 4)
        if stage == 3:
            triples = [
                (line_z(step), z_send.at[two, step - 1], z_got.at[four, step - 1])
                for step in range(1, 4)
            ]
        else:
            triples = [
                (
                    (here["twin"], mat_send, mat_got.at[two]),
                    (here["second"], pair_send.at[two], pair_got.at[four]),
                    (here["first"], line_send.at[two], line_got.at[four]),
                )[stage]
            ]
        return [
            send(
                source,
                target,
                reduce_sent.at[stage + step, two],
                reduce_got.at[stage + step, four],
                device,
            )
            for step, (device, source, target) in enumerate(triples)
        ]

    def line_z(step):
        return ((z + step) % 4 * 2 + y, x * 2 + core)

    def begin(index, stage):
        for copy in reduce_copies(index, stage):
            copy.start()

    def end(index, stage):
        for copy in reduce_copies(index, stage):
            copy.wait()

    def folded(rows):
        return jnp.concatenate([rows[..., :HALF], rows[..., HALF:]], axis=-2)

    def reduce(notch):
        def first(index):
            end(index, 0)
            turn, got = turn_of(index, 2), turn_of(index, 2)

            ours = pl.ds(pl.multiple_of(24 * core, 8), 24)

            def column(row, col):
                own_rows = folded(mat[:, :, row, col, ours, :])
                return own_rows + mat_got[got, :, :, row, col].astype(SUM)

            pair_send[turn, 0] = column(y2, x2).astype(LOW)
            pair_send[turn, 1] = column(1 - y, 1 - x).astype(LOW)
            begin(index, 1)
            pair_keep[turn, 0] = column(y, x)
            pair_keep[turn, 1] = column(y1, x1)

        def third(index):
            end(index, 2)
            turn, got = turn_of(index, 2), turn_of(index, 4)

            def block(place):
                row, col = place // 2, place % 2
                return line_keep[turn, row, col] + line_got[got, row, col].astype(SUM)

            for step in range(1, 4):
                z_send[turn, step - 1] = block((z + step) % 4).astype(LOW)
            begin(index, 3)
            z_keep[turn] = block(z)

        guarded(notch - 4, third)
        guarded(notch - 1, first)

    def reduce_odd(notch):
        def second(index):
            end(index, 1)
            turn, got = turn_of(index, 2), turn_of(index, 4)
            line_send[turn] = (pair_keep[turn, 1] + pair_got[got, 1].astype(SUM)).astype(LOW)
            begin(index, 2)
            line_keep[turn] = pair_keep[turn, 0] + pair_got[got, 0].astype(SUM)

        def fourth(index):
            end(index, 3)
            turn, got = turn_of(index, 2), turn_of(index, 4)
            total = z_keep[turn]
            for step in range(3):
                total += z_got[got, step].astype(SUM)
            rows = pl.ds(pl.multiple_of(24 * index, 8), 24)
            shares[rows, :HALF] = total[:24]
            shares[rows, HALF:] = total[24:]

        guarded(notch - 2, second)
        guarded(notch - 5, fourth)

    def emit(index, left, right, unroll=2):
        reduce(index)
        shape = mat.shape[1:]


        def multiply(part):
            lanes = pl.ds(pl.multiple_of(part * HALF, 128), HALF)
            mat[part] = dot(left[:, lanes], right[...], 0, 0).reshape(shape)

        each(2, multiply, unroll)
        theirs = pl.ds(pl.multiple_of(24 * (1 - core), 8), 24)
        for part in range(2):
            mat_send[part] = folded(mat[part, :, :, :, theirs, :]).astype(LOW)
        begin(index, 0)
        reduce_odd(index)

    def back_chunk(chunk):
        emit(2 * chunk, act.at[chunk], grad_low)

        def back_slot(slot):
            rows = slot_rows(slot)
            values = dot(grad_low[rows, :], weight(8 + chunk), 1, 1)
            rounded = (values * slope[chunk, rows, :].astype(SUM)).astype(LOW)
            slope[chunk, rows, :] = rounded
            row = pl.ds(8 + chunk, 1)
            vec_grad[row, :] += sum_rows(rounded.astype(SUM))

        each(4, back_slot, 4)
        emit(2 * chunk + 1, hidden_low, slope.at[chunk])

        def back_hidden(slot):
            rows = slot_rows(slot)
            grad[rows, :] += dot(slope[chunk, rows, :], weight(4 + chunk), 1, 1)

        each(4, back_hidden, 4)

    each(4, back_chunk, 4)

    def back_norm(slot):
        rows = slot_rows(slot)
        total = grad[rows, :]
        unit_values = normed[rows, :]
        vec_grad[3:4, :] += sum_rows(total * unit_values)
        vec_grad[4:5, :] += sum_rows(total)
        scaled = total * vectors[3:4, :]
        inv = inverse[rows, 0:1]
        result = inv * (
            scaled - mean_lanes(scaled) - unit_values * mean_lanes(scaled * unit_values)
        )
        grad[rows, :] = result
        rounded = result.astype(LOW)
        grad_low[rows, :] = rounded
        vec_grad[2:3, :] += sum_rows(rounded.astype(SUM))

    each(4, back_norm, 2)
    emit(8, context, grad_low)
    states = (moment1, moment2, weights)
    for quarter, array in enumerate(states):
        for chunk in range(PIECES):
            state_copy(array, normed, quarter, chunk).start()

    def back_context(slot):
        rows = slot_rows(slot)
        context[rows, :] = dot(grad_low[rows, :], weight(3), 1, 1).astype(LOW)

    each(4, back_context, 4)

    def back_unit(unit):
        each(
            4,
            lambda slot: attend_back(unit, slot, valid(slot), qkv, context, log_total, vec_grad),
        )
        emit(9 + unit, token_low, qkv.at[unit], 1)

    each(3, back_unit)

    def exchange(group, source, slots, sems):
        index, size, device_of = here[group]

        def copies(outgoing):
            found = []
            for step in range(1, size):
                other_index = (index + (step if outgoing else size - step)) % size
                found.append(
                    send(
                        source,
                        slots(index if outgoing else other_index),
                        sems.at[0, step],
                        sems.at[1, index if outgoing else other_index],
                        device_of(other_index),
                    )
                )
            return found

        def start():
            for copy in copies(True):
                copy.start()
            slots(index)[...] = source[...]

        def wait():
            for copy in copies(True):
                copy.wait_send()
            for copy in copies(False):
                copy.wait_recv()
            total = slots(0)[...]
            for slot in range(1, size):
                total += slots(slot)[...]
            source[...] = total

        return start, wait

    def back_tokens(slot):
        rows = slot_rows(slot)
        total = grad[rows, :]
        for unit in range(3):
            total += dot(qkv[unit, rows, :], weight(unit), 1, 1)
        grad[rows, :] = total
        grad_copy(slot).start()

    def adapt(first, second, value, held):
        new_first = 0.5 * first + 0.5 * value
        new_second = 0.5 * second + 0.5 * value * value
        step = (new_first / CORRECTION) / (jnp.sqrt(new_second / CORRECTION) + 1e-06)
        if held is not None:
            step = step + 0.01 * held
        return new_first, new_second, step

    def lane_sums(values):
        total = sum_rows(values)
        return sum(total[:, 128 * index : 128 * index + 128] for index in range(6))

    def group_of(chunk):
        return 0 if chunk < 3 else 1 if chunk == 3 else 2 if chunk < 8 else 3

    def adapt_chunk(chunk):
        row = 4 + group_of(chunk)
        first, second, step = adapt(
            *(normed[state_rows(quarter, chunk), :] for quarter in (0, 1, 3, 2))
        )
        normed[state_rows(0, chunk), :] = first
        normed[state_rows(1, chunk), :] = second
        normed[state_rows(3, chunk), :] = step
        result_copy(new_moment1, 0, chunk).start()
        result_copy(new_moment2, 1, chunk).start()
        result_copy(update, 3, chunk).start()
        squares[row : row + 1, :] += lane_sums(step * step)

    def weight_squares():
        squares[...] = jnp.zeros_like(squares)
        for quarter, array in enumerate(states):
            for chunk in range(PIECES):
                state_copy(array, normed, quarter, chunk).wait()
        for chunk in range(PIECES):
            held = normed[state_rows(2, chunk), :]
            row = group_of(chunk)
            squares[row : row + 1, :] += lane_sums(held * held)

    def adapt_early():
        make_order(act)
        normed[state_rows(3, 3), :] = shares[pl.ds(24 * 8, 24), :]
        for chunk in range(4):
            normed[state_rows(3, 8 + chunk), :] = shares[pl.ds(24 * 2 * chunk, 24), :]
        for block in range(6):
            values = jnp.concatenate(
                [
                    shares[pl.ds(24 * (2 * chunk + 1), 24), block * 128 : block * 128 + 128]
                    for chunk in range(4)
                ],
                axis=1,
            )
            ordered = reorder(values, act, 0)
            for half in range(2):
                part = 2 * block + half
                lanes = slice(part % 3 * 256, part % 3 * 256 + 256)
                normed[state_rows(3, 4 + part // 3), lanes] = ordered[
                    :, half * 256 : half * 256 + 256
                ]
        for chunk in range(3, PIECES):
            adapt_chunk(chunk)

    def adapt_late():
        for unit in range(3):
            for half in range(2):
                for part in range(3):
                    lanes = slice((unit + 3 * half) * 128, (unit + 3 * half + 1) * 128)
                    source = slice((3 * half + part) * 128, (3 * half + part + 1) * 128)
                    normed[state_rows(3, part), lanes] = shares[pl.ds(24 * (9 + unit), 24), source]
        for chunk in range(3):
            adapt_chunk(chunk)

    def adapt_vectors():
        for block in range(6):
            values = jnp.concatenate(
                [
                    vec_grad[8 + chunk : 9 + chunk, block * 128 : block * 128 + 128]
                    for chunk in range(4)
                ],
                axis=1,
            )
            ordered = reorder(values, act, 0)
            for half in range(2):
                part = 2 * block + half
                lanes = slice(part % 3 * 256, part % 3 * 256 + 256)
                row = 8 + part // 3
                side[0, row : row + 1, lanes] = ordered[:, half * 256 : half * 256 + 256]
        side[0, 0:8, :] = vec_grad[0:8, :]
        first, second, step = adapt(
            vec_moment1[...], vec_moment2[...], side[0, 0:12, :], None
        )
        new_vec_moment1[...] = first
        new_vec_moment2[...] = second
        new_vectors[...] = vectors[...] - 0.3 * step

    def vec_slots(turn):
        return lambda slot: side.at[turn, pl.ds(pl.multiple_of(16 * slot, 8), 16), :]

    def square_slots(turn):
        return lambda slot: squares_got.at[turn, slot]

    exchanges = [
        exchange(group, array, slots, sems)
        for group, array, slots, sems in (
            ("line_group", vec_grad, vec_slots(0), vec_sem.at[0]),
            ("plane_group", vec_grad, vec_slots(1), vec_sem.at[1]),
            ("line_group", squares, square_slots(0), square_sem.at[0]),
            ("plane_group", squares, square_slots(1), square_sem.at[1]),
        )
    ]
    exchanges[0][0]()
    for step in range(5):
        reduce(12 + step)
        if step < 4:
            back_tokens(step)
        reduce_odd(12 + step)
        if step == 0:
            weight_squares()
        if step == 1:
            exchanges[0][1]()
            exchanges[1][0]()
            adapt_early()
    exchanges[1][1]()
    adapt_late()
    exchanges[2][0]()
    adapt_vectors()
    exchanges[2][1]()
    exchanges[3][0]()
    exchanges[3][1]()
    norms = jnp.sqrt(jnp.sum(squares[...], axis=1, keepdims=True))
    ratio = norms[0:4] / (norms[4:8] + 1e-06)
    norm_pairs[:, 0:1] = norms[0:4]
    norm_pairs[:, 1:2] = norms[4:8]
    for group in range(4):
        trust[group] = ratio[group, 0]
    for quarter, array in enumerate((new_moment1, new_moment2, None, update)):
        if array is not None:
            for chunk in range(PIECES):
                result_copy(array, quarter, chunk).wait()
    for slot in range(4):
        grad_copy(slot).wait()


def finish(
    output, input_grad, moment1, moment2, update, vec_moment1, vec_moment2, vectors, pairs, trust,
    weights, *refs
):
    results, (held, step, sem) = refs[:10], refs[10:13]
    stages = refs[13:]
    loads = [
        pltpu.make_async_copy(update, step, sem.at[0, 0]),
        pltpu.make_async_copy(weights, held, sem.at[0, 1]),
    ]
    moves = []
    for source, stage, target in zip((moment1, moment2, output, input_grad), stages, (
        results[2], results[3], results[0], results[1]
    )):
        count = 1 if source.shape[0] < SLOT else source.shape[0] // SLOT
        size = source.shape[0] // count
        for part in range(count):
            rows = pl.ds(part * size, size)
            index = len(moves)
            moves.append(
                (
                    pltpu.make_async_copy(
                        source.at[rows, :], stage.at[rows, :], sem.at[1, index]
                    ),
                    pltpu.make_async_copy(
                        stage.at[rows, :], target.at[rows, :], sem.at[2, index]
                    ),
                )
            )
    for copy in loads:
        copy.start()
    for move in moves:
        move[0].start()
    for source, target in zip((vec_moment1, vec_moment2, vectors, pairs), results[5:9]):
        target[...] = source[...]
    for group in range(4):
        results[9][group] = trust[group]
    for copy in loads:
        copy.wait()
    for group, (low, high) in enumerate(((0, 2304), (2304, 3072), (3072, 6144), (6144, 9216))):
        held[:, low:high] = held[:, low:high] - 0.3 * trust[group] * step[:, low:high]
    last = pltpu.make_async_copy(held, results[4], sem.at[0, 0])
    last.start()
    for load, store in moves:
        load.wait()
        store.start()
    for _, store in moves:
        store.wait()
    last.wait()


def fused(
    tokens,
    cotangent,
    lengths,
    null_flags,
    weights,
    moment1,
    moment2,
    vectors,
    vec_moment1,
    vec_moment2,
):
    rows = tokens.shape[0]
    vmem = pl.BlockSpec(memory_space=pltpu.VMEM)
    smem = pl.BlockSpec(memory_space=pltpu.SMEM)
    hbm = pl.BlockSpec(memory_space=pl.ANY)
    full = lambda *shape: pltpu.VMEM(shape, SUM)
    low = lambda *shape: pltpu.VMEM(shape, LOW)
    copies = lambda *shape: pltpu.SemaphoreType.DMA(shape)
    like = lambda array: jax.ShapeDtypeStruct(array.shape, array.dtype)
    results = pl.pallas_call(
        layer,
        out_shape=[
            like(tokens),
            like(tokens),
            like(weights),
            like(weights),
            like(weights),
            like(vectors),
            like(vectors),
            like(vectors),
            jax.ShapeDtypeStruct((4, 2), SUM),
            jax.ShapeDtypeStruct((4,), SUM),
        ],
        in_specs=[smem, smem] + [hbm] * 5 + [vmem] * 3,
        out_specs=[hbm] * 5 + [vmem] * 4 + [smem],
        scratch_shapes=[
            low(PIECES, 2, 2, 2, 2, 48, TILE),
            full(rows, TILE),
            low(rows, TILE),
            low(3, rows, TILE),
            low(rows, TILE),
            low(rows, TILE),
            low(4, rows, TILE),
            low(4, rows, TILE),
            full(rows, TILE),
            low(rows, TILE),
            full(2, SLOT, TILE),
            full(rows, 128),
            full(3, 4, 4, SLOT),
            full(16, TILE),
            full(2, 2, 2, 2, 48, TILE),
            low(2, 2, 2, 2, 48, HALF),
            low(2, 2, 2, 2, 2, 48, HALF),
            full(2, 2, 2, 2, 48, HALF),
            low(2, 2, 2, 2, 48, HALF),
            low(4, 2, 2, 2, 48, HALF),
            full(2, 2, 2, 48, HALF),
            low(2, 2, 2, 48, HALF),
            low(4, 2, 2, 48, HALF),
            full(2, 48, HALF),
            low(2, 3, 48, HALF),
            low(4, 3, 48, HALF),
            full(SLOT, TILE),
            full(3, 1, TILE),
            full(4, 1, TILE),
            full(8, 128),
            full(2, 8, 8, 128),
            copies(2),
            copies(4),
            copies(2, 4),
            copies(PIECES, 8),
            copies(PIECES, 8),
            copies(6, 2),
            copies(6, 4),
            copies(2, 2, 8),
            copies(4, PIECES),
            copies(2, 2, 8),
            copies(4),
        ],
        compiler_params=pltpu.CompilerParams(
            collective_id=0, has_side_effects=True, vmem_limit_bytes=64 * 2**20
        ),
        cost_estimate=pl.CostEstimate(
            flops=60 * 10**9, bytes_accessed=60 * 10**6, transcendentals=10**7
        ),
    )(
        lengths,
        null_flags,
        tokens,
        cotangent,
        weights,
        moment1,
        moment2,
        vectors,
        vec_moment1,
        vec_moment2,
    )
    return pl.pallas_call(
        finish,
        out_shape=[like(array) for array in results],
        in_specs=[hbm] * 5 + [vmem] * 4 + [smem, hbm],
        out_specs=[hbm] * 5 + [vmem] * 4 + [smem],
        scratch_shapes=[
            full(*weights.shape),
            full(*weights.shape),
            copies(3, 10),
            full(*weights.shape),
            full(*weights.shape),
            full(*tokens.shape),
            full(*tokens.shape),
        ],
        compiler_params=pltpu.CompilerParams(vmem_limit_bytes=63 * 2**20),
        cost_estimate=pl.CostEstimate(
            flops=10**6, bytes_accessed=20 * 10**6, transcendentals=0
        ),
    )(*results, weights)


def solution(mesh):
    split = P(("dp", "shard"), None)
    flat = P(("dp", "shard"))
    in_specs = (split, split, flat, flat, split, split, split, P(), P(), P())
    out_specs = (split,) * 5 + (P(),) * 5
    body = fused if mesh.shape["dp"] == 8 and mesh.shape["shard"] == 4 else plain
    return jax.shard_map(body, mesh=mesh, in_specs=in_specs, out_specs=out_specs, check_vma=False)
```

```python
import jax
import jax.numpy as jnp
from jax import lax
from jax.experimental import pallas as pl
from jax.experimental.pallas import tpu as pltpu
from jax.sharding import PartitionSpec as P

HEADS = 12
SLOT = 288
QLEN = 64
STEP = 5


def norm_forward(values, gain, shift):
    centred = values - jnp.mean(values, axis=-1, keepdims=True)
    inverse = lax.rsqrt(jnp.mean(centred * centred, axis=-1, keepdims=True) + 1e-05)
    normed = centred * inverse
    return (normed * gain + shift, normed, inverse)


def norm_backward(grad_result, normed, inverse, gain):
    scaled = grad_result * gain
    grad_gain = jnp.sum(grad_result * normed, axis=0)
    grad_shift = jnp.sum(grad_result, axis=0)
    centred = scaled - jnp.mean(scaled, axis=-1, keepdims=True)
    grad_input = inverse * (centred - normed * jnp.mean(scaled * normed, axis=-1, keepdims=True))
    return (grad_input, grad_gain, grad_shift)


def gelu_slope(values):
    return (
        0.5 * (1.0 + jax.scipy.special.erf(values * 0.7071067811865476))
        + values * jnp.exp(-0.5 * values * values) * 0.3989422804014327
    )


def plain(
    tokens,
    cotangent,
    lengths,
    null_flags,
    weights,
    moment1,
    moment2,
    vectors,
    vec_moment1,
    vec_moment2,
):
    model_width = tokens.shape[1]
    row_count = tokens.shape[0]
    slot_count = lengths.shape[0]
    head_size = model_width // HEADS
    score_scale = head_size ** (-0.5)
    block_slots = min(2, slot_count)
    block_count = slot_count // block_slots
    valid_len = jnp.where(null_flags == 1, QLEN, lengths)
    key_valid = jnp.arange(SLOT, dtype=jnp.int32)[None, :] < valid_len[:, None]
    key_blocks = key_valid.reshape(block_count, block_slots, SLOT)
    row_weight = key_valid.reshape(row_count, 1).astype(jnp.float32)
    qkv_bias = jnp.concatenate([vectors[0], jnp.zeros((model_width,), jnp.float32), vectors[1]])
    ffn_bias = vectors[8:12].reshape(4 * model_width)
    token_low = tokens.astype(jnp.bfloat16)

    def block_scores(qkv_block, valid_keys):
        scores = (
            jnp.einsum(
                "bqhd,bkhd->bhqk",
                qkv_block[:, :, 0],
                qkv_block[:, :, 1],
                preferred_element_type=jnp.float32,
            )
            * score_scale
        )
        return jnp.where(valid_keys[:, None, None, :], scores, -1000000000.0)

    def attend_block(packed):
        qkv_block, valid_keys = packed
        scores = block_scores(qkv_block, valid_keys)
        row_top = jnp.max(scores, axis=-1, keepdims=True)
        exponent = jnp.exp(scores - row_top)
        row_total = jnp.sum(exponent, axis=-1, keepdims=True)
        softmax_out = (exponent / row_total).astype(jnp.bfloat16)
        context = jnp.einsum(
            "bhqk,bkhd->bqhd", softmax_out, qkv_block[:, :, 2], preferred_element_type=jnp.float32
        )
        return (context.astype(jnp.bfloat16), (row_top + jnp.log(row_total))[..., 0])

    def attend_back(packed):
        qkv_block, valid_keys, log_block, grad_block = packed
        scores = block_scores(qkv_block, valid_keys)
        softmax_out = jnp.exp(scores - log_block[..., None])
        grad_values = jnp.einsum(
            "bhqk,bqhd->bkhd",
            softmax_out.astype(jnp.bfloat16),
            grad_block,
            preferred_element_type=jnp.float32,
        )
        grad_soft = jnp.einsum(
            "bqhd,bkhd->bhqk", grad_block, qkv_block[:, :, 2], preferred_element_type=jnp.float32
        )
        grad_scores = softmax_out * (
            grad_soft - jnp.sum(grad_soft * softmax_out, axis=-1, keepdims=True)
        )
        scores_low = grad_scores.astype(jnp.bfloat16)
        grad_query = (
            jnp.einsum(
                "bhqk,bkhd->bqhd",
                scores_low,
                qkv_block[:, :, 1],
                preferred_element_type=jnp.float32,
            )
            * score_scale
        )
        grad_keys = (
            jnp.einsum(
                "bhqk,bqhd->bkhd",
                scores_low,
                qkv_block[:, :, 0],
                preferred_element_type=jnp.float32,
            )
            * score_scale
        )
        return jnp.stack([grad_query, grad_keys, grad_values], axis=2).astype(jnp.bfloat16)

    gathered = lax.all_gather(weights.astype(jnp.bfloat16), ("dp", "shard"), axis=0, tiled=True)
    first_mats = (
        gathered[:, : 3 * model_width],
        gathered[:, 3 * model_width : 4 * model_width],
        gathered[:, 4 * model_width : 8 * model_width],
        gathered[:, 8 * model_width :].reshape(4 * model_width, model_width),
    )
    w_qkv, w_out, w_in, w_down = first_mats
    qkv_low = (jnp.dot(token_low, w_qkv, preferred_element_type=jnp.float32) + qkv_bias).astype(
        jnp.bfloat16
    )
    qkv_blocks = qkv_low.reshape(block_count, block_slots, SLOT, 3, HEADS, head_size)
    contexts, log_total = lax.map(attend_block, (qkv_blocks, key_blocks))
    context_low = contexts.reshape(row_count, model_width)
    attention = jnp.dot(context_low, w_out, preferred_element_type=jnp.float32) + vectors[2]
    hidden_one, normed_one, inverse_one = norm_forward(tokens + attention, vectors[3], vectors[4])
    hidden_low = hidden_one.astype(jnp.bfloat16)
    pre_act = jnp.dot(hidden_low, w_in, preferred_element_type=jnp.float32) + ffn_bias
    act_low = jax.nn.gelu(pre_act, approximate=False).astype(jnp.bfloat16)
    ffn_out = jnp.dot(act_low, w_down, preferred_element_type=jnp.float32) + vectors[5]
    result, normed_two, inverse_two = norm_forward(hidden_one + ffn_out, vectors[6], vectors[7])
    first_kept = (
        qkv_blocks,
        log_total,
        context_low,
        normed_one,
        inverse_one,
        hidden_low,
        pre_act,
        act_low,
        normed_two,
        inverse_two,
        result,
    )
    output = first_kept[10]
    w_qkv, w_out, w_in, w_down = first_mats
    (
        qkv_blocks,
        log_total,
        context_low,
        normed_one,
        inverse_one,
        hidden_low,
        pre_act,
        act_low,
        normed_two,
        inverse_two,
    ) = first_kept[:10]
    grad_result = cotangent * row_weight
    grad_two, grad_gain_two, grad_shift_two = norm_backward(
        grad_result, normed_two, inverse_two, vectors[6]
    )
    grad_ffn_low = grad_two.astype(jnp.bfloat16)
    grad_bias_down = jnp.sum(grad_ffn_low, axis=0, dtype=jnp.float32)
    grad_down = jnp.einsum("tf,td->fd", act_low, grad_ffn_low, preferred_element_type=jnp.float32)
    grad_act = jnp.einsum("td,fd->tf", grad_ffn_low, w_down, preferred_element_type=jnp.float32)
    grad_pre_low = (grad_act * gelu_slope(pre_act)).astype(jnp.bfloat16)
    grad_bias_in = jnp.sum(grad_pre_low, axis=0, dtype=jnp.float32)
    grad_in = jnp.einsum("td,tf->df", hidden_low, grad_pre_low, preferred_element_type=jnp.float32)
    grad_hidden = grad_two + jnp.einsum(
        "tf,df->td", grad_pre_low, w_in, preferred_element_type=jnp.float32
    )
    grad_residual, grad_gain_one, grad_shift_one = norm_backward(
        grad_hidden, normed_one, inverse_one, vectors[3]
    )
    grad_attn_low = grad_residual.astype(jnp.bfloat16)
    grad_bias_out = jnp.sum(grad_attn_low, axis=0, dtype=jnp.float32)
    grad_out = jnp.einsum(
        "tc,td->cd", context_low, grad_attn_low, preferred_element_type=jnp.float32
    )
    grad_context = jnp.einsum(
        "td,cd->tc", grad_attn_low, w_out, preferred_element_type=jnp.float32
    ).astype(jnp.bfloat16)
    grad_blocks = grad_context.reshape(block_count, block_slots, SLOT, HEADS, head_size)
    grad_qkv_low = lax.map(attend_back, (qkv_blocks, key_blocks, log_total, grad_blocks)).reshape(
        row_count, 3 * model_width
    )
    grad_bias_qkv = jnp.sum(grad_qkv_low, axis=0, dtype=jnp.float32)
    grad_qkv = jnp.einsum("td,te->de", token_low, grad_qkv_low, preferred_element_type=jnp.float32)
    input_grad = grad_residual + jnp.einsum(
        "te,de->td", grad_qkv_low, w_qkv, preferred_element_type=jnp.float32
    )
    vector_grad = jnp.concatenate(
        [
            jnp.stack(
                [
                    grad_bias_qkv[:model_width],
                    grad_bias_qkv[2 * model_width :],
                    grad_bias_out,
                    grad_gain_one,
                    grad_shift_one,
                    grad_bias_down,
                    grad_gain_two,
                    grad_shift_two,
                ]
            ),
            grad_bias_in.reshape(4, model_width),
        ],
        axis=0,
    )
    qkv_shard, out_shard, in_shard, down_shard = (
        lax.psum_scatter(grad_qkv, ("dp", "shard"), scatter_dimension=0, tiled=True),
        lax.psum_scatter(grad_out, ("dp", "shard"), scatter_dimension=0, tiled=True),
        lax.psum_scatter(grad_in, ("dp", "shard"), scatter_dimension=0, tiled=True),
        lax.psum_scatter(
            grad_down.reshape(model_width, 4 * model_width),
            ("dp", "shard"),
            scatter_dimension=0,
            tiled=True,
        ),
    )
    vector_total = lax.psum(vector_grad, ("dp", "shard"))
    grad_shard = jnp.concatenate([qkv_shard, out_shard, in_shard, down_shard], axis=1)
    correction = 1.0 - 0.5**STEP
    new_first = 0.5 * moment1 + 0.5 * grad_shard
    new_second = 0.5 * moment2 + 0.5 * grad_shard * grad_shard
    update = new_first / correction / (jnp.sqrt(new_second / correction) + 1e-06) + 0.01 * weights
    column_edges = (0, 3 * model_width, 4 * model_width, 8 * model_width, 12 * model_width)
    pair_rows = []
    for group_index in range(4):
        weight_part = weights[:, column_edges[group_index] : column_edges[group_index + 1]]
        update_part = update[:, column_edges[group_index] : column_edges[group_index + 1]]
        pair_rows.append(
            jnp.stack([jnp.sum(weight_part * weight_part), jnp.sum(update_part * update_part)])
        )
    pair_squares = jnp.stack(pair_rows)
    pair_total = lax.psum(pair_squares, ("dp", "shard"))
    norm_pairs = jnp.sqrt(pair_total)
    trust_ratio = norm_pairs[:, 0] / (norm_pairs[:, 1] + 1e-06)
    column_trust = jnp.concatenate(
        [
            jnp.ones((column_edges[group_index + 1] - column_edges[group_index],), jnp.float32)
            * trust_ratio[group_index]
            for group_index in range(4)
        ]
    )
    new_weights = weights - 0.3 * column_trust * update
    vec_first = 0.5 * vec_moment1 + 0.5 * vector_total
    vec_second = 0.5 * vec_moment2 + 0.5 * vector_total * vector_total
    new_vectors = vectors - 0.3 * (vec_first / correction) / (
        jnp.sqrt(vec_second / correction) + 1e-06
    )
    return (
        output,
        input_grad,
        new_first,
        new_second,
        new_weights,
        vec_first,
        vec_second,
        new_vectors,
        norm_pairs,
        trust_ratio,
    )


SUM = jnp.float32
LOW = jnp.bfloat16
PIECES = 12
TILE = 768
HALF = 384
NEG = -1e9
CORRECTION = 1.0 - 0.5**STEP


def dot(left, right, left_dim, right_dim):
    return lax.dot_general(
        left, right, (((left_dim,), (right_dim,)), ((), ())), preferred_element_type=SUM
    )


def slot_rows(slot):
    return pl.ds(pl.multiple_of(slot * SLOT, SLOT), SLOT)


def each(count, body, unroll=1):
    def step(index, carry):
        body(index)
        return carry

    lax.fori_loop(0, count, step, 0, unroll=unroll)


def mean_lanes(values):
    return jnp.mean(values, axis=-1, keepdims=True)


def sum_rows(values):
    return jnp.sum(values, axis=0, keepdims=True)


def head_operands(query, key, valid):
    lane = lax.broadcasted_iota(jnp.int32, query.shape, 1)
    row = lax.broadcasted_iota(jnp.int32, query.shape, 0)
    low_head = lane < 64
    bias = jnp.where(row < valid, 0.0, NEG).astype(LOW)
    scaled = query * jnp.asarray(0.125, LOW)
    one, zero = jnp.ones_like(query), jnp.zeros_like(query)
    queries = (
        jnp.where(low_head, scaled, jnp.where(lane == 64, one, zero)),
        jnp.where(low_head, jnp.where(lane == 0, one, zero), scaled),
    )
    keys = (
        jnp.where(low_head, key, jnp.where(lane == 64, bias, zero)),
        jnp.where(low_head, jnp.where(lane == 0, bias, zero), key),
    )
    return queries, keys, low_head


def attend(unit, slot, valid, qkv, context, log_total):
    rows = slot_rows(slot)
    items = []
    for half in range(2):
        query, key, value = (
            qkv[unit, rows, (3 * half + part) * 128 : (3 * half + part + 1) * 128]
            for part in range(3)
        )
        queries, keys, low_head = head_operands(query, key, valid)
        items += [(queries[head], keys[head], value) for head in range(2)]
    scores = [dot(key, query, 1, 1) for query, key, _ in items]
    results = []
    for index, values in enumerate(scores):
        top = jnp.max(values, axis=0, keepdims=True)
        exponent = jnp.exp(values - top)
        total = sum_rows(exponent)
        log_total[unit, slot, index : index + 1, :] = top + jnp.log(total)
        results.append((exponent * (1.0 / total)).astype(LOW))
    results = [dot(probs, item[2], 0, 0) for probs, item in zip(results, items)]
    for half in range(2):
        lanes = pl.ds(pl.multiple_of((unit + 3 * half) * 128, 128), 128)
        joined = jnp.where(low_head, results[2 * half], results[2 * half + 1])
        context[rows, lanes] = joined.astype(LOW)


def attend_back(unit, slot, valid, qkv, grad_context, log_total, vec_grad):
    rows = slot_rows(slot)
    for half in range(2):
        query, key, value = (
            qkv[unit, rows, (3 * half + part) * 128 : (3 * half + part + 1) * 128]
            for part in range(3)
        )
        lanes = pl.ds(pl.multiple_of((unit + 3 * half) * 128, 128), 128)
        grad = grad_context[rows, lanes]
        queries, keys, low_head = head_operands(query, key, valid)
        zero = jnp.zeros_like(grad)
        grads = (jnp.where(low_head, grad, zero), jnp.where(low_head, zero, grad))
        scores = [dot(keys[head], queries[head], 1, 1) for head in range(2)]
        grad_probs = [dot(value, grads[head], 1, 1) for head in range(2)]
        probs, grad_value = [], []
        for head in range(2):
            index = 2 * half + head
            probs.append(jnp.exp(scores[head] - log_total[unit, slot, index : index + 1, :]))
            grad_value.append(dot(probs[head].astype(LOW), grad, 1, 0))
        grad_key, grad_query = [], []
        for head in range(2):
            inner = sum_rows(grad_probs[head] * probs[head])
            low = (probs[head] * (grad_probs[head] - inner)).astype(LOW)
            grad_key.append(dot(low, query, 1, 0))
            grad_query.append(dot(low, key, 0, 0))
        for part, parts, scale in (
            (0, grad_query, 0.125),
            (1, grad_key, 0.125),
            (2, grad_value, 1.0),
        ):
            joined = (jnp.where(low_head, parts[0], parts[1]) * scale).astype(LOW)
            qkv[unit, rows, (3 * half + part) * 128 : (3 * half + part + 1) * 128] = joined
            if part != 1:
                row = part // 2
                vec_grad[row : row + 1, lanes] += sum_rows(joined.astype(SUM))


def make_order(buffer):
    row = lax.broadcasted_iota(jnp.int32, (512, 512), 0)
    column = lax.broadcasted_iota(jnp.int32, (512, 512), 1)
    chosen = column == 4 * (row % 128) + row // 128
    buffer[0, 0:512, 0:512] = jnp.where(chosen, 1.0, 0.0).astype(LOW)


def reorder(values, buffer, side):
    first = values.astype(LOW)
    rest = values - first.astype(SUM)
    second = rest.astype(LOW)
    third = (rest - second.astype(SUM)).astype(LOW)
    order = buffer[0, 0:512, 0:512]
    return (dot(first, order, 1, side) + dot(second, order, 1, side)) + dot(third, order, 1, side)


def place():
    outer, inner = lax.axis_index("dp"), lax.axis_index("shard")
    z, y, x, core = outer // 2, outer % 2, inner // 2, inner % 2
    here = dict(z=z, y=y, x=x, core=core, high=z // 2, low=z % 2)
    here["y1"], here["x1"] = y + core * (1 - 2 * y), x + (1 - core) * (1 - 2 * x)
    here["y2"], here["x2"] = y + (1 - core) * (1 - 2 * y), x + core * (1 - 2 * x)
    device = lambda z, y, x, core: (z * 2 + y, x * 2 + core)
    here["twin"] = device(z, y, x, 1 - core)
    here["near_z"] = device(z + 1 - 2 * (z % 2), y, x, core)
    here["far_z"] = device((z + 2) % 4, y, x, core)
    here["first"] = device(z, here["y1"], here["x1"], core)
    here["second"] = device(z, here["y2"], here["x2"], core)
    here["along_x"] = device(z, y, 1 - x, core)
    here["along_y"] = device(z, 1 - y, x, core)
    here["line_group"] = (
        z * 2 + core, 8, lambda index: device(index // 2, y, x, index % 2)
    )
    here["plane_group"] = (
        y * 2 + x, 4, lambda index: device(z, index // 2, index % 2, core)
    )
    here["mine"] = pl.ds(pl.multiple_of(core * HALF, 128), HALF)
    here["other"] = pl.ds(pl.multiple_of((1 - core) * HALF, 128), HALF)
    return here


def send(source, target, sent, arrived, device):
    return pltpu.make_async_remote_copy(
        src_ref=source,
        dst_ref=target,
        send_sem=sent,
        recv_sem=arrived,
        device_id=device,
        device_id_type=pl.DeviceIdType.MESH,
    )


def inside(index):
    if isinstance(index, int):
        return 0 <= index < PIECES
    return jnp.logical_and(index >= 0, index < PIECES)


def guarded(index, body):
    if isinstance(index, int):
        if inside(index):
            body(index)
    else:
        pl.when(inside(index))(lambda: body(index))


def layer(
    lengths, null_flags, tokens, cotangent, weights, moment1, moment2, vectors, vec_moment1,
    vec_moment2,
    output, input_grad, new_moment1, new_moment2, new_weights, new_vec_moment1, new_vec_moment2,
    new_vectors, norm_pairs, trust,
    walls, normed, token_low, qkv, context, hidden_low, act, slope, grad, grad_low, side, inverse,
    log_total, vec_grad, mat, mat_send, mat_got, pair_keep, pair_send, pair_got,
    line_keep, line_send, line_got, z_keep, z_send, z_got,
    shares, qkv_bias, ffn_bias, squares, squares_got,
    in_sem, out_sem, twin_sem, gather_sent, gather_got, reduce_sent, reduce_got,
    vec_sem, state_sem, square_sem, cot_sem,
):
    here = place()
    z, y, x, core, high, low = (here[name] for name in ("z", "y", "x", "core", "high", "low"))
    y1, x1, y2, x2 = (here[name] for name in ("y1", "x1", "y2", "x2"))
    mine, other = here["mine"], here["other"]

    def valid(slot):
        return jnp.where(null_flags[slot] == 1, QLEN, lengths[slot])

    def state_rows(quarter, chunk):
        return pl.ds(quarter * SLOT + 24 * chunk, 24)

    def state_copy(array, buffer, quarter, chunk):
        return pltpu.make_async_copy(
            array.at[:, pl.ds(TILE * chunk, TILE)],
            buffer.at[state_rows(quarter, chunk), :],
            state_sem.at[quarter, chunk],
        )

    def result_copy(array, quarter, chunk):
        return pltpu.make_async_copy(
            normed.at[state_rows(quarter, chunk), :],
            array.at[:, pl.ds(TILE * chunk, TILE)],
            state_sem.at[quarter, chunk],
        )

    for chunk in range(PIECES):
        state_copy(weights, grad, 0, chunk).start()
    def cot_copy(slot):
        return pltpu.make_async_copy(
            cotangent.at[slot_rows(slot), :], side.at[slot % 2], cot_sem.at[slot]
        )

    def output_copy(slot):
        return pltpu.make_async_copy(
            side.at[slot % 2], output.at[slot_rows(slot), :], out_sem.at[slot]
        )

    def grad_copy(slot):
        rows = slot_rows(slot)
        return pltpu.make_async_copy(grad.at[rows, :], input_grad.at[rows, :], out_sem.at[slot])

    for slot in range(2):
        cot_copy(slot).start()
    tok_copy = pltpu.make_async_copy(tokens, normed, in_sem.at[1])
    tok_copy.start()

    barrier = pltpu.get_barrier_semaphore()
    peers = []
    for group in ("line_group", "plane_group"):
        index, size, device_of = here[group]
        peers += [device_of((index + step) % size) for step in range(1, size)]
    for peer in peers:
        pl.semaphore_signal(barrier, inc=1, device_id=peer, device_id_type=pl.DeviceIdType.MESH)
    pl.semaphore_wait(barrier, len(peers))

    for chunk in range(PIECES):
        state_copy(weights, grad, 0, chunk).wait()
    for unit in range(3):
        for half in range(2):
            for part in range(3):
                lanes = slice((unit + 3 * half) * 128, (unit + 3 * half + 1) * 128)
                place_lanes = slice((3 * half + part) * 128, (3 * half + part + 1) * 128)
                grad[state_rows(1, unit), place_lanes] = grad[state_rows(0, part), lanes]

    def swap(first, count):
        rows = pl.ds(24 * first, 24 * count)
        return send(
            grad.at[pl.ds(SLOT + 24 * first, 24 * count), other],
            shares.at[rows, other],
            twin_sem.at[0, first],
            twin_sem.at[1, first],
            here["twin"],
        )

    swap(0, 3).start()
    def fill(piece):
        rows = pl.ds(pl.multiple_of(24 * piece, 8), 24)
        own, twin = grad[pl.ds(pl.multiple_of(SLOT + 24 * piece, 8), 24), mine], shares[rows, mine]
        upper = jnp.where(core == 0, own, twin)
        lower = jnp.where(core == 0, twin, own)
        joined = jnp.concatenate([upper, lower], axis=0)
        walls[piece, high, low, y, x, :, mine] = joined.astype(LOW)

    swap(0, 3).wait()
    each(3, fill)

    own, line = (high, low, y, x), (slice(None), low, y, x)
    column, next_column = (slice(None), slice(None), y, x), (slice(None), slice(None), y1, x1)
    everything = (slice(None),) * 4
    paths = (
        (
            ((own, "far_z"),),
            ((line, "near_z"),),
            ((column, "first"), (column, "second")),
            ((next_column, "second"),),
            ((everything, "twin"),),
        ),
        (
            ((own, "first"), (own, "far_z")),
            (((high, low, y1, x1), "far_z"), (line, "near_z")),
            (((slice(None), low, y1, x1), "near_z"), (column, "second")),
            ((next_column, "second"),),
            ((everything, "twin"),),
        ),
    )

    def gather_copies(piece, path, stage):
        first = sum(len(copies) for copies in paths[path][:stage])
        copies = []
        for index, (blocks, device) in enumerate(paths[path][stage]):
            part = walls.at[(piece,) + blocks + (slice(None), mine)]
            sent, got = (
                array.at[piece, first + index] for array in (gather_sent, gather_got)
            )
            copies.append(send(part, part, sent, got, here[device]))
        return copies

    def gather(base, index=0):
        def advance(piece, path, stage):
            if stage > 0:
                for copy in gather_copies(piece, path, stage - 1):
                    copy.wait_recv()
            if stage < 5:
                for copy in gather_copies(piece, path, stage):
                    copy.start()
            else:
                for done in range(5):
                    for copy in gather_copies(piece, path, done):
                        copy.wait_send()

        for stage in range(5, -1, -1):
            if (base - 3 * stage) % 2:
                continue

            def step(piece, stage=stage):
                if isinstance(piece, int):
                    advance(piece, min(piece % 3, 1), stage)
                else:
                    turn = lax.rem(piece, 3)
                    pl.when(turn == 0)(lambda: advance(piece, 0, stage))
                    pl.when(turn != 0)(lambda: advance(piece, 1, stage))

            guarded((base - 3 * stage) // 2 + index, step)

    def weight(piece):
        return walls[piece].reshape(TILE, TILE)

    gather(0)
    gather(1)
    make_order(act)
    for block in range(6):
        values = jnp.concatenate(
            [
                grad[state_rows(0, 4 + part // 3), part % 3 * 256 : part % 3 * 256 + 256]
                for part in (2 * block, 2 * block + 1)
            ],
            axis=1,
        )
        ordered = dot(values.astype(LOW), act[0, 0:512, 0:512], 1, 1)
        for chunk in range(4):
            grad[state_rows(1, 4 + chunk), block * 128 : block * 128 + 128] = ordered[
                :, chunk * 128 : chunk * 128 + 128
            ]
    for chunk in (3, 8, 9, 10, 11):
        grad[state_rows(1, chunk), :] = grad[state_rows(0, chunk), :]
    swap(3, 9).start()
    gather(2)
    gather(3)
    vec_grad[...] = jnp.zeros_like(vec_grad)
    for unit in range(3):
        for half in range(2):
            lanes = slice((unit + 3 * half) * 128, (unit + 3 * half + 1) * 128)
            for part, row in ((0, 0), (2, 1)):
                target = slice((3 * half + part) * 128, (3 * half + part + 1) * 128)
                qkv_bias[unit, :, target] = vectors[row : row + 1, lanes]
            target = slice((3 * half + 1) * 128, (3 * half + 2) * 128)
            qkv_bias[unit, :, target] = jnp.zeros((1, 128), SUM)
    for block in range(6):
        values = jnp.concatenate(
            [
                vectors[8 + part // 3 : 9 + part // 3, part % 3 * 256 : part % 3 * 256 + 256]
                for part in (2 * block, 2 * block + 1)
            ],
            axis=1,
        )
        ordered = reorder(values, act, 1)
        for chunk in range(4):
            ffn_bias[chunk, :, block * 128 : block * 128 + 128] = ordered[
                :, chunk * 128 : chunk * 128 + 128
            ]

    gather(4)
    gather(5)
    swap(3, 9).wait()
    each(9, lambda piece: fill(3 + piece))
    gather(6)
    gather(7)
    tok_copy.wait()

    def cast_slot(slot):
        rows = slot_rows(slot)
        token_low[rows, :] = normed[rows, :].astype(LOW)

    each(4, cast_slot, 4)
    for tick in range(8, 16):
        gather(tick)

    def project(unit):
        def project_slot(slot):
            rows = slot_rows(slot)
            values = dot(token_low[rows, :], weight(unit), 1, 0) + qkv_bias[unit]
            qkv[unit, rows, :] = values.astype(LOW)

        each(4, project_slot, 4)

        def attend_slots(pair):
            for slot in range(2):
                index = 2 * pair + slot
                attend(unit, index, valid(index), qkv, context, log_total)
            pl.when(pair == 0)(lambda: gather(16, unit))
            pl.when(pair == 1)(lambda: gather(17, unit))

        each(2, attend_slots)

    each(3, project)

    def attend_out(slot):
        rows = slot_rows(slot)
        values = normed[rows, :] + (dot(context[rows, :], weight(3), 1, 0) + vectors[2:3, :])
        centred = values - mean_lanes(values)
        inv = lax.rsqrt(mean_lanes(centred * centred) + 1e-05)
        unit_values = centred * inv
        normed[rows, :] = unit_values
        inverse[rows, :] = jnp.broadcast_to(inv, (SLOT, 128))
        hidden_low[rows, :] = (unit_values * vectors[3:4, :] + vectors[4:5, :]).astype(LOW)

    gather(22)
    each(4, attend_out, 2)

    def widen(chunk):
        gather(23, chunk)

        def widen_slot(slot):
            rows = slot_rows(slot)
            pre = dot(hidden_low[rows, :], weight(4 + chunk), 1, 0) + ffn_bias[chunk]
            phi = 0.5 + 0.5 * lax.erf(pre * 0.7071067811865476)
            act[chunk, rows, :] = (pre * phi).astype(LOW)
            bell = jnp.exp(pre * pre * -0.5) * 0.3989422804014327
            slope[chunk, rows, :] = (phi + pre * bell).astype(LOW)

        each(2, widen_slot, 2)
        gather(24, chunk)
        each(2, lambda slot: widen_slot(2 + slot), 2)

    each(4, widen, 4)
    def narrow_first(slot):
        rows = slot_rows(slot)
        start = normed[rows, :] * vectors[3:4, :] + (vectors[4:5, :] + vectors[5:6, :])
        grad[rows, :] = start + dot(act[0, rows, :], weight(8), 1, 0)

    gather(31)
    each(4, narrow_first, 4)
    gather(32)

    def narrow(chunk):
        def narrow_slot(slot):
            rows = slot_rows(slot)
            grad[rows, :] += dot(act[1 + chunk, rows, :], weight(9 + chunk), 1, 0)

        each(4, narrow_slot, 4)

    gather(33)
    narrow(0)
    gather(34)
    gather(35)
    narrow(1)
    gather(36)
    gather(37)

    def finish_slot(slot):
        rows = slot_rows(slot)
        if 1 <= slot < 3:
            output_copy(slot - 1).wait()
            cot_copy(slot + 1).start()
        values = grad[rows, :] + dot(act[3, rows, :], weight(11), 1, 0)
        centred = values - mean_lanes(values)
        inv = lax.rsqrt(mean_lanes(centred * centred) + 1e-05)
        unit_values = centred * inv
        kept = lax.broadcasted_iota(jnp.int32, (SLOT, 1), 0) < valid(slot)
        cot_copy(slot).wait()
        grad_out = jnp.where(kept, side[slot % 2], 0.0)
        side[slot % 2] = unit_values * vectors[6:7, :] + vectors[7:8, :]
        output_copy(slot).start()
        vec_grad[6:7, :] += sum_rows(grad_out * unit_values)
        vec_grad[7:8, :] += sum_rows(grad_out)
        scaled = grad_out * vectors[6:7, :]
        result = inv * (
            scaled - mean_lanes(scaled) - unit_values * mean_lanes(scaled * unit_values)
        )
        grad[rows, :] = result
        rounded = result.astype(LOW)
        grad_low[rows, :] = rounded
        vec_grad[5:6, :] += sum_rows(rounded.astype(SUM))

    for slot in range(4):
        finish_slot(slot)
    output_copy(2).wait()
    output_copy(3).wait()

    def turn_of(index, count):
        return index % count if isinstance(index, int) else lax.rem(index, count)

    def reduce_copies(index, stage):
        two, four = turn_of(index, 2), turn_of(index, 4)
        if stage == 3:
            triples = [
                (line_z(step), z_send.at[two, step - 1], z_got.at[four, step - 1])
                for step in range(1, 4)
            ]
        else:
            triples = [
                (
                    None,
                    (here["second"], pair_send.at[two], pair_got.at[four]),
                    (here["first"], line_send.at[two], line_got.at[four]),
                )[stage]
            ]
        return [
            send(
                source,
                target,
                reduce_sent.at[stage + step, two],
                reduce_got.at[stage + step, four],
                device,
            )
            for step, (device, source, target) in enumerate(triples)
        ]

    def half_copy(index, part):
        two = turn_of(index, 2)
        return send(
            mat_send.at[part],
            mat_got.at[two, part],
            reduce_sent.at[6 * part, two],
            reduce_got.at[6 * part, two],
            here["twin"],
        )

    def line_z(step):
        return ((z + step) % 4 * 2 + y, x * 2 + core)

    def begin(index, stage):
        for copy in reduce_copies(index, stage):
            copy.start()

    def end(index, stage):
        for copy in reduce_copies(index, stage):
            copy.wait()

    def folded(rows):
        return jnp.concatenate([rows[..., :HALF], rows[..., HALF:]], axis=-2)

    def reduce(notch):
        def first(index):
            for part in range(2):
                half_copy(index, part).wait()
            turn, got = turn_of(index, 2), turn_of(index, 2)

            ours = pl.ds(pl.multiple_of(24 * core, 8), 24)

            def column(row, col):
                own_rows = folded(mat[:, :, row, col, ours, :])
                return own_rows + mat_got[got, :, :, row, col].astype(SUM)

            pair_send[turn, 0] = column(y2, x2).astype(LOW)
            pair_send[turn, 1] = column(1 - y, 1 - x).astype(LOW)
            begin(index, 1)
            pair_keep[turn, 0] = column(y, x)
            pair_keep[turn, 1] = column(y1, x1)

        def third(index):
            end(index, 2)
            turn, got = turn_of(index, 2), turn_of(index, 4)

            def block(place):
                row, col = place // 2, place % 2
                return line_keep[turn, row, col] + line_got[got, row, col].astype(SUM)

            for step in range(1, 4):
                z_send[turn, step - 1] = block((z + step) % 4).astype(LOW)
            begin(index, 3)
            z_keep[turn] = block(z)

        guarded(notch - 4, third)
        guarded(notch - 1, first)

    def reduce_odd(notch):
        def second(index):
            end(index, 1)
            turn, got = turn_of(index, 2), turn_of(index, 4)
            line_send[turn] = (pair_keep[turn, 1] + pair_got[got, 1].astype(SUM)).astype(LOW)
            begin(index, 2)
            line_keep[turn] = pair_keep[turn, 0] + pair_got[got, 0].astype(SUM)

        def fourth(index):
            end(index, 3)
            turn, got = turn_of(index, 2), turn_of(index, 4)
            total = z_keep[turn]
            for step in range(3):
                total += z_got[got, step].astype(SUM)
            rows = pl.ds(pl.multiple_of(24 * index, 8), 24)
            shares[rows, :HALF] = total[:24]
            shares[rows, HALF:] = total[24:]

        guarded(notch - 2, second)
        guarded(notch - 5, fourth)

    def emit(index, left, right, unroll=2):
        reduce(index)
        shape = mat.shape[1:]


        theirs = pl.ds(pl.multiple_of(24 * (1 - core), 8), 24)

        def multiply(part):
            lanes = pl.ds(pl.multiple_of(part * HALF, 128), HALF)
            mat[part] = dot(left[:, lanes], right[...], 0, 0).reshape(shape)
            mat_send[part] = folded(mat[part, :, :, :, theirs, :]).astype(LOW)
            half_copy(index, part).start()

        each(2, multiply, unroll)
        reduce_odd(index)

    def back_chunk(chunk):
        emit(2 * chunk, act.at[chunk], grad_low)

        def back_slot(slot):
            rows = slot_rows(slot)
            values = dot(grad_low[rows, :], weight(8 + chunk), 1, 1)
            rounded = (values * slope[chunk, rows, :].astype(SUM)).astype(LOW)
            slope[chunk, rows, :] = rounded
            row = pl.ds(8 + chunk, 1)
            vec_grad[row, :] += sum_rows(rounded.astype(SUM))

        each(4, back_slot, 4)
        emit(2 * chunk + 1, hidden_low, slope.at[chunk])

        def back_hidden(slot):
            rows = slot_rows(slot)
            grad[rows, :] += dot(slope[chunk, rows, :], weight(4 + chunk), 1, 1)

        each(4, back_hidden, 4)

    each(4, back_chunk, 4)

    def back_norm(slot):
        rows = slot_rows(slot)
        total = grad[rows, :]
        unit_values = normed[rows, :]
        vec_grad[3:4, :] += sum_rows(total * unit_values)
        vec_grad[4:5, :] += sum_rows(total)
        scaled = total * vectors[3:4, :]
        inv = inverse[rows, 0:1]
        result = inv * (
            scaled - mean_lanes(scaled) - unit_values * mean_lanes(scaled * unit_values)
        )
        grad[rows, :] = result
        rounded = result.astype(LOW)
        grad_low[rows, :] = rounded
        vec_grad[2:3, :] += sum_rows(rounded.astype(SUM))

    each(4, back_norm, 2)
    emit(8, context, grad_low)
    states = (moment1, moment2, weights)
    for quarter, array in enumerate(states):
        for chunk in range(PIECES):
            state_copy(array, normed, quarter, chunk).start()

    def back_context(slot):
        rows = slot_rows(slot)
        context[rows, :] = dot(grad_low[rows, :], weight(3), 1, 1).astype(LOW)

    each(4, back_context, 4)

    def back_unit(unit):
        each(
            4,
            lambda slot: attend_back(unit, slot, valid(slot), qkv, context, log_total, vec_grad),
        )
        emit(9 + unit, token_low, qkv.at[unit], 1)

    each(3, back_unit)

    def exchange(group, source, slots, sems):
        index, size, device_of = here[group]

        def copies(outgoing):
            found = []
            for step in range(1, size):
                other_index = (index + (step if outgoing else size - step)) % size
                found.append(
                    send(
                        source,
                        slots(index if outgoing else other_index),
                        sems.at[0, step],
                        sems.at[1, index if outgoing else other_index],
                        device_of(other_index),
                    )
                )
            return found

        def start():
            for copy in copies(True):
                copy.start()
            slots(index)[...] = source[...]

        def wait():
            for copy in copies(True):
                copy.wait_send()
            for copy in copies(False):
                copy.wait_recv()
            total = slots(0)[...]
            for slot in range(1, size):
                total += slots(slot)[...]
            source[...] = total

        return start, wait

    def back_tokens(slot):
        rows = slot_rows(slot)
        total = grad[rows, :]
        for unit in range(3):
            total += dot(qkv[unit, rows, :], weight(unit), 1, 1)
        grad[rows, :] = total
        grad_copy(slot).start()

    def adapt(first, second, value, held):
        new_first = 0.5 * first + 0.5 * value
        new_second = 0.5 * second + 0.5 * value * value
        step = (new_first / CORRECTION) / (jnp.sqrt(new_second / CORRECTION) + 1e-06)
        if held is not None:
            step = step + 0.01 * held
        return new_first, new_second, step

    def lane_sums(values):
        total = sum_rows(values)
        return sum(total[:, 128 * index : 128 * index + 128] for index in range(6))

    def group_of(chunk):
        return 0 if chunk < 3 else 1 if chunk == 3 else 2 if chunk < 8 else 3

    def adapt_chunk(chunk):
        row = 4 + group_of(chunk)
        first, second, step = adapt(
            *(normed[state_rows(quarter, chunk), :] for quarter in (0, 1, 3, 2))
        )
        normed[state_rows(0, chunk), :] = first
        normed[state_rows(1, chunk), :] = second
        normed[state_rows(3, chunk), :] = step
        result_copy(new_moment1, 0, chunk).start()
        result_copy(new_moment2, 1, chunk).start()
        squares[row : row + 1, :] += lane_sums(step * step)

    def weight_squares():
        squares[...] = jnp.zeros_like(squares)
        for quarter, array in enumerate(states):
            for chunk in range(PIECES):
                state_copy(array, normed, quarter, chunk).wait()
        for chunk in range(PIECES):
            held = normed[state_rows(2, chunk), :]
            row = group_of(chunk)
            squares[row : row + 1, :] += lane_sums(held * held)

    def adapt_early():
        make_order(act)
        normed[state_rows(3, 3), :] = shares[pl.ds(24 * 8, 24), :]
        for chunk in range(4):
            normed[state_rows(3, 8 + chunk), :] = shares[pl.ds(24 * 2 * chunk, 24), :]
        for block in range(6):
            values = jnp.concatenate(
                [
                    shares[pl.ds(24 * (2 * chunk + 1), 24), block * 128 : block * 128 + 128]
                    for chunk in range(4)
                ],
                axis=1,
            )
            ordered = reorder(values, act, 0)
            for half in range(2):
                part = 2 * block + half
                lanes = slice(part % 3 * 256, part % 3 * 256 + 256)
                normed[state_rows(3, 4 + part // 3), lanes] = ordered[
                    :, half * 256 : half * 256 + 256
                ]
        for chunk in range(3, PIECES):
            adapt_chunk(chunk)

    def adapt_late():
        for unit in range(3):
            for half in range(2):
                for part in range(3):
                    lanes = slice((unit + 3 * half) * 128, (unit + 3 * half + 1) * 128)
                    source = slice((3 * half + part) * 128, (3 * half + part + 1) * 128)
                    normed[state_rows(3, part), lanes] = shares[pl.ds(24 * (9 + unit), 24), source]
        for chunk in range(3):
            adapt_chunk(chunk)

    def adapt_vectors():
        for block in range(6):
            values = jnp.concatenate(
                [
                    vec_grad[8 + chunk : 9 + chunk, block * 128 : block * 128 + 128]
                    for chunk in range(4)
                ],
                axis=1,
            )
            ordered = reorder(values, act, 0)
            for half in range(2):
                part = 2 * block + half
                lanes = slice(part % 3 * 256, part % 3 * 256 + 256)
                row = 8 + part // 3
                side[0, row : row + 1, lanes] = ordered[:, half * 256 : half * 256 + 256]
        side[0, 0:8, :] = vec_grad[0:8, :]
        first, second, step = adapt(
            vec_moment1[...], vec_moment2[...], side[0, 0:12, :], None
        )
        new_vec_moment1[...] = first
        new_vec_moment2[...] = second
        new_vectors[...] = vectors[...] - 0.3 * step

    def vec_slots(turn):
        return lambda slot: side.at[turn, pl.ds(pl.multiple_of(16 * slot, 8), 16), :]

    def square_slots(turn):
        return lambda slot: squares_got.at[turn, slot]

    exchanges = [
        exchange(group, array, slots, sems)
        for group, array, slots, sems in (
            ("line_group", vec_grad, vec_slots(0), vec_sem.at[0]),
            ("plane_group", vec_grad, vec_slots(1), vec_sem.at[1]),
            ("line_group", squares, square_slots(0), square_sem.at[0]),
            ("plane_group", squares, square_slots(1), square_sem.at[1]),
        )
    ]
    exchanges[0][0]()
    for step in range(5):
        reduce(12 + step)
        if step < 4:
            back_tokens(step)
        if step == 0:
            weight_squares()
        if step == 1:
            exchanges[0][1]()
            exchanges[1][0]()
        if step == 3:
            adapt_early()
        reduce_odd(12 + step)
    exchanges[1][1]()
    adapt_late()
    exchanges[2][0]()
    adapt_vectors()
    exchanges[2][1]()
    exchanges[3][0]()
    exchanges[3][1]()
    norms = jnp.sqrt(jnp.sum(squares[...], axis=1, keepdims=True))
    ratio = norms[0:4] / (norms[4:8] + 1e-06)
    norm_pairs[:, 0:1] = norms[0:4]
    norm_pairs[:, 1:2] = norms[4:8]
    for group in range(4):
        trust[group] = ratio[group, 0]
    for chunk in range(PIECES):
        group = group_of(chunk)
        rows = state_rows(2, chunk)
        factor = 0.3 * ratio[group : group + 1, :]
        normed[rows, :] = normed[rows, :] - factor * normed[state_rows(3, chunk), :]
        result_copy(new_weights, 2, chunk).start()
    for quarter, array in enumerate((new_moment1, new_moment2, new_weights)):
        for chunk in range(PIECES):
            result_copy(array, quarter, chunk).wait()
    for slot in range(4):
        grad_copy(slot).wait()


def fused(
    tokens,
    cotangent,
    lengths,
    null_flags,
    weights,
    moment1,
    moment2,
    vectors,
    vec_moment1,
    vec_moment2,
):
    rows = tokens.shape[0]
    vmem = pl.BlockSpec(memory_space=pltpu.VMEM)
    smem = pl.BlockSpec(memory_space=pltpu.SMEM)
    hbm = pl.BlockSpec(memory_space=pl.ANY)
    full = lambda *shape: pltpu.VMEM(shape, SUM)
    low = lambda *shape: pltpu.VMEM(shape, LOW)
    copies = lambda *shape: pltpu.SemaphoreType.DMA(shape)
    like = lambda array: jax.ShapeDtypeStruct(array.shape, array.dtype)
    return pl.pallas_call(
        layer,
        out_shape=[
            like(tokens),
            like(tokens),
            like(weights),
            like(weights),
            like(weights),
            like(vectors),
            like(vectors),
            like(vectors),
            jax.ShapeDtypeStruct((4, 2), SUM),
            jax.ShapeDtypeStruct((4,), SUM),
        ],
        in_specs=[smem, smem] + [hbm] * 5 + [vmem] * 3,
        out_specs=[hbm] * 5 + [vmem] * 4 + [smem],
        scratch_shapes=[
            low(PIECES, 2, 2, 2, 2, 48, TILE),
            full(rows, TILE),
            low(rows, TILE),
            low(3, rows, TILE),
            low(rows, TILE),
            low(rows, TILE),
            low(4, rows, TILE),
            low(4, rows, TILE),
            full(rows, TILE),
            low(rows, TILE),
            full(2, SLOT, TILE),
            full(rows, 128),
            full(3, 4, 4, SLOT),
            full(16, TILE),
            full(2, 2, 2, 2, 48, TILE),
            low(2, 2, 2, 2, 48, HALF),
            low(2, 2, 2, 2, 2, 48, HALF),
            full(2, 2, 2, 2, 48, HALF),
            low(2, 2, 2, 2, 48, HALF),
            low(4, 2, 2, 2, 48, HALF),
            full(2, 2, 2, 48, HALF),
            low(2, 2, 2, 48, HALF),
            low(4, 2, 2, 48, HALF),
            full(2, 48, HALF),
            low(2, 3, 48, HALF),
            low(4, 3, 48, HALF),
            full(SLOT, TILE),
            full(3, 1, TILE),
            full(4, 1, TILE),
            full(8, 128),
            full(2, 8, 8, 128),
            copies(2),
            copies(4),
            copies(2, 4),
            copies(PIECES, 8),
            copies(PIECES, 8),
            copies(7, 2),
            copies(7, 4),
            copies(2, 2, 8),
            copies(4, PIECES),
            copies(2, 2, 8),
            copies(4),
        ],
        compiler_params=pltpu.CompilerParams(
            collective_id=0, has_side_effects=True, vmem_limit_bytes=64 * 2**20
        ),
        cost_estimate=pl.CostEstimate(
            flops=60 * 10**9, bytes_accessed=60 * 10**6, transcendentals=10**7
        ),
    )(
        lengths,
        null_flags,
        tokens,
        cotangent,
        weights,
        moment1,
        moment2,
        vectors,
        vec_moment1,
        vec_moment2,
    )


def solution(mesh):
    split = P(("dp", "shard"), None)
    flat = P(("dp", "shard"))
    in_specs = (split, split, flat, flat, split, split, split, P(), P(), P())
    out_specs = (split,) * 5 + (P(),) * 5
    body = fused if mesh.shape["dp"] == 8 and mesh.shape["shard"] == 4 else plain
    return jax.shard_map(body, mesh=mesh, in_specs=in_specs, out_specs=out_specs, check_vma=False)
```

```python
import jax
import jax.numpy as jnp
from jax import lax
from jax.experimental import pallas as pl
from jax.experimental.pallas import tpu as pltpu
from jax.sharding import PartitionSpec as P

HEADS = 12
SLOT = 288
QLEN = 64
STEP = 5


def norm_forward(values, gain, shift):
    centred = values - jnp.mean(values, axis=-1, keepdims=True)
    inverse = lax.rsqrt(jnp.mean(centred * centred, axis=-1, keepdims=True) + 1e-05)
    normed = centred * inverse
    return (normed * gain + shift, normed, inverse)


def norm_backward(grad_result, normed, inverse, gain):
    scaled = grad_result * gain
    grad_gain = jnp.sum(grad_result * normed, axis=0)
    grad_shift = jnp.sum(grad_result, axis=0)
    centred = scaled - jnp.mean(scaled, axis=-1, keepdims=True)
    grad_input = inverse * (centred - normed * jnp.mean(scaled * normed, axis=-1, keepdims=True))
    return (grad_input, grad_gain, grad_shift)


def gelu_slope(values):
    return (
        0.5 * (1.0 + jax.scipy.special.erf(values * 0.7071067811865476))
        + values * jnp.exp(-0.5 * values * values) * 0.3989422804014327
    )


def plain(
    tokens,
    cotangent,
    lengths,
    null_flags,
    weights,
    moment1,
    moment2,
    vectors,
    vec_moment1,
    vec_moment2,
):
    model_width = tokens.shape[1]
    row_count = tokens.shape[0]
    slot_count = lengths.shape[0]
    head_size = model_width // HEADS
    score_scale = head_size ** (-0.5)
    block_slots = min(2, slot_count)
    block_count = slot_count // block_slots
    valid_len = jnp.where(null_flags == 1, QLEN, lengths)
    key_valid = jnp.arange(SLOT, dtype=jnp.int32)[None, :] < valid_len[:, None]
    key_blocks = key_valid.reshape(block_count, block_slots, SLOT)
    row_weight = key_valid.reshape(row_count, 1).astype(jnp.float32)
    qkv_bias = jnp.concatenate([vectors[0], jnp.zeros((model_width,), jnp.float32), vectors[1]])
    ffn_bias = vectors[8:12].reshape(4 * model_width)
    token_low = tokens.astype(jnp.bfloat16)

    def block_scores(qkv_block, valid_keys):
        scores = (
            jnp.einsum(
                "bqhd,bkhd->bhqk",
                qkv_block[:, :, 0],
                qkv_block[:, :, 1],
                preferred_element_type=jnp.float32,
            )
            * score_scale
        )
        return jnp.where(valid_keys[:, None, None, :], scores, -1000000000.0)

    def attend_block(packed):
        qkv_block, valid_keys = packed
        scores = block_scores(qkv_block, valid_keys)
        row_top = jnp.max(scores, axis=-1, keepdims=True)
        exponent = jnp.exp(scores - row_top)
        row_total = jnp.sum(exponent, axis=-1, keepdims=True)
        softmax_out = (exponent / row_total).astype(jnp.bfloat16)
        context = jnp.einsum(
            "bhqk,bkhd->bqhd", softmax_out, qkv_block[:, :, 2], preferred_element_type=jnp.float32
        )
        return (context.astype(jnp.bfloat16), (row_top + jnp.log(row_total))[..., 0])

    def attend_back(packed):
        qkv_block, valid_keys, log_block, grad_block = packed
        scores = block_scores(qkv_block, valid_keys)
        softmax_out = jnp.exp(scores - log_block[..., None])
        grad_values = jnp.einsum(
            "bhqk,bqhd->bkhd",
            softmax_out.astype(jnp.bfloat16),
            grad_block,
            preferred_element_type=jnp.float32,
        )
        grad_soft = jnp.einsum(
            "bqhd,bkhd->bhqk", grad_block, qkv_block[:, :, 2], preferred_element_type=jnp.float32
        )
        grad_scores = softmax_out * (
            grad_soft - jnp.sum(grad_soft * softmax_out, axis=-1, keepdims=True)
        )
        scores_low = grad_scores.astype(jnp.bfloat16)
        grad_query = (
            jnp.einsum(
                "bhqk,bkhd->bqhd",
                scores_low,
                qkv_block[:, :, 1],
                preferred_element_type=jnp.float32,
            )
            * score_scale
        )
        grad_keys = (
            jnp.einsum(
                "bhqk,bqhd->bkhd",
                scores_low,
                qkv_block[:, :, 0],
                preferred_element_type=jnp.float32,
            )
            * score_scale
        )
        return jnp.stack([grad_query, grad_keys, grad_values], axis=2).astype(jnp.bfloat16)

    gathered = lax.all_gather(weights.astype(jnp.bfloat16), ("dp", "shard"), axis=0, tiled=True)
    first_mats = (
        gathered[:, : 3 * model_width],
        gathered[:, 3 * model_width : 4 * model_width],
        gathered[:, 4 * model_width : 8 * model_width],
        gathered[:, 8 * model_width :].reshape(4 * model_width, model_width),
    )
    w_qkv, w_out, w_in, w_down = first_mats
    qkv_low = (jnp.dot(token_low, w_qkv, preferred_element_type=jnp.float32) + qkv_bias).astype(
        jnp.bfloat16
    )
    qkv_blocks = qkv_low.reshape(block_count, block_slots, SLOT, 3, HEADS, head_size)
    contexts, log_total = lax.map(attend_block, (qkv_blocks, key_blocks))
    context_low = contexts.reshape(row_count, model_width)
    attention = jnp.dot(context_low, w_out, preferred_element_type=jnp.float32) + vectors[2]
    hidden_one, normed_one, inverse_one = norm_forward(tokens + attention, vectors[3], vectors[4])
    hidden_low = hidden_one.astype(jnp.bfloat16)
    pre_act = jnp.dot(hidden_low, w_in, preferred_element_type=jnp.float32) + ffn_bias
    act_low = jax.nn.gelu(pre_act, approximate=False).astype(jnp.bfloat16)
    ffn_out = jnp.dot(act_low, w_down, preferred_element_type=jnp.float32) + vectors[5]
    result, normed_two, inverse_two = norm_forward(hidden_one + ffn_out, vectors[6], vectors[7])
    first_kept = (
        qkv_blocks,
        log_total,
        context_low,
        normed_one,
        inverse_one,
        hidden_low,
        pre_act,
        act_low,
        normed_two,
        inverse_two,
        result,
    )
    output = first_kept[10]
    w_qkv, w_out, w_in, w_down = first_mats
    (
        qkv_blocks,
        log_total,
        context_low,
        normed_one,
        inverse_one,
        hidden_low,
        pre_act,
        act_low,
        normed_two,
        inverse_two,
    ) = first_kept[:10]
    grad_result = cotangent * row_weight
    grad_two, grad_gain_two, grad_shift_two = norm_backward(
        grad_result, normed_two, inverse_two, vectors[6]
    )
    grad_ffn_low = grad_two.astype(jnp.bfloat16)
    grad_bias_down = jnp.sum(grad_ffn_low, axis=0, dtype=jnp.float32)
    grad_down = jnp.einsum("tf,td->fd", act_low, grad_ffn_low, preferred_element_type=jnp.float32)
    grad_act = jnp.einsum("td,fd->tf", grad_ffn_low, w_down, preferred_element_type=jnp.float32)
    grad_pre_low = (grad_act * gelu_slope(pre_act)).astype(jnp.bfloat16)
    grad_bias_in = jnp.sum(grad_pre_low, axis=0, dtype=jnp.float32)
    grad_in = jnp.einsum("td,tf->df", hidden_low, grad_pre_low, preferred_element_type=jnp.float32)
    grad_hidden = grad_two + jnp.einsum(
        "tf,df->td", grad_pre_low, w_in, preferred_element_type=jnp.float32
    )
    grad_residual, grad_gain_one, grad_shift_one = norm_backward(
        grad_hidden, normed_one, inverse_one, vectors[3]
    )
    grad_attn_low = grad_residual.astype(jnp.bfloat16)
    grad_bias_out = jnp.sum(grad_attn_low, axis=0, dtype=jnp.float32)
    grad_out = jnp.einsum(
        "tc,td->cd", context_low, grad_attn_low, preferred_element_type=jnp.float32
    )
    grad_context = jnp.einsum(
        "td,cd->tc", grad_attn_low, w_out, preferred_element_type=jnp.float32
    ).astype(jnp.bfloat16)
    grad_blocks = grad_context.reshape(block_count, block_slots, SLOT, HEADS, head_size)
    grad_qkv_low = lax.map(attend_back, (qkv_blocks, key_blocks, log_total, grad_blocks)).reshape(
        row_count, 3 * model_width
    )
    grad_bias_qkv = jnp.sum(grad_qkv_low, axis=0, dtype=jnp.float32)
    grad_qkv = jnp.einsum("td,te->de", token_low, grad_qkv_low, preferred_element_type=jnp.float32)
    input_grad = grad_residual + jnp.einsum(
        "te,de->td", grad_qkv_low, w_qkv, preferred_element_type=jnp.float32
    )
    vector_grad = jnp.concatenate(
        [
            jnp.stack(
                [
                    grad_bias_qkv[:model_width],
                    grad_bias_qkv[2 * model_width :],
                    grad_bias_out,
                    grad_gain_one,
                    grad_shift_one,
                    grad_bias_down,
                    grad_gain_two,
                    grad_shift_two,
                ]
            ),
            grad_bias_in.reshape(4, model_width),
        ],
        axis=0,
    )
    qkv_shard, out_shard, in_shard, down_shard = (
        lax.psum_scatter(grad_qkv, ("dp", "shard"), scatter_dimension=0, tiled=True),
        lax.psum_scatter(grad_out, ("dp", "shard"), scatter_dimension=0, tiled=True),
        lax.psum_scatter(grad_in, ("dp", "shard"), scatter_dimension=0, tiled=True),
        lax.psum_scatter(
            grad_down.reshape(model_width, 4 * model_width),
            ("dp", "shard"),
            scatter_dimension=0,
            tiled=True,
        ),
    )
    vector_total = lax.psum(vector_grad, ("dp", "shard"))
    grad_shard = jnp.concatenate([qkv_shard, out_shard, in_shard, down_shard], axis=1)
    correction = 1.0 - 0.5**STEP
    new_first = 0.5 * moment1 + 0.5 * grad_shard
    new_second = 0.5 * moment2 + 0.5 * grad_shard * grad_shard
    update = new_first / correction / (jnp.sqrt(new_second / correction) + 1e-06) + 0.01 * weights
    column_edges = (0, 3 * model_width, 4 * model_width, 8 * model_width, 12 * model_width)
    pair_rows = []
    for group_index in range(4):
        weight_part = weights[:, column_edges[group_index] : column_edges[group_index + 1]]
        update_part = update[:, column_edges[group_index] : column_edges[group_index + 1]]
        pair_rows.append(
            jnp.stack([jnp.sum(weight_part * weight_part), jnp.sum(update_part * update_part)])
        )
    pair_squares = jnp.stack(pair_rows)
    pair_total = lax.psum(pair_squares, ("dp", "shard"))
    norm_pairs = jnp.sqrt(pair_total)
    trust_ratio = norm_pairs[:, 0] / (norm_pairs[:, 1] + 1e-06)
    column_trust = jnp.concatenate(
        [
            jnp.ones((column_edges[group_index + 1] - column_edges[group_index],), jnp.float32)
            * trust_ratio[group_index]
            for group_index in range(4)
        ]
    )
    new_weights = weights - 0.3 * column_trust * update
    vec_first = 0.5 * vec_moment1 + 0.5 * vector_total
    vec_second = 0.5 * vec_moment2 + 0.5 * vector_total * vector_total
    new_vectors = vectors - 0.3 * (vec_first / correction) / (
        jnp.sqrt(vec_second / correction) + 1e-06
    )
    return (
        output,
        input_grad,
        new_first,
        new_second,
        new_weights,
        vec_first,
        vec_second,
        new_vectors,
        norm_pairs,
        trust_ratio,
    )


SUM = jnp.float32
LOW = jnp.bfloat16
PIECES = 12
TILE = 768
HALF = 384
NEG = -1e9
CORRECTION = 1.0 - 0.5**STEP


def dot(left, right, left_dim, right_dim):
    return lax.dot_general(
        left, right, (((left_dim,), (right_dim,)), ((), ())), preferred_element_type=SUM
    )


def slot_rows(slot):
    return pl.ds(pl.multiple_of(slot * SLOT, SLOT), SLOT)


def each(count, body, unroll=1):
    def step(index, carry):
        body(index)
        return carry

    lax.fori_loop(0, count, step, 0, unroll=unroll)


def mean_lanes(values):
    return jnp.mean(values, axis=-1, keepdims=True)


def sum_rows(values):
    return jnp.sum(values, axis=0, keepdims=True)


def head_operands(query, key, valid):
    lane = lax.broadcasted_iota(jnp.int32, query.shape, 1)
    row = lax.broadcasted_iota(jnp.int32, query.shape, 0)
    low_head = lane < 64
    bias = jnp.where(row < valid, 0.0, NEG).astype(LOW)
    scaled = query * jnp.asarray(0.125, LOW)
    one, zero = jnp.ones_like(query), jnp.zeros_like(query)
    queries = (
        jnp.where(low_head, scaled, jnp.where(lane == 64, one, zero)),
        jnp.where(low_head, jnp.where(lane == 0, one, zero), scaled),
    )
    keys = (
        jnp.where(low_head, key, jnp.where(lane == 64, bias, zero)),
        jnp.where(low_head, jnp.where(lane == 0, bias, zero), key),
    )
    return queries, keys, low_head


def attend(unit, slot, valid, qkv, context, log_total):
    rows = slot_rows(slot)
    items = []
    for half in range(2):
        query, key, value = (
            qkv[unit, rows, (3 * half + part) * 128 : (3 * half + part + 1) * 128]
            for part in range(3)
        )
        queries, keys, low_head = head_operands(query, key, valid)
        items += [(queries[head], keys[head], value) for head in range(2)]
    scores = [dot(key, query, 1, 1) for query, key, _ in items]
    results = []
    for index, values in enumerate(scores):
        top = jnp.max(values, axis=0, keepdims=True)
        exponent = jnp.exp(values - top)
        total = sum_rows(exponent)
        log_total[unit, slot, index : index + 1, :] = top + jnp.log(total)
        results.append((exponent * (1.0 / total)).astype(LOW))
    results = [dot(probs, item[2], 0, 0) for probs, item in zip(results, items)]
    for half in range(2):
        lanes = pl.ds(pl.multiple_of((unit + 3 * half) * 128, 128), 128)
        joined = jnp.where(low_head, results[2 * half], results[2 * half + 1])
        context[rows, lanes] = joined.astype(LOW)


def attend_back(unit, slot, valid, qkv, grad_context, log_total, vec_grad):
    rows = slot_rows(slot)
    for half in range(2):
        query, key, value = (
            qkv[unit, rows, (3 * half + part) * 128 : (3 * half + part + 1) * 128]
            for part in range(3)
        )
        lanes = pl.ds(pl.multiple_of((unit + 3 * half) * 128, 128), 128)
        grad = grad_context[rows, lanes]
        queries, keys, low_head = head_operands(query, key, valid)
        zero = jnp.zeros_like(grad)
        grads = (jnp.where(low_head, grad, zero), jnp.where(low_head, zero, grad))
        scores = [dot(keys[head], queries[head], 1, 1) for head in range(2)]
        grad_probs = [dot(value, grads[head], 1, 1) for head in range(2)]
        probs, grad_value = [], []
        for head in range(2):
            index = 2 * half + head
            probs.append(jnp.exp(scores[head] - log_total[unit, slot, index : index + 1, :]))
            grad_value.append(dot(probs[head].astype(LOW), grad, 1, 0))
        grad_key, grad_query = [], []
        for head in range(2):
            inner = sum_rows(grad_probs[head] * probs[head])
            low = (probs[head] * (grad_probs[head] - inner)).astype(LOW)
            grad_key.append(dot(low, query, 1, 0))
            grad_query.append(dot(low, key, 0, 0))
        for part, parts, scale in (
            (0, grad_query, 0.125),
            (1, grad_key, 0.125),
            (2, grad_value, 1.0),
        ):
            joined = (jnp.where(low_head, parts[0], parts[1]) * scale).astype(LOW)
            qkv[unit, rows, (3 * half + part) * 128 : (3 * half + part + 1) * 128] = joined
            if part != 1:
                row = part // 2
                vec_grad[row : row + 1, lanes] += sum_rows(joined.astype(SUM))


def adapt(first, second, value):
    new_first = 0.5 * first + 0.5 * value
    new_second = 0.5 * second + 0.5 * value * value
    step = (new_first / CORRECTION) / (jnp.sqrt(new_second / CORRECTION) + 1e-06)
    return new_first, new_second, step


def make_order(buffer):
    row = lax.broadcasted_iota(jnp.int32, (512, 512), 0)
    column = lax.broadcasted_iota(jnp.int32, (512, 512), 1)
    chosen = column == 4 * (row % 128) + row // 128
    buffer[0, 0:512, 0:512] = jnp.where(chosen, 1.0, 0.0).astype(LOW)


def reorder(values, buffer, side):
    first = values.astype(LOW)
    rest = values - first.astype(SUM)
    second = rest.astype(LOW)
    third = (rest - second.astype(SUM)).astype(LOW)
    order = buffer[0, 0:512, 0:512]
    return (dot(first, order, 1, side) + dot(second, order, 1, side)) + dot(third, order, 1, side)


def place():
    outer, inner = lax.axis_index("dp"), lax.axis_index("shard")
    z, y, x, core = outer // 2, outer % 2, inner // 2, inner % 2
    here = dict(z=z, y=y, x=x, core=core, high=z // 2, low=z % 2)
    here["y1"], here["x1"] = y + core * (1 - 2 * y), x + (1 - core) * (1 - 2 * x)
    here["y2"], here["x2"] = y + (1 - core) * (1 - 2 * y), x + core * (1 - 2 * x)
    device = lambda z, y, x, core: (z * 2 + y, x * 2 + core)
    here["twin"] = device(z, y, x, 1 - core)
    here["near_z"] = device(z + 1 - 2 * (z % 2), y, x, core)
    here["far_z"] = device((z + 2) % 4, y, x, core)
    here["first"] = device(z, here["y1"], here["x1"], core)
    here["second"] = device(z, here["y2"], here["x2"], core)
    here["along_x"] = device(z, y, 1 - x, core)
    here["along_y"] = device(z, 1 - y, x, core)
    here["line_group"] = (
        z * 2 + core, 8, lambda index: device(index // 2, y, x, index % 2)
    )
    here["plane_group"] = (
        y * 2 + x, 4, lambda index: device(z, index // 2, index % 2, core)
    )
    here["mine"] = pl.ds(pl.multiple_of(core * HALF, 128), HALF)
    here["other"] = pl.ds(pl.multiple_of((1 - core) * HALF, 128), HALF)
    return here


def send(source, target, sent, arrived, device):
    return pltpu.make_async_remote_copy(
        src_ref=source,
        dst_ref=target,
        send_sem=sent,
        recv_sem=arrived,
        device_id=device,
        device_id_type=pl.DeviceIdType.MESH,
    )


def inside(index):
    if isinstance(index, int):
        return 0 <= index < PIECES
    return jnp.logical_and(index >= 0, index < PIECES)


def guarded(index, body):
    if isinstance(index, int):
        if inside(index):
            body(index)
    else:
        pl.when(inside(index))(lambda: body(index))


def layer(
    lengths, null_flags, tokens, cotangent, weights, moment1, moment2, vectors,
    normed_out, input_grad, new_moment1, new_moment2, new_weights, vec_total, square_pairs,
    walls, normed, token_low, qkv, context, hidden_low, act, slope, grad, grad_low, side, inverse,
    log_total, vec_grad, mat, mat_send, mat_got, pair_keep, pair_send, pair_got,
    line_keep, line_send, line_got, z_keep, z_send, z_got,
    shares, qkv_bias, ffn_bias, squares, squares_got,
    in_sem, out_sem, twin_sem, gather_sent, gather_got, reduce_sent, reduce_got,
    vec_sem, state_sem, square_sem, cot_sem,
):
    here = place()
    z, y, x, core, high, low = (here[name] for name in ("z", "y", "x", "core", "high", "low"))
    y1, x1, y2, x2 = (here[name] for name in ("y1", "x1", "y2", "x2"))
    mine, other = here["mine"], here["other"]

    def turn_of(index, count):
        return index % count if isinstance(index, int) else lax.rem(index, count)

    def valid(slot):
        return jnp.where(null_flags[slot] == 1, QLEN, lengths[slot])

    def state_rows(quarter, chunk):
        return pl.ds(quarter * SLOT + 24 * chunk, 24)

    def state_copy(array, buffer, quarter, chunk):
        return pltpu.make_async_copy(
            array.at[:, pl.ds(TILE * chunk, TILE)],
            buffer.at[state_rows(quarter, chunk), :],
            state_sem.at[quarter, chunk],
        )

    def result_copy(array, quarter, chunk):
        return pltpu.make_async_copy(
            normed.at[state_rows(quarter, chunk), :],
            array.at[:, pl.ds(TILE * chunk, TILE)],
            state_sem.at[quarter, chunk],
        )

    for chunk in range(PIECES):
        state_copy(weights, grad, 0, chunk).start()
    def cot_copy(slot):
        return pltpu.make_async_copy(
            cotangent.at[slot_rows(slot), :], side.at[turn_of(slot, 2)], cot_sem.at[slot]
        )

    def output_copy(slot):
        return pltpu.make_async_copy(
            side.at[turn_of(slot, 2)], normed_out.at[slot_rows(slot), :], out_sem.at[slot]
        )

    def grad_copy(slot):
        rows = slot_rows(slot)
        return pltpu.make_async_copy(grad.at[rows, :], input_grad.at[rows, :], out_sem.at[slot])

    for slot in range(2):
        cot_copy(slot).start()
    tok_copy = pltpu.make_async_copy(tokens, normed, in_sem.at[1])
    tok_copy.start()

    barrier = pltpu.get_barrier_semaphore()
    peers = []
    for group in ("line_group", "plane_group"):
        index, size, device_of = here[group]
        peers += [device_of((index + step) % size) for step in range(1, size)]
    for peer in peers:
        pl.semaphore_signal(barrier, inc=1, device_id=peer, device_id_type=pl.DeviceIdType.MESH)
    pl.semaphore_wait(barrier, len(peers))

    for chunk in range(PIECES):
        state_copy(weights, grad, 0, chunk).wait()
    for unit in range(3):
        for half in range(2):
            for part in range(3):
                lanes = slice((unit + 3 * half) * 128, (unit + 3 * half + 1) * 128)
                place_lanes = slice((3 * half + part) * 128, (3 * half + part + 1) * 128)
                grad[state_rows(1, unit), place_lanes] = grad[state_rows(0, part), lanes]

    def swap(first, count):
        rows = pl.ds(24 * first, 24 * count)
        return send(
            grad.at[pl.ds(SLOT + 24 * first, 24 * count), other],
            shares.at[rows, other],
            twin_sem.at[0, first],
            twin_sem.at[1, first],
            here["twin"],
        )

    swap(0, 3).start()
    def fill(piece):
        rows = pl.ds(pl.multiple_of(24 * piece, 8), 24)
        own, twin = grad[pl.ds(pl.multiple_of(SLOT + 24 * piece, 8), 24), mine], shares[rows, mine]
        upper = jnp.where(core == 0, own, twin)
        lower = jnp.where(core == 0, twin, own)
        joined = jnp.concatenate([upper, lower], axis=0)
        walls[piece, high, low, y, x, :, mine] = joined.astype(LOW)

    swap(0, 3).wait()
    each(3, fill)

    own, line = (high, low, y, x), (slice(None), low, y, x)
    column, next_column = (slice(None), slice(None), y, x), (slice(None), slice(None), y1, x1)
    everything = (slice(None),) * 4
    paths = (
        (
            ((own, "far_z"),),
            ((line, "near_z"),),
            ((column, "first"), (column, "second")),
            ((next_column, "second"),),
            ((everything, "twin"),),
        ),
        (
            ((own, "first"), (own, "far_z")),
            (((high, low, y1, x1), "far_z"), (line, "near_z")),
            (((slice(None), low, y1, x1), "near_z"), (column, "second")),
            ((next_column, "second"),),
            ((everything, "twin"),),
        ),
    )

    def gather_copies(piece, path, stage):
        first = sum(len(copies) for copies in paths[path][:stage])
        copies = []
        for index, (blocks, device) in enumerate(paths[path][stage]):
            part = walls.at[(piece,) + blocks + (slice(None), mine)]
            sent, got = (
                array.at[piece, first + index] for array in (gather_sent, gather_got)
            )
            copies.append(send(part, part, sent, got, here[device]))
        return copies

    def gather(base, index=0):
        def advance(piece, path, stage):
            if stage > 0:
                for copy in gather_copies(piece, path, stage - 1):
                    copy.wait_recv()
            if stage < 5:
                for copy in gather_copies(piece, path, stage):
                    copy.start()
            else:
                for done in range(5):
                    for copy in gather_copies(piece, path, done):
                        copy.wait_send()

        for stage in range(5, -1, -1):
            if (base - 3 * stage) % 2:
                continue

            def step(piece, stage=stage):
                if isinstance(piece, int):
                    advance(piece, min(piece % 3, 1), stage)
                else:
                    turn = lax.rem(piece, 3)
                    pl.when(turn == 0)(lambda: advance(piece, 0, stage))
                    pl.when(turn != 0)(lambda: advance(piece, 1, stage))

            guarded((base - 3 * stage) // 2 + index, step)

    def weight(piece):
        return walls[piece].reshape(TILE, TILE)

    gather(0)
    gather(1)
    make_order(act)
    for block in range(6):
        values = jnp.concatenate(
            [
                grad[state_rows(0, 4 + part // 3), part % 3 * 256 : part % 3 * 256 + 256]
                for part in (2 * block, 2 * block + 1)
            ],
            axis=1,
        )
        ordered = dot(values.astype(LOW), act[0, 0:512, 0:512], 1, 1)
        for chunk in range(4):
            grad[state_rows(1, 4 + chunk), block * 128 : block * 128 + 128] = ordered[
                :, chunk * 128 : chunk * 128 + 128
            ]
    for chunk in (3, 8, 9, 10, 11):
        grad[state_rows(1, chunk), :] = grad[state_rows(0, chunk), :]
    swap(3, 9).start()
    gather(2)
    gather(3)
    vec_grad[...] = jnp.zeros_like(vec_grad)
    for unit in range(3):
        for half in range(2):
            lanes = slice((unit + 3 * half) * 128, (unit + 3 * half + 1) * 128)
            for part, row in ((0, 0), (2, 1)):
                target = slice((3 * half + part) * 128, (3 * half + part + 1) * 128)
                qkv_bias[unit, :, target] = vectors[row : row + 1, lanes]
            target = slice((3 * half + 1) * 128, (3 * half + 2) * 128)
            qkv_bias[unit, :, target] = jnp.zeros((1, 128), SUM)
    for block in range(6):
        values = jnp.concatenate(
            [
                vectors[8 + part // 3 : 9 + part // 3, part % 3 * 256 : part % 3 * 256 + 256]
                for part in (2 * block, 2 * block + 1)
            ],
            axis=1,
        )
        ordered = reorder(values, act, 1)
        for chunk in range(4):
            ffn_bias[chunk, :, block * 128 : block * 128 + 128] = ordered[
                :, chunk * 128 : chunk * 128 + 128
            ]

    gather(4)
    gather(5)
    swap(3, 9).wait()
    each(9, lambda piece: fill(3 + piece))
    gather(6)
    gather(7)
    tok_copy.wait()

    def cast_slot(slot):
        rows = slot_rows(slot)
        token_low[rows, :] = normed[rows, :].astype(LOW)

    each(4, cast_slot)
    for tick in range(8, 16):
        gather(tick)

    def project(unit):
        def project_slot(slot):
            rows = slot_rows(slot)
            values = dot(token_low[rows, :], weight(unit), 1, 0) + qkv_bias[unit]
            qkv[unit, rows, :] = values.astype(LOW)

        each(4, project_slot, 2)

        def attend_slots(pair):
            def attend_slot(slot):
                index = 2 * pair + slot
                attend(unit, index, valid(index), qkv, context, log_total)

            each(2, attend_slot, 2)
            pl.when(pair == 0)(lambda: gather(16, unit))
            pl.when(pair == 1)(lambda: gather(17, unit))

        each(2, attend_slots)

    each(3, project)

    def attend_out(slot):
        rows = slot_rows(slot)
        values = normed[rows, :] + (dot(context[rows, :], weight(3), 1, 0) + vectors[2:3, :])
        centred = values - mean_lanes(values)
        inv = lax.rsqrt(mean_lanes(centred * centred) + 1e-05)
        unit_values = centred * inv
        normed[rows, :] = unit_values
        inverse[rows, :] = jnp.broadcast_to(inv, (SLOT, 128))
        hidden_low[rows, :] = (unit_values * vectors[3:4, :] + vectors[4:5, :]).astype(LOW)

    gather(22)
    each(4, attend_out, 2)

    def widen(chunk):
        gather(23, chunk)

        def widen_slot(slot):
            rows = slot_rows(slot)
            pre = dot(hidden_low[rows, :], weight(4 + chunk), 1, 0) + ffn_bias[chunk]
            phi = 0.5 + 0.5 * lax.erf(pre * 0.7071067811865476)
            act[chunk, rows, :] = (pre * phi).astype(LOW)
            bell = jnp.exp(pre * pre * -0.5) * 0.3989422804014327
            slope[chunk, rows, :] = (phi + pre * bell).astype(LOW)

        each(2, widen_slot, 2)
        gather(24, chunk)
        each(2, lambda slot: widen_slot(2 + slot), 2)

    each(4, widen, 4)
    def narrow_first(slot):
        rows = slot_rows(slot)
        start = normed[rows, :] * vectors[3:4, :] + (vectors[4:5, :] + vectors[5:6, :])
        grad[rows, :] = start + dot(act[0, rows, :], weight(8), 1, 0)

    gather(31)
    each(4, narrow_first, 2)
    gather(32)

    def narrow(chunk):
        def narrow_slot(slot):
            rows = slot_rows(slot)
            grad[rows, :] += dot(act[1 + chunk, rows, :], weight(9 + chunk), 1, 0)

        each(4, narrow_slot, 2)

    gather(33)
    narrow(0)
    gather(34)
    gather(35)
    narrow(1)
    gather(36)
    gather(37)

    def finish_slot(slot):
        rows = slot_rows(slot)

        @pl.when(jnp.logical_and(slot >= 1, slot < 3))
        def _():
            output_copy(slot - 1).wait()
            cot_copy(slot + 1).start()

        values = grad[rows, :] + dot(act[3, rows, :], weight(11), 1, 0)
        centred = values - mean_lanes(values)
        inv = lax.rsqrt(mean_lanes(centred * centred) + 1e-05)
        unit_values = centred * inv
        kept = lax.broadcasted_iota(jnp.int32, (SLOT, 1), 0) < valid(slot)
        cot_copy(slot).wait()
        grad_out = jnp.where(kept, side[turn_of(slot, 2)], 0.0)
        side[turn_of(slot, 2)] = unit_values
        output_copy(slot).start()
        vec_grad[6:7, :] += sum_rows(grad_out * unit_values)
        vec_grad[7:8, :] += sum_rows(grad_out)
        scaled = grad_out * vectors[6:7, :]
        result = inv * (
            scaled - mean_lanes(scaled) - unit_values * mean_lanes(scaled * unit_values)
        )
        grad[rows, :] = result
        rounded = result.astype(LOW)
        grad_low[rows, :] = rounded
        vec_grad[5:6, :] += sum_rows(rounded.astype(SUM))

    each(4, finish_slot)
    output_copy(2).wait()
    output_copy(3).wait()

    def reduce_copies(index, stage):
        two, four = turn_of(index, 2), turn_of(index, 4)
        if stage == 3:
            triples = [
                (line_z(step), z_send.at[two, step - 1], z_got.at[four, step - 1])
                for step in range(1, 4)
            ]
        else:
            triples = [
                (
                    None,
                    (here["second"], pair_send.at[two], pair_got.at[four]),
                    (here["first"], line_send.at[two], line_got.at[four]),
                )[stage]
            ]
        return [
            send(
                source,
                target,
                reduce_sent.at[stage + step, two],
                reduce_got.at[stage + step, four],
                device,
            )
            for step, (device, source, target) in enumerate(triples)
        ]

    def half_copy(index, part):
        two = turn_of(index, 2)
        return send(
            mat_send.at[part],
            mat_got.at[two, part],
            reduce_sent.at[6 * part, two],
            reduce_got.at[6 * part, two],
            here["twin"],
        )

    def line_z(step):
        return ((z + step) % 4 * 2 + y, x * 2 + core)

    def begin(index, stage):
        for copy in reduce_copies(index, stage):
            copy.start()

    def end(index, stage):
        for copy in reduce_copies(index, stage):
            copy.wait()

    def folded(rows):
        return jnp.concatenate([rows[..., :HALF], rows[..., HALF:]], axis=-2)

    def reduce(notch):
        def first(index):
            for part in range(2):
                half_copy(index, part).wait()
            turn, got = turn_of(index, 2), turn_of(index, 2)

            ours = pl.ds(pl.multiple_of(24 * core, 8), 24)

            def column(row, col):
                own_rows = folded(mat[:, :, row, col, ours, :])
                return own_rows + mat_got[got, :, :, row, col].astype(SUM)

            pair_send[turn, 0] = column(y2, x2).astype(LOW)
            pair_send[turn, 1] = column(1 - y, 1 - x).astype(LOW)
            begin(index, 1)
            pair_keep[turn, 0] = column(y, x)
            pair_keep[turn, 1] = column(y1, x1)

        def third(index):
            end(index, 2)
            turn, got = turn_of(index, 2), turn_of(index, 4)

            def block(place):
                row, col = place // 2, place % 2
                return line_keep[turn, row, col] + line_got[got, row, col].astype(SUM)

            for step in range(1, 4):
                z_send[turn, step - 1] = block((z + step) % 4).astype(LOW)
            begin(index, 3)
            z_keep[turn] = block(z)

        guarded(notch - 4, third)
        guarded(notch - 1, first)

    def reduce_odd(notch):
        def second(index):
            end(index, 1)
            turn, got = turn_of(index, 2), turn_of(index, 4)
            line_send[turn] = (pair_keep[turn, 1] + pair_got[got, 1].astype(SUM)).astype(LOW)
            begin(index, 2)
            line_keep[turn] = pair_keep[turn, 0] + pair_got[got, 0].astype(SUM)

        def fourth(index):
            end(index, 3)
            turn, got = turn_of(index, 2), turn_of(index, 4)
            total = z_keep[turn]
            for step in range(3):
                total += z_got[got, step].astype(SUM)
            rows = pl.ds(pl.multiple_of(24 * index, 8), 24)
            shares[rows, :HALF] = total[:24]
            shares[rows, HALF:] = total[24:]

        guarded(notch - 2, second)
        guarded(notch - 5, fourth)

    def emit(index, left, right, unroll=2):
        reduce(index)
        shape = mat.shape[1:]


        theirs = pl.ds(pl.multiple_of(24 * (1 - core), 8), 24)

        def multiply(part):
            lanes = pl.ds(pl.multiple_of(part * HALF, 128), HALF)
            mat[part] = dot(left[:, lanes], right[...], 0, 0).reshape(shape)
            mat_send[part] = folded(mat[part, :, :, :, theirs, :]).astype(LOW)
            half_copy(index, part).start()

        each(2, multiply, unroll)
        reduce_odd(index)

    def back_chunk(chunk):
        emit(2 * chunk, act.at[chunk], grad_low)

        def back_slot(slot):
            rows = slot_rows(slot)
            values = dot(grad_low[rows, :], weight(8 + chunk), 1, 1)
            rounded = (values * slope[chunk, rows, :].astype(SUM)).astype(LOW)
            slope[chunk, rows, :] = rounded
            row = pl.ds(8 + chunk, 1)
            vec_grad[row, :] += sum_rows(rounded.astype(SUM))

        each(4, back_slot, 4)
        emit(2 * chunk + 1, hidden_low, slope.at[chunk])

        def back_hidden(slot):
            rows = slot_rows(slot)
            grad[rows, :] += dot(slope[chunk, rows, :], weight(4 + chunk), 1, 1)

        each(4, back_hidden, 4)

    each(4, back_chunk, 4)

    def back_norm(slot):
        rows = slot_rows(slot)
        total = grad[rows, :]
        unit_values = normed[rows, :]
        vec_grad[3:4, :] += sum_rows(total * unit_values)
        vec_grad[4:5, :] += sum_rows(total)
        scaled = total * vectors[3:4, :]
        inv = inverse[rows, 0:1]
        result = inv * (
            scaled - mean_lanes(scaled) - unit_values * mean_lanes(scaled * unit_values)
        )
        grad[rows, :] = result
        rounded = result.astype(LOW)
        grad_low[rows, :] = rounded
        vec_grad[2:3, :] += sum_rows(rounded.astype(SUM))

    each(4, back_norm)
    emit(8, context, grad_low)
    states = (moment1, moment2, weights)
    for quarter, array in enumerate(states):
        for chunk in range(PIECES):
            state_copy(array, normed, quarter, chunk).start()

    def back_context(slot):
        rows = slot_rows(slot)
        context[rows, :] = dot(grad_low[rows, :], weight(3), 1, 1).astype(LOW)

    each(4, back_context, 4)

    def back_unit(unit):
        each(
            4,
            lambda slot: attend_back(unit, slot, valid(slot), qkv, context, log_total, vec_grad),
        )
        emit(9 + unit, token_low, qkv.at[unit], 1)

    each(3, back_unit)

    def exchange(group, source, slots, sems):
        index, size, device_of = here[group]

        def copies(outgoing):
            found = []
            for step in range(1, size):
                other_index = (index + (step if outgoing else size - step)) % size
                found.append(
                    send(
                        source,
                        slots(index if outgoing else other_index),
                        sems.at[0, step],
                        sems.at[1, index if outgoing else other_index],
                        device_of(other_index),
                    )
                )
            return found

        def start():
            for copy in copies(True):
                copy.start()
            slots(index)[...] = source[...]

        def wait():
            for copy in copies(True):
                copy.wait_send()
            for copy in copies(False):
                copy.wait_recv()
            total = slots(0)[...]
            for slot in range(1, size):
                total += slots(slot)[...]
            source[...] = total

        return start, wait

    def back_tokens(slot):
        rows = slot_rows(slot)
        total = grad[rows, :]
        for unit in range(3):
            total += dot(qkv[unit, rows, :], weight(unit), 1, 1)
        grad[rows, :] = total
        grad_copy(slot).start()

    def lane_sums(values):
        total = sum_rows(values)
        return sum(total[:, 128 * index : 128 * index + 128] for index in range(6))

    def group_of(chunk):
        return 0 if chunk < 3 else 1 if chunk == 3 else 2 if chunk < 8 else 3

    def adapt_chunk(chunk):
        row = 4 + group_of(chunk)
        first, second, step = adapt(
            *(normed[state_rows(quarter, chunk), :] for quarter in (0, 1, 3))
        )
        step = step + 0.01 * normed[state_rows(2, chunk), :]
        normed[state_rows(0, chunk), :] = first
        normed[state_rows(1, chunk), :] = second
        normed[state_rows(3, chunk), :] = step
        result_copy(new_moment1, 0, chunk).start()
        result_copy(new_moment2, 1, chunk).start()
        squares[row : row + 1, :] += lane_sums(step * step)

    def weight_squares():
        squares[...] = jnp.zeros_like(squares)
        for quarter, array in enumerate(states):
            for chunk in range(PIECES):
                state_copy(array, normed, quarter, chunk).wait()
        for chunk in range(PIECES):
            held = normed[state_rows(2, chunk), :]
            row = group_of(chunk)
            squares[row : row + 1, :] += lane_sums(held * held)

    def adapt_early():
        make_order(act)
        normed[state_rows(3, 3), :] = shares[pl.ds(24 * 8, 24), :]
        for chunk in range(4):
            normed[state_rows(3, 8 + chunk), :] = shares[pl.ds(24 * 2 * chunk, 24), :]
        for block in range(6):
            values = jnp.concatenate(
                [
                    shares[pl.ds(24 * (2 * chunk + 1), 24), block * 128 : block * 128 + 128]
                    for chunk in range(4)
                ],
                axis=1,
            )
            ordered = reorder(values, act, 0)
            for half in range(2):
                part = 2 * block + half
                lanes = slice(part % 3 * 256, part % 3 * 256 + 256)
                normed[state_rows(3, 4 + part // 3), lanes] = ordered[
                    :, half * 256 : half * 256 + 256
                ]
        for chunk in range(3, PIECES):
            adapt_chunk(chunk)

    def adapt_late():
        for unit in range(3):
            for half in range(2):
                for part in range(3):
                    lanes = slice((unit + 3 * half) * 128, (unit + 3 * half + 1) * 128)
                    source = slice((3 * half + part) * 128, (3 * half + part + 1) * 128)
                    normed[state_rows(3, part), lanes] = shares[pl.ds(24 * (9 + unit), 24), source]
        for chunk in range(3):
            adapt_chunk(chunk)

    def order_vectors():
        for block in range(6):
            values = jnp.concatenate(
                [
                    vec_grad[8 + chunk : 9 + chunk, block * 128 : block * 128 + 128]
                    for chunk in range(4)
                ],
                axis=1,
            )
            ordered = reorder(values, act, 0)
            for half in range(2):
                part = 2 * block + half
                lanes = slice(part % 3 * 256, part % 3 * 256 + 256)
                row = 8 + part // 3
                vec_total[row : row + 1, lanes] = ordered[:, half * 256 : half * 256 + 256]
        vec_total[0:8, :] = vec_grad[0:8, :]

    def vec_slots(turn):
        return lambda slot: side.at[turn, pl.ds(pl.multiple_of(16 * slot, 8), 16), :]

    def square_slots(turn):
        return lambda slot: squares_got.at[turn, slot]

    exchanges = [
        exchange(group, array, slots, sems)
        for group, array, slots, sems in (
            ("line_group", vec_grad, vec_slots(0), vec_sem.at[0]),
            ("plane_group", vec_grad, vec_slots(1), vec_sem.at[1]),
            ("line_group", squares, square_slots(0), square_sem.at[0]),
            ("plane_group", squares, square_slots(1), square_sem.at[1]),
        )
    ]
    exchanges[0][0]()

    def drain(step):
        reduce(12 + step)
        pl.when(step < 4)(lambda: back_tokens(step))
        pl.when(step == 0)(weight_squares)

        @pl.when(step == 1)
        def _():
            exchanges[0][1]()
            exchanges[1][0]()

        pl.when(step == 3)(adapt_early)
        reduce_odd(12 + step)

    each(5, drain)
    exchanges[1][1]()
    adapt_late()
    exchanges[2][0]()
    order_vectors()
    exchanges[2][1]()
    exchanges[3][0]()
    exchanges[3][1]()
    sums = jnp.sum(squares[...], axis=1, keepdims=True)
    square_pairs[:, 0:1] = sums[0:4]
    square_pairs[:, 1:2] = sums[4:8]
    norms = jnp.sqrt(sums)
    ratio = norms[0:4] / (norms[4:8] + 1e-06)
    for chunk in range(PIECES):
        group = group_of(chunk)
        rows = state_rows(2, chunk)
        factor = 0.3 * ratio[group : group + 1, :]
        normed[rows, :] = normed[rows, :] - factor * normed[state_rows(3, chunk), :]
        result_copy(new_weights, 2, chunk).start()
    for quarter, array in enumerate((new_moment1, new_moment2, new_weights)):
        for chunk in range(PIECES):
            result_copy(array, quarter, chunk).wait()
    for slot in range(4):
        grad_copy(slot).wait()


def fused(
    tokens,
    cotangent,
    lengths,
    null_flags,
    weights,
    moment1,
    moment2,
    vectors,
    vec_moment1,
    vec_moment2,
):
    rows = tokens.shape[0]
    vmem = pl.BlockSpec(memory_space=pltpu.VMEM)
    smem = pl.BlockSpec(memory_space=pltpu.SMEM)
    hbm = pl.BlockSpec(memory_space=pl.ANY)
    full = lambda *shape: pltpu.VMEM(shape, SUM)
    low = lambda *shape: pltpu.VMEM(shape, LOW)
    copies = lambda *shape: pltpu.SemaphoreType.DMA(shape)
    like = lambda array: jax.ShapeDtypeStruct(array.shape, array.dtype)
    unit_values, input_grad, first, second, new_weights, vec_total, squares = pl.pallas_call(
        layer,
        out_shape=[
            like(tokens),
            like(tokens),
            like(weights),
            like(weights),
            like(weights),
            like(vectors),
            jax.ShapeDtypeStruct((4, 2), SUM),
        ],
        in_specs=[smem, smem] + [hbm] * 5 + [vmem],
        out_specs=[hbm] * 5 + [vmem] * 2,
        scratch_shapes=[
            low(PIECES, 2, 2, 2, 2, 48, TILE),
            full(rows, TILE),
            low(rows, TILE),
            low(3, rows, TILE),
            low(rows, TILE),
            low(rows, TILE),
            low(4, rows, TILE),
            low(4, rows, TILE),
            full(rows, TILE),
            low(rows, TILE),
            full(2, SLOT, TILE),
            full(rows, 128),
            full(3, 4, 4, SLOT),
            full(16, TILE),
            full(2, 2, 2, 2, 48, TILE),
            low(2, 2, 2, 2, 48, HALF),
            low(2, 2, 2, 2, 2, 48, HALF),
            full(2, 2, 2, 2, 48, HALF),
            low(2, 2, 2, 2, 48, HALF),
            low(4, 2, 2, 2, 48, HALF),
            full(2, 2, 2, 48, HALF),
            low(2, 2, 2, 48, HALF),
            low(4, 2, 2, 48, HALF),
            full(2, 48, HALF),
            low(2, 3, 48, HALF),
            low(4, 3, 48, HALF),
            full(SLOT, TILE),
            full(3, 1, TILE),
            full(4, 1, TILE),
            full(8, 128),
            full(2, 8, 8, 128),
            copies(2),
            copies(4),
            copies(2, 4),
            copies(PIECES, 8),
            copies(PIECES, 8),
            copies(7, 2),
            copies(7, 4),
            copies(2, 2, 8),
            copies(4, PIECES),
            copies(2, 2, 8),
            copies(4),
        ],
        compiler_params=pltpu.CompilerParams(
            collective_id=0, has_side_effects=True, vmem_limit_bytes=64 * 2**20
        ),
        cost_estimate=pl.CostEstimate(
            flops=60 * 10**9, bytes_accessed=60 * 10**6, transcendentals=10**7
        ),
    )(
        lengths,
        null_flags,
        tokens,
        cotangent,
        weights,
        moment1,
        moment2,
        vectors,
    )
    output = unit_values * vectors[6] + vectors[7]
    vec_first, vec_second, vec_step = adapt(vec_moment1, vec_moment2, vec_total)
    norm_pairs = jnp.sqrt(squares)
    trust = norm_pairs[:, 0] / (norm_pairs[:, 1] + 1e-06)
    return (
        output,
        input_grad,
        first,
        second,
        new_weights,
        vec_first,
        vec_second,
        vectors - 0.3 * vec_step,
        norm_pairs,
        trust,
    )


def solution(mesh):
    split = P(("dp", "shard"), None)
    flat = P(("dp", "shard"))
    in_specs = (split, split, flat, flat, split, split, split, P(), P(), P())
    out_specs = (split,) * 5 + (P(),) * 5
    body = fused if mesh.shape["dp"] == 8 and mesh.shape["shard"] == 4 else plain
    return jax.shard_map(body, mesh=mesh, in_specs=in_specs, out_specs=out_specs, check_vma=False)
```

```python
import jax
import jax.numpy as jnp
from jax import lax
from jax.experimental import pallas as pl
from jax.experimental.pallas import tpu as pltpu
from jax.sharding import PartitionSpec as P

HEADS = 12
SLOT = 288
QLEN = 64
STEP = 5


def norm_forward(values, gain, shift):
    centred = values - jnp.mean(values, axis=-1, keepdims=True)
    inverse = lax.rsqrt(jnp.mean(centred * centred, axis=-1, keepdims=True) + 1e-05)
    normed = centred * inverse
    return (normed * gain + shift, normed, inverse)


def norm_backward(grad_result, normed, inverse, gain):
    scaled = grad_result * gain
    grad_gain = jnp.sum(grad_result * normed, axis=0)
    grad_shift = jnp.sum(grad_result, axis=0)
    centred = scaled - jnp.mean(scaled, axis=-1, keepdims=True)
    grad_input = inverse * (centred - normed * jnp.mean(scaled * normed, axis=-1, keepdims=True))
    return (grad_input, grad_gain, grad_shift)


def gelu_slope(values):
    return (
        0.5 * (1.0 + jax.scipy.special.erf(values * 0.7071067811865476))
        + values * jnp.exp(-0.5 * values * values) * 0.3989422804014327
    )


def plain(
    tokens,
    cotangent,
    lengths,
    null_flags,
    weights,
    moment1,
    moment2,
    vectors,
    vec_moment1,
    vec_moment2,
):
    model_width = tokens.shape[1]
    row_count = tokens.shape[0]
    slot_count = lengths.shape[0]
    head_size = model_width // HEADS
    score_scale = head_size ** (-0.5)
    block_slots = min(2, slot_count)
    block_count = slot_count // block_slots
    valid_len = jnp.where(null_flags == 1, QLEN, lengths)
    key_valid = jnp.arange(SLOT, dtype=jnp.int32)[None, :] < valid_len[:, None]
    key_blocks = key_valid.reshape(block_count, block_slots, SLOT)
    row_weight = key_valid.reshape(row_count, 1).astype(jnp.float32)
    qkv_bias = jnp.concatenate([vectors[0], jnp.zeros((model_width,), jnp.float32), vectors[1]])
    ffn_bias = vectors[8:12].reshape(4 * model_width)
    token_low = tokens.astype(jnp.bfloat16)

    def block_scores(qkv_block, valid_keys):
        scores = (
            jnp.einsum(
                "bqhd,bkhd->bhqk",
                qkv_block[:, :, 0],
                qkv_block[:, :, 1],
                preferred_element_type=jnp.float32,
            )
            * score_scale
        )
        return jnp.where(valid_keys[:, None, None, :], scores, -1000000000.0)

    def attend_block(packed):
        qkv_block, valid_keys = packed
        scores = block_scores(qkv_block, valid_keys)
        row_top = jnp.max(scores, axis=-1, keepdims=True)
        exponent = jnp.exp(scores - row_top)
        row_total = jnp.sum(exponent, axis=-1, keepdims=True)
        softmax_out = (exponent / row_total).astype(jnp.bfloat16)
        context = jnp.einsum(
            "bhqk,bkhd->bqhd", softmax_out, qkv_block[:, :, 2], preferred_element_type=jnp.float32
        )
        return (context.astype(jnp.bfloat16), (row_top + jnp.log(row_total))[..., 0])

    def attend_back(packed):
        qkv_block, valid_keys, log_block, grad_block = packed
        scores = block_scores(qkv_block, valid_keys)
        softmax_out = jnp.exp(scores - log_block[..., None])
        grad_values = jnp.einsum(
            "bhqk,bqhd->bkhd",
            softmax_out.astype(jnp.bfloat16),
            grad_block,
            preferred_element_type=jnp.float32,
        )
        grad_soft = jnp.einsum(
            "bqhd,bkhd->bhqk", grad_block, qkv_block[:, :, 2], preferred_element_type=jnp.float32
        )
        grad_scores = softmax_out * (
            grad_soft - jnp.sum(grad_soft * softmax_out, axis=-1, keepdims=True)
        )
        scores_low = grad_scores.astype(jnp.bfloat16)
        grad_query = (
            jnp.einsum(
                "bhqk,bkhd->bqhd",
                scores_low,
                qkv_block[:, :, 1],
                preferred_element_type=jnp.float32,
            )
            * score_scale
        )
        grad_keys = (
            jnp.einsum(
                "bhqk,bqhd->bkhd",
                scores_low,
                qkv_block[:, :, 0],
                preferred_element_type=jnp.float32,
            )
            * score_scale
        )
        return jnp.stack([grad_query, grad_keys, grad_values], axis=2).astype(jnp.bfloat16)

    gathered = lax.all_gather(weights.astype(jnp.bfloat16), ("dp", "shard"), axis=0, tiled=True)
    first_mats = (
        gathered[:, : 3 * model_width],
        gathered[:, 3 * model_width : 4 * model_width],
        gathered[:, 4 * model_width : 8 * model_width],
        gathered[:, 8 * model_width :].reshape(4 * model_width, model_width),
    )
    w_qkv, w_out, w_in, w_down = first_mats
    qkv_low = (jnp.dot(token_low, w_qkv, preferred_element_type=jnp.float32) + qkv_bias).astype(
        jnp.bfloat16
    )
    qkv_blocks = qkv_low.reshape(block_count, block_slots, SLOT, 3, HEADS, head_size)
    contexts, log_total = lax.map(attend_block, (qkv_blocks, key_blocks))
    context_low = contexts.reshape(row_count, model_width)
    attention = jnp.dot(context_low, w_out, preferred_element_type=jnp.float32) + vectors[2]
    hidden_one, normed_one, inverse_one = norm_forward(tokens + attention, vectors[3], vectors[4])
    hidden_low = hidden_one.astype(jnp.bfloat16)
    pre_act = jnp.dot(hidden_low, w_in, preferred_element_type=jnp.float32) + ffn_bias
    act_low = jax.nn.gelu(pre_act, approximate=False).astype(jnp.bfloat16)
    ffn_out = jnp.dot(act_low, w_down, preferred_element_type=jnp.float32) + vectors[5]
    result, normed_two, inverse_two = norm_forward(hidden_one + ffn_out, vectors[6], vectors[7])
    first_kept = (
        qkv_blocks,
        log_total,
        context_low,
        normed_one,
        inverse_one,
        hidden_low,
        pre_act,
        act_low,
        normed_two,
        inverse_two,
        result,
    )
    output = first_kept[10]
    w_qkv, w_out, w_in, w_down = first_mats
    (
        qkv_blocks,
        log_total,
        context_low,
        normed_one,
        inverse_one,
        hidden_low,
        pre_act,
        act_low,
        normed_two,
        inverse_two,
    ) = first_kept[:10]
    grad_result = cotangent * row_weight
    grad_two, grad_gain_two, grad_shift_two = norm_backward(
        grad_result, normed_two, inverse_two, vectors[6]
    )
    grad_ffn_low = grad_two.astype(jnp.bfloat16)
    grad_bias_down = jnp.sum(grad_ffn_low, axis=0, dtype=jnp.float32)
    grad_down = jnp.einsum("tf,td->fd", act_low, grad_ffn_low, preferred_element_type=jnp.float32)
    grad_act = jnp.einsum("td,fd->tf", grad_ffn_low, w_down, preferred_element_type=jnp.float32)
    grad_pre_low = (grad_act * gelu_slope(pre_act)).astype(jnp.bfloat16)
    grad_bias_in = jnp.sum(grad_pre_low, axis=0, dtype=jnp.float32)
    grad_in = jnp.einsum("td,tf->df", hidden_low, grad_pre_low, preferred_element_type=jnp.float32)
    grad_hidden = grad_two + jnp.einsum(
        "tf,df->td", grad_pre_low, w_in, preferred_element_type=jnp.float32
    )
    grad_residual, grad_gain_one, grad_shift_one = norm_backward(
        grad_hidden, normed_one, inverse_one, vectors[3]
    )
    grad_attn_low = grad_residual.astype(jnp.bfloat16)
    grad_bias_out = jnp.sum(grad_attn_low, axis=0, dtype=jnp.float32)
    grad_out = jnp.einsum(
        "tc,td->cd", context_low, grad_attn_low, preferred_element_type=jnp.float32
    )
    grad_context = jnp.einsum(
        "td,cd->tc", grad_attn_low, w_out, preferred_element_type=jnp.float32
    ).astype(jnp.bfloat16)
    grad_blocks = grad_context.reshape(block_count, block_slots, SLOT, HEADS, head_size)
    grad_qkv_low = lax.map(attend_back, (qkv_blocks, key_blocks, log_total, grad_blocks)).reshape(
        row_count, 3 * model_width
    )
    grad_bias_qkv = jnp.sum(grad_qkv_low, axis=0, dtype=jnp.float32)
    grad_qkv = jnp.einsum("td,te->de", token_low, grad_qkv_low, preferred_element_type=jnp.float32)
    input_grad = grad_residual + jnp.einsum(
        "te,de->td", grad_qkv_low, w_qkv, preferred_element_type=jnp.float32
    )
    vector_grad = jnp.concatenate(
        [
            jnp.stack(
                [
                    grad_bias_qkv[:model_width],
                    grad_bias_qkv[2 * model_width :],
                    grad_bias_out,
                    grad_gain_one,
                    grad_shift_one,
                    grad_bias_down,
                    grad_gain_two,
                    grad_shift_two,
                ]
            ),
            grad_bias_in.reshape(4, model_width),
        ],
        axis=0,
    )
    qkv_shard, out_shard, in_shard, down_shard = (
        lax.psum_scatter(grad_qkv, ("dp", "shard"), scatter_dimension=0, tiled=True),
        lax.psum_scatter(grad_out, ("dp", "shard"), scatter_dimension=0, tiled=True),
        lax.psum_scatter(grad_in, ("dp", "shard"), scatter_dimension=0, tiled=True),
        lax.psum_scatter(
            grad_down.reshape(model_width, 4 * model_width),
            ("dp", "shard"),
            scatter_dimension=0,
            tiled=True,
        ),
    )
    vector_total = lax.psum(vector_grad, ("dp", "shard"))
    grad_shard = jnp.concatenate([qkv_shard, out_shard, in_shard, down_shard], axis=1)
    correction = 1.0 - 0.5**STEP
    new_first = 0.5 * moment1 + 0.5 * grad_shard
    new_second = 0.5 * moment2 + 0.5 * grad_shard * grad_shard
    update = new_first / correction / (jnp.sqrt(new_second / correction) + 1e-06) + 0.01 * weights
    column_edges = (0, 3 * model_width, 4 * model_width, 8 * model_width, 12 * model_width)
    pair_rows = []
    for group_index in range(4):
        weight_part = weights[:, column_edges[group_index] : column_edges[group_index + 1]]
        update_part = update[:, column_edges[group_index] : column_edges[group_index + 1]]
        pair_rows.append(
            jnp.stack([jnp.sum(weight_part * weight_part), jnp.sum(update_part * update_part)])
        )
    pair_squares = jnp.stack(pair_rows)
    pair_total = lax.psum(pair_squares, ("dp", "shard"))
    norm_pairs = jnp.sqrt(pair_total)
    trust_ratio = norm_pairs[:, 0] / (norm_pairs[:, 1] + 1e-06)
    column_trust = jnp.concatenate(
        [
            jnp.ones((column_edges[group_index + 1] - column_edges[group_index],), jnp.float32)
            * trust_ratio[group_index]
            for group_index in range(4)
        ]
    )
    new_weights = weights - 0.3 * column_trust * update
    vec_first = 0.5 * vec_moment1 + 0.5 * vector_total
    vec_second = 0.5 * vec_moment2 + 0.5 * vector_total * vector_total
    new_vectors = vectors - 0.3 * (vec_first / correction) / (
        jnp.sqrt(vec_second / correction) + 1e-06
    )
    return (
        output,
        input_grad,
        new_first,
        new_second,
        new_weights,
        vec_first,
        vec_second,
        new_vectors,
        norm_pairs,
        trust_ratio,
    )


SUM = jnp.float32
LOW = jnp.bfloat16
PIECES = 12
TILE = 768
HALF = 384
NEG = -1e9
CORRECTION = 1.0 - 0.5**STEP


def dot(left, right, left_dim, right_dim):
    return lax.dot_general(
        left, right, (((left_dim,), (right_dim,)), ((), ())), preferred_element_type=SUM
    )


def slot_rows(slot):
    return pl.ds(pl.multiple_of(slot * SLOT, SLOT), SLOT)


def each(count, body, unroll=1):
    def step(index, carry):
        body(index)
        return carry

    lax.fori_loop(0, count, step, 0, unroll=unroll)


def mean_lanes(values):
    return jnp.mean(values, axis=-1, keepdims=True)


def sum_rows(values):
    return jnp.sum(values, axis=0, keepdims=True)


def head_operands(query, key, valid):
    lane = lax.broadcasted_iota(jnp.int32, query.shape, 1)
    row = lax.broadcasted_iota(jnp.int32, query.shape, 0)
    low_head = lane < 64
    bias = jnp.where(row < valid, 0.0, NEG).astype(LOW)
    scaled = query * jnp.asarray(0.125, LOW)
    one, zero = jnp.ones_like(query), jnp.zeros_like(query)
    queries = (
        jnp.where(low_head, scaled, jnp.where(lane == 64, one, zero)),
        jnp.where(low_head, jnp.where(lane == 0, one, zero), scaled),
    )
    keys = (
        jnp.where(low_head, key, jnp.where(lane == 64, bias, zero)),
        jnp.where(low_head, jnp.where(lane == 0, bias, zero), key),
    )
    return queries, keys, low_head


def attend(unit, slot, valid, qkv, context, log_total):
    rows = slot_rows(slot)
    items = []
    for half in range(2):
        query, key, value = (
            qkv[unit, rows, (3 * half + part) * 128 : (3 * half + part + 1) * 128]
            for part in range(3)
        )
        queries, keys, low_head = head_operands(query, key, valid)
        items += [(queries[head], keys[head], value) for head in range(2)]
    scores = [dot(key, query, 1, 1) for query, key, _ in items]
    results = []
    for index, values in enumerate(scores):
        top = jnp.max(values, axis=0, keepdims=True)
        exponent = jnp.exp(values - top)
        total = sum_rows(exponent)
        log_total[unit, slot, index : index + 1, :] = top + jnp.log(total)
        results.append((exponent * (1.0 / total)).astype(LOW))
    results = [dot(probs, item[2], 0, 0) for probs, item in zip(results, items)]
    for half in range(2):
        lanes = pl.ds(pl.multiple_of((unit + 3 * half) * 128, 128), 128)
        joined = jnp.where(low_head, results[2 * half], results[2 * half + 1])
        context[rows, lanes] = joined.astype(LOW)


def attend_back(unit, slot, valid, qkv, grad_context, log_total, vec_grad):
    rows = slot_rows(slot)
    for half in range(2):
        query, key, value = (
            qkv[unit, rows, (3 * half + part) * 128 : (3 * half + part + 1) * 128]
            for part in range(3)
        )
        lanes = pl.ds(pl.multiple_of((unit + 3 * half) * 128, 128), 128)
        grad = grad_context[rows, lanes]
        queries, keys, low_head = head_operands(query, key, valid)
        zero = jnp.zeros_like(grad)
        grads = (jnp.where(low_head, grad, zero), jnp.where(low_head, zero, grad))
        scores = [dot(keys[head], queries[head], 1, 1) for head in range(2)]
        grad_probs = [dot(value, grads[head], 1, 1) for head in range(2)]
        probs, grad_value = [], []
        for head in range(2):
            index = 2 * half + head
            probs.append(jnp.exp(scores[head] - log_total[unit, slot, index : index + 1, :]))
            grad_value.append(dot(probs[head].astype(LOW), grad, 1, 0))
        grad_key, grad_query = [], []
        for head in range(2):
            inner = sum_rows(grad_probs[head] * probs[head])
            low = (probs[head] * (grad_probs[head] - inner)).astype(LOW)
            grad_key.append(dot(low, query, 1, 0))
            grad_query.append(dot(low, key, 0, 0))
        for part, parts, scale in (
            (0, grad_query, 0.125),
            (1, grad_key, 0.125),
            (2, grad_value, 1.0),
        ):
            joined = (jnp.where(low_head, parts[0], parts[1]) * scale).astype(LOW)
            qkv[unit, rows, (3 * half + part) * 128 : (3 * half + part + 1) * 128] = joined
            if part != 1:
                row = part // 2
                vec_grad[row : row + 1, lanes] += sum_rows(joined.astype(SUM))


def adapt(first, second, value):
    new_first = 0.5 * first + 0.5 * value
    new_second = 0.5 * second + 0.5 * value * value
    step = (new_first / CORRECTION) / (jnp.sqrt(new_second / CORRECTION) + 1e-06)
    return new_first, new_second, step


def make_order(buffer):
    row = lax.broadcasted_iota(jnp.int32, (512, 512), 0)
    column = lax.broadcasted_iota(jnp.int32, (512, 512), 1)
    chosen = column == 4 * (row % 128) + row // 128
    buffer[0, 0:512, 0:512] = jnp.where(chosen, 1.0, 0.0).astype(LOW)


def reorder(values, buffer, side):
    first = values.astype(LOW)
    rest = values - first.astype(SUM)
    second = rest.astype(LOW)
    third = (rest - second.astype(SUM)).astype(LOW)
    order = buffer[0, 0:512, 0:512]
    return (dot(first, order, 1, side) + dot(second, order, 1, side)) + dot(third, order, 1, side)


def place():
    outer, inner = lax.axis_index("dp"), lax.axis_index("shard")
    z, y, x, core = outer // 2, outer % 2, inner // 2, inner % 2
    here = dict(z=z, y=y, x=x, core=core, high=z // 2, low=z % 2)
    here["y1"], here["x1"] = y + core * (1 - 2 * y), x + (1 - core) * (1 - 2 * x)
    here["y2"], here["x2"] = y + (1 - core) * (1 - 2 * y), x + core * (1 - 2 * x)
    device = lambda z, y, x, core: (z * 2 + y, x * 2 + core)
    here["twin"] = device(z, y, x, 1 - core)
    here["near_z"] = device(z + 1 - 2 * (z % 2), y, x, core)
    here["far_z"] = device((z + 2) % 4, y, x, core)
    here["first"] = device(z, here["y1"], here["x1"], core)
    here["second"] = device(z, here["y2"], here["x2"], core)
    here["along_x"] = device(z, y, 1 - x, core)
    here["along_y"] = device(z, 1 - y, x, core)
    here["line_group"] = (
        z * 2 + core, 8, lambda index: device(index // 2, y, x, index % 2)
    )
    here["plane_group"] = (
        y * 2 + x, 4, lambda index: device(z, index // 2, index % 2, core)
    )
    here["mine"] = pl.ds(pl.multiple_of(core * HALF, 128), HALF)
    here["other"] = pl.ds(pl.multiple_of((1 - core) * HALF, 128), HALF)
    return here


def send(source, target, sent, arrived, device):
    return pltpu.make_async_remote_copy(
        src_ref=source,
        dst_ref=target,
        send_sem=sent,
        recv_sem=arrived,
        device_id=device,
        device_id_type=pl.DeviceIdType.MESH,
    )


def inside(index):
    if isinstance(index, int):
        return 0 <= index < PIECES
    return jnp.logical_and(index >= 0, index < PIECES)


def guarded(index, body):
    if isinstance(index, int):
        if inside(index):
            body(index)
    else:
        pl.when(inside(index))(lambda: body(index))


def layer(
    lengths, null_flags, tokens, cotangent, weights, moment1, moment2, vectors,
    normed_out, input_grad, new_moment1, new_moment2, new_weights, vec_total, square_pairs,
    walls, normed, token_low, qkv, context, hidden_low, act, slope, grad, grad_low, side, inverse,
    log_total, vec_grad, mat, mat_send, mat_got, pair_keep, pair_send, pair_got,
    line_keep, line_send, line_got, z_keep, z_send, z_got,
    shares, qkv_bias, ffn_bias, squares, squares_got,
    in_sem, out_sem, twin_sem, gather_sent, gather_got, reduce_sent, reduce_got,
    vec_sem, state_sem, square_sem, cot_sem,
):
    here = place()
    z, y, x, core, high, low = (here[name] for name in ("z", "y", "x", "core", "high", "low"))
    y1, x1, y2, x2 = (here[name] for name in ("y1", "x1", "y2", "x2"))
    mine, other = here["mine"], here["other"]

    def turn_of(index, count):
        return index % count if isinstance(index, int) else lax.rem(index, count)

    def valid(slot):
        return jnp.where(null_flags[slot] == 1, QLEN, lengths[slot])

    def state_rows(quarter, chunk):
        return pl.ds(quarter * SLOT + 24 * chunk, 24)

    def state_copy(array, buffer, quarter, chunk):
        return pltpu.make_async_copy(
            array.at[:, pl.ds(TILE * chunk, TILE)],
            buffer.at[state_rows(quarter, chunk), :],
            state_sem.at[quarter, chunk],
        )

    def result_copy(array, quarter, chunk):
        return pltpu.make_async_copy(
            normed.at[state_rows(quarter, chunk), :],
            array.at[:, pl.ds(TILE * chunk, TILE)],
            state_sem.at[quarter, chunk],
        )

    for chunk in range(PIECES):
        state_copy(weights, grad, 0, chunk).start()
    def cot_copy(slot):
        return pltpu.make_async_copy(
            cotangent.at[slot_rows(slot), :], side.at[turn_of(slot, 2)], cot_sem.at[slot]
        )

    def output_copy(slot):
        return pltpu.make_async_copy(
            side.at[turn_of(slot, 2)], normed_out.at[slot_rows(slot), :], out_sem.at[slot]
        )

    def grad_copy(slot):
        rows = slot_rows(slot)
        return pltpu.make_async_copy(grad.at[rows, :], input_grad.at[rows, :], out_sem.at[slot])

    for slot in range(2):
        cot_copy(slot).start()
    tok_copy = pltpu.make_async_copy(tokens, normed, in_sem.at[1])
    tok_copy.start()

    barrier = pltpu.get_barrier_semaphore()
    peers = []
    for group in ("line_group", "plane_group"):
        index, size, device_of = here[group]
        peers += [device_of((index + step) % size) for step in range(1, size)]
    for peer in peers:
        pl.semaphore_signal(barrier, inc=1, device_id=peer, device_id_type=pl.DeviceIdType.MESH)
    pl.semaphore_wait(barrier, len(peers))

    for chunk in range(PIECES):
        state_copy(weights, grad, 0, chunk).wait()
    for unit in range(3):
        for half in range(2):
            for part in range(3):
                lanes = slice((unit + 3 * half) * 128, (unit + 3 * half + 1) * 128)
                place_lanes = slice((3 * half + part) * 128, (3 * half + part + 1) * 128)
                grad[state_rows(1, unit), place_lanes] = grad[state_rows(0, part), lanes]

    def swap(first, count):
        rows = pl.ds(24 * first, 24 * count)
        return send(
            grad.at[pl.ds(SLOT + 24 * first, 24 * count), other],
            shares.at[rows, other],
            twin_sem.at[0, first],
            twin_sem.at[1, first],
            here["twin"],
        )

    swap(0, 3).start()
    def fill(piece):
        rows = pl.ds(pl.multiple_of(24 * piece, 8), 24)
        own, twin = grad[pl.ds(pl.multiple_of(SLOT + 24 * piece, 8), 24), mine], shares[rows, mine]
        upper = jnp.where(core == 0, own, twin)
        lower = jnp.where(core == 0, twin, own)
        joined = jnp.concatenate([upper, lower], axis=0)
        walls[piece, high, low, y, x, :, mine] = joined.astype(LOW)

    swap(0, 3).wait()
    each(3, fill)

    own, line = (high, low, y, x), (slice(None), low, y, x)
    column, next_column = (slice(None), slice(None), y, x), (slice(None), slice(None), y1, x1)
    everything = (slice(None),) * 4
    paths = (
        (
            ((own, "far_z"),),
            ((line, "near_z"),),
            ((column, "first"), (column, "second")),
            ((next_column, "second"),),
            ((everything, "twin"),),
        ),
        (
            ((own, "first"), (own, "far_z")),
            (((high, low, y1, x1), "far_z"), (line, "near_z")),
            (((slice(None), low, y1, x1), "near_z"), (column, "second")),
            ((next_column, "second"),),
            ((everything, "twin"),),
        ),
    )

    def gather_copies(piece, path, stage):
        first = sum(len(copies) for copies in paths[path][:stage])
        copies = []
        for index, (blocks, device) in enumerate(paths[path][stage]):
            part = walls.at[(piece,) + blocks + (slice(None), mine)]
            sent, got = (
                array.at[piece, first + index] for array in (gather_sent, gather_got)
            )
            copies.append(send(part, part, sent, got, here[device]))
        return copies

    def gather(base, index=0):
        def advance(piece, path, stage):
            if stage > 0:
                for copy in gather_copies(piece, path, stage - 1):
                    copy.wait_recv()
            if stage < 5:
                for copy in gather_copies(piece, path, stage):
                    copy.start()
            else:
                for done in range(5):
                    for copy in gather_copies(piece, path, done):
                        copy.wait_send()

        for stage in range(5, -1, -1):
            if (base - 3 * stage) % 2:
                continue

            def step(piece, stage=stage):
                if isinstance(piece, int):
                    advance(piece, min(piece % 3, 1), stage)
                else:
                    turn = lax.rem(piece, 3)
                    pl.when(turn == 0)(lambda: advance(piece, 0, stage))
                    pl.when(turn != 0)(lambda: advance(piece, 1, stage))

            guarded((base - 3 * stage) // 2 + index, step)

    def weight(piece):
        return walls[piece].reshape(TILE, TILE)

    gather(0)
    gather(1)
    make_order(act)
    for block in range(6):
        values = jnp.concatenate(
            [
                grad[state_rows(0, 4 + part // 3), part % 3 * 256 : part % 3 * 256 + 256]
                for part in (2 * block, 2 * block + 1)
            ],
            axis=1,
        )
        ordered = dot(values.astype(LOW), act[0, 0:512, 0:512], 1, 1)
        for chunk in range(4):
            grad[state_rows(1, 4 + chunk), block * 128 : block * 128 + 128] = ordered[
                :, chunk * 128 : chunk * 128 + 128
            ]
    for chunk in (3, 8, 9, 10, 11):
        grad[state_rows(1, chunk), :] = grad[state_rows(0, chunk), :]
    swap(3, 9).start()
    gather(2)
    gather(3)
    vec_grad[...] = jnp.zeros_like(vec_grad)
    for unit in range(3):
        for half in range(2):
            lanes = slice((unit + 3 * half) * 128, (unit + 3 * half + 1) * 128)
            for part, row in ((0, 0), (2, 1)):
                target = slice((3 * half + part) * 128, (3 * half + part + 1) * 128)
                qkv_bias[unit, :, target] = vectors[row : row + 1, lanes]
            target = slice((3 * half + 1) * 128, (3 * half + 2) * 128)
            qkv_bias[unit, :, target] = jnp.zeros((1, 128), SUM)
    for block in range(6):
        values = jnp.concatenate(
            [
                vectors[8 + part // 3 : 9 + part // 3, part % 3 * 256 : part % 3 * 256 + 256]
                for part in (2 * block, 2 * block + 1)
            ],
            axis=1,
        )
        ordered = reorder(values, act, 1)
        for chunk in range(4):
            ffn_bias[chunk, :, block * 128 : block * 128 + 128] = ordered[
                :, chunk * 128 : chunk * 128 + 128
            ]

    gather(4)
    gather(5)
    swap(3, 9).wait()
    each(9, lambda piece: fill(3 + piece))
    gather(6)
    gather(7)
    tok_copy.wait()

    def cast_slot(slot):
        rows = slot_rows(slot)
        token_low[rows, :] = normed[rows, :].astype(LOW)

    each(4, cast_slot)
    for tick in range(8, 16):
        gather(tick)

    def project(unit):
        def project_slot(slot):
            rows = slot_rows(slot)
            values = dot(token_low[rows, :], weight(unit), 1, 0) + qkv_bias[unit]
            qkv[unit, rows, :] = values.astype(LOW)

        each(4, project_slot, 2)

        def attend_slots(pair):
            def attend_slot(slot):
                index = 2 * pair + slot
                attend(unit, index, valid(index), qkv, context, log_total)

            each(2, attend_slot, 2)
            pl.when(pair == 0)(lambda: gather(16, unit))
            pl.when(pair == 1)(lambda: gather(17, unit))

        each(2, attend_slots)

    each(3, project)

    def attend_out(slot):
        rows = slot_rows(slot)
        values = normed[rows, :] + (dot(context[rows, :], weight(3), 1, 0) + vectors[2:3, :])
        centred = values - mean_lanes(values)
        inv = lax.rsqrt(mean_lanes(centred * centred) + 1e-05)
        unit_values = centred * inv
        normed[rows, :] = unit_values
        inverse[rows, :] = jnp.broadcast_to(inv, (SLOT, 128))
        hidden_low[rows, :] = (unit_values * vectors[3:4, :] + vectors[4:5, :]).astype(LOW)

    gather(22)
    each(4, attend_out, 2)

    def widen(chunk):
        gather(23, chunk)

        def widen_slot(slot):
            rows = slot_rows(slot)
            pre = dot(hidden_low[rows, :], weight(4 + chunk), 1, 0) + ffn_bias[chunk]
            phi = 0.5 + 0.5 * lax.erf(pre * 0.7071067811865476)
            act[chunk, rows, :] = (pre * phi).astype(LOW)
            bell = jnp.exp(pre * pre * -0.5) * 0.3989422804014327
            slope[chunk, rows, :] = (phi + pre * bell).astype(LOW)

        each(2, widen_slot, 2)
        gather(24, chunk)
        each(2, lambda slot: widen_slot(2 + slot), 2)

    each(4, widen, 4)
    def narrow_first(slot):
        rows = slot_rows(slot)
        start = normed[rows, :] * vectors[3:4, :] + (vectors[4:5, :] + vectors[5:6, :])
        grad[rows, :] = start + dot(act[0, rows, :], weight(8), 1, 0)

    gather(31)
    each(4, narrow_first, 2)
    gather(32)

    def narrow(chunk):
        def narrow_slot(slot):
            rows = slot_rows(slot)
            grad[rows, :] += dot(act[1 + chunk, rows, :], weight(9 + chunk), 1, 0)

        each(4, narrow_slot, 2)

    gather(33)
    narrow(0)
    gather(34)
    gather(35)
    narrow(1)
    gather(36)
    gather(37)

    def finish_slot(slot):
        rows = slot_rows(slot)

        @pl.when(jnp.logical_and(slot >= 1, slot < 3))
        def _():
            output_copy(slot - 1).wait()
            cot_copy(slot + 1).start()

        values = grad[rows, :] + dot(act[3, rows, :], weight(11), 1, 0)
        centred = values - mean_lanes(values)
        inv = lax.rsqrt(mean_lanes(centred * centred) + 1e-05)
        unit_values = centred * inv
        kept = lax.broadcasted_iota(jnp.int32, (SLOT, 1), 0) < valid(slot)
        cot_copy(slot).wait()
        grad_out = jnp.where(kept, side[turn_of(slot, 2)], 0.0)
        side[turn_of(slot, 2)] = unit_values
        output_copy(slot).start()
        vec_grad[6:7, :] += sum_rows(grad_out * unit_values)
        vec_grad[7:8, :] += sum_rows(grad_out)
        scaled = grad_out * vectors[6:7, :]
        result = inv * (
            scaled - mean_lanes(scaled) - unit_values * mean_lanes(scaled * unit_values)
        )
        grad[rows, :] = result
        rounded = result.astype(LOW)
        grad_low[rows, :] = rounded
        vec_grad[5:6, :] += sum_rows(rounded.astype(SUM))

    each(4, finish_slot, 2)
    output_copy(2).wait()
    output_copy(3).wait()

    def reduce_copies(index, stage):
        two, four = turn_of(index, 2), turn_of(index, 4)
        if stage == 3:
            triples = [
                (line_z(step), z_send.at[two, step - 1], z_got.at[four, step - 1])
                for step in range(1, 4)
            ]
        else:
            triples = [
                (
                    None,
                    (here["second"], pair_send.at[two], pair_got.at[four]),
                    (here["first"], line_send.at[two], line_got.at[four]),
                )[stage]
            ]
        return [
            send(
                source,
                target,
                reduce_sent.at[stage + step, two],
                reduce_got.at[stage + step, four],
                device,
            )
            for step, (device, source, target) in enumerate(triples)
        ]

    def half_copy(index, part):
        two = turn_of(index, 2)
        return send(
            mat_send.at[part],
            mat_got.at[two, part],
            reduce_sent.at[6 * part, two],
            reduce_got.at[6 * part, two],
            here["twin"],
        )

    def line_z(step):
        return ((z + step) % 4 * 2 + y, x * 2 + core)

    def begin(index, stage):
        for copy in reduce_copies(index, stage):
            copy.start()

    def end(index, stage):
        for copy in reduce_copies(index, stage):
            copy.wait()

    def folded(rows):
        return jnp.concatenate([rows[..., :HALF], rows[..., HALF:]], axis=-2)

    def reduce(notch):
        def first(index):
            for part in range(2):
                half_copy(index, part).wait()
            turn, got = turn_of(index, 2), turn_of(index, 2)

            ours = pl.ds(pl.multiple_of(24 * core, 8), 24)

            def column(row, col):
                own_rows = folded(mat[:, :, row, col, ours, :])
                return own_rows + mat_got[got, :, :, row, col].astype(SUM)

            pair_send[turn, 0] = column(y2, x2).astype(LOW)
            pair_send[turn, 1] = column(1 - y, 1 - x).astype(LOW)
            begin(index, 1)
            pair_keep[turn, 0] = column(y, x)
            pair_keep[turn, 1] = column(y1, x1)

        def third(index):
            end(index, 2)
            turn, got = turn_of(index, 2), turn_of(index, 4)

            def block(place):
                row, col = place // 2, place % 2
                return line_keep[turn, row, col] + line_got[got, row, col].astype(SUM)

            for step in range(1, 4):
                z_send[turn, step - 1] = block((z + step) % 4).astype(LOW)
            begin(index, 3)
            z_keep[turn] = block(z)

        guarded(notch - 4, third)
        guarded(notch - 1, first)

    def reduce_odd(notch):
        def second(index):
            end(index, 1)
            turn, got = turn_of(index, 2), turn_of(index, 4)
            line_send[turn] = (pair_keep[turn, 1] + pair_got[got, 1].astype(SUM)).astype(LOW)
            begin(index, 2)
            line_keep[turn] = pair_keep[turn, 0] + pair_got[got, 0].astype(SUM)

        def fourth(index):
            end(index, 3)
            turn, got = turn_of(index, 2), turn_of(index, 4)
            total = z_keep[turn]
            for step in range(3):
                total += z_got[got, step].astype(SUM)
            rows = pl.ds(pl.multiple_of(24 * index, 8), 24)
            shares[rows, :HALF] = total[:24]
            shares[rows, HALF:] = total[24:]

        guarded(notch - 2, second)
        guarded(notch - 5, fourth)

    def emit(index, left, right, unroll=1):
        reduce(index)
        shape = mat.shape[1:]


        theirs = pl.ds(pl.multiple_of(24 * (1 - core), 8), 24)

        def multiply(part):
            lanes = pl.ds(pl.multiple_of(part * HALF, 128), HALF)
            mat[part] = dot(left[:, lanes], right[...], 0, 0).reshape(shape)
            mat_send[part] = folded(mat[part, :, :, :, theirs, :]).astype(LOW)
            half_copy(index, part).start()

        each(2, multiply, unroll)
        reduce_odd(index)

    def back_chunk(chunk):
        emit(2 * chunk, act.at[chunk], grad_low)

        def back_slot(slot):
            rows = slot_rows(slot)
            values = dot(grad_low[rows, :], weight(8 + chunk), 1, 1)
            rounded = (values * slope[chunk, rows, :].astype(SUM)).astype(LOW)
            slope[chunk, rows, :] = rounded
            row = pl.ds(8 + chunk, 1)
            vec_grad[row, :] += sum_rows(rounded.astype(SUM))

        each(4, back_slot, 4)
        emit(2 * chunk + 1, hidden_low, slope.at[chunk])

        def back_hidden(slot):
            rows = slot_rows(slot)
            grad[rows, :] += dot(slope[chunk, rows, :], weight(4 + chunk), 1, 1)

        each(4, back_hidden, 4)

    each(4, back_chunk, 4)

    def back_norm(slot):
        rows = slot_rows(slot)
        total = grad[rows, :]
        unit_values = normed[rows, :]
        vec_grad[3:4, :] += sum_rows(total * unit_values)
        vec_grad[4:5, :] += sum_rows(total)
        scaled = total * vectors[3:4, :]
        inv = inverse[rows, 0:1]
        result = inv * (
            scaled - mean_lanes(scaled) - unit_values * mean_lanes(scaled * unit_values)
        )
        grad[rows, :] = result
        rounded = result.astype(LOW)
        grad_low[rows, :] = rounded
        vec_grad[2:3, :] += sum_rows(rounded.astype(SUM))

    each(4, back_norm, 2)
    emit(8, context, grad_low)
    states = (moment1, moment2, weights)
    for quarter, array in enumerate(states):
        for chunk in range(PIECES):
            state_copy(array, normed, quarter, chunk).start()

    def back_context(slot):
        rows = slot_rows(slot)
        context[rows, :] = dot(grad_low[rows, :], weight(3), 1, 1).astype(LOW)

    each(4, back_context, 4)

    def back_unit(unit):
        each(
            4,
            lambda slot: attend_back(unit, slot, valid(slot), qkv, context, log_total, vec_grad),
        )
        emit(9 + unit, token_low, qkv.at[unit], 1)

    each(3, back_unit)

    def exchange(group, source, slots, sems):
        index, size, device_of = here[group]

        def copies(outgoing):
            found = []
            for step in range(1, size):
                other_index = (index + (step if outgoing else size - step)) % size
                found.append(
                    send(
                        source,
                        slots(index if outgoing else other_index),
                        sems.at[0, step],
                        sems.at[1, index if outgoing else other_index],
                        device_of(other_index),
                    )
                )
            return found

        def start():
            for copy in copies(True):
                copy.start()
            slots(index)[...] = source[...]

        def wait():
            for copy in copies(True):
                copy.wait_send()
            for copy in copies(False):
                copy.wait_recv()
            total = slots(0)[...]
            for slot in range(1, size):
                total += slots(slot)[...]
            source[...] = total

        return start, wait

    def back_tokens(slot):
        rows = slot_rows(slot)
        total = grad[rows, :]
        for unit in range(3):
            total += dot(qkv[unit, rows, :], weight(unit), 1, 1)
        grad[rows, :] = total
        grad_copy(slot).start()

    def lane_sums(values):
        total = sum_rows(values)
        return sum(total[:, 128 * index : 128 * index + 128] for index in range(6))

    def group_of(chunk):
        return 0 if chunk < 3 else 1 if chunk == 3 else 2 if chunk < 8 else 3

    def adapt_chunk(chunk):
        row = 4 + group_of(chunk)
        first, second, step = adapt(
            *(normed[state_rows(quarter, chunk), :] for quarter in (0, 1, 3))
        )
        step = step + 0.01 * normed[state_rows(2, chunk), :]
        normed[state_rows(0, chunk), :] = first
        normed[state_rows(1, chunk), :] = second
        normed[state_rows(3, chunk), :] = step
        result_copy(new_moment1, 0, chunk).start()
        result_copy(new_moment2, 1, chunk).start()
        squares[row : row + 1, :] += lane_sums(step * step)

    def weight_squares():
        squares[...] = jnp.zeros_like(squares)
        for quarter, array in enumerate(states):
            for chunk in range(PIECES):
                state_copy(array, normed, quarter, chunk).wait()
        for chunk in range(PIECES):
            held = normed[state_rows(2, chunk), :]
            row = group_of(chunk)
            squares[row : row + 1, :] += lane_sums(held * held)

    def adapt_early():
        make_order(act)
        normed[state_rows(3, 3), :] = shares[pl.ds(24 * 8, 24), :]
        for chunk in range(4):
            normed[state_rows(3, 8 + chunk), :] = shares[pl.ds(24 * 2 * chunk, 24), :]
        for block in range(6):
            values = jnp.concatenate(
                [
                    shares[pl.ds(24 * (2 * chunk + 1), 24), block * 128 : block * 128 + 128]
                    for chunk in range(4)
                ],
                axis=1,
            )
            ordered = reorder(values, act, 0)
            for half in range(2):
                part = 2 * block + half
                lanes = slice(part % 3 * 256, part % 3 * 256 + 256)
                normed[state_rows(3, 4 + part // 3), lanes] = ordered[
                    :, half * 256 : half * 256 + 256
                ]
        for chunk in range(3, PIECES):
            adapt_chunk(chunk)

    def adapt_late():
        for unit in range(3):
            for half in range(2):
                for part in range(3):
                    lanes = slice((unit + 3 * half) * 128, (unit + 3 * half + 1) * 128)
                    source = slice((3 * half + part) * 128, (3 * half + part + 1) * 128)
                    normed[state_rows(3, part), lanes] = shares[pl.ds(24 * (9 + unit), 24), source]
        for chunk in range(3):
            adapt_chunk(chunk)

    def order_vectors():
        for block in range(6):
            values = jnp.concatenate(
                [
                    vec_grad[8 + chunk : 9 + chunk, block * 128 : block * 128 + 128]
                    for chunk in range(4)
                ],
                axis=1,
            )
            ordered = reorder(values, act, 0)
            for half in range(2):
                part = 2 * block + half
                lanes = slice(part % 3 * 256, part % 3 * 256 + 256)
                row = 8 + part // 3
                vec_total[row : row + 1, lanes] = ordered[:, half * 256 : half * 256 + 256]
        vec_total[0:8, :] = vec_grad[0:8, :]

    def vec_slots(turn):
        return lambda slot: side.at[turn, pl.ds(pl.multiple_of(16 * slot, 8), 16), :]

    def square_slots(turn):
        return lambda slot: squares_got.at[turn, slot]

    exchanges = [
        exchange(group, array, slots, sems)
        for group, array, slots, sems in (
            ("line_group", vec_grad, vec_slots(0), vec_sem.at[0]),
            ("plane_group", vec_grad, vec_slots(1), vec_sem.at[1]),
            ("line_group", squares, square_slots(0), square_sem.at[0]),
            ("plane_group", squares, square_slots(1), square_sem.at[1]),
        )
    ]
    exchanges[0][0]()

    def drain(step):
        reduce(12 + step)
        pl.when(step < 4)(lambda: back_tokens(step))
        pl.when(step == 0)(weight_squares)

        @pl.when(step == 1)
        def _():
            exchanges[0][1]()
            exchanges[1][0]()

        pl.when(step == 3)(adapt_early)
        reduce_odd(12 + step)

    each(5, drain)
    exchanges[1][1]()
    adapt_late()
    exchanges[2][0]()
    order_vectors()
    exchanges[2][1]()
    exchanges[3][0]()
    exchanges[3][1]()
    sums = jnp.sum(squares[...], axis=1, keepdims=True)
    square_pairs[:, 0:1] = sums[0:4]
    square_pairs[:, 1:2] = sums[4:8]
    norms = jnp.sqrt(sums)
    ratio = norms[0:4] / (norms[4:8] + 1e-06)
    for chunk in range(PIECES):
        group = group_of(chunk)
        rows = state_rows(2, chunk)
        factor = 0.3 * ratio[group : group + 1, :]
        normed[rows, :] = normed[rows, :] - factor * normed[state_rows(3, chunk), :]
        result_copy(new_weights, 2, chunk).start()
    for quarter, array in enumerate((new_moment1, new_moment2, new_weights)):
        for chunk in range(PIECES):
            result_copy(array, quarter, chunk).wait()
    for slot in range(4):
        grad_copy(slot).wait()


def fused(
    tokens,
    cotangent,
    lengths,
    null_flags,
    weights,
    moment1,
    moment2,
    vectors,
    vec_moment1,
    vec_moment2,
):
    rows = tokens.shape[0]
    vmem = pl.BlockSpec(memory_space=pltpu.VMEM)
    smem = pl.BlockSpec(memory_space=pltpu.SMEM)
    hbm = pl.BlockSpec(memory_space=pl.ANY)
    full = lambda *shape: pltpu.VMEM(shape, SUM)
    low = lambda *shape: pltpu.VMEM(shape, LOW)
    copies = lambda *shape: pltpu.SemaphoreType.DMA(shape)
    like = lambda array: jax.ShapeDtypeStruct(array.shape, array.dtype)
    unit_values, input_grad, first, second, new_weights, vec_total, squares = pl.pallas_call(
        layer,
        out_shape=[
            like(tokens),
            like(tokens),
            like(weights),
            like(weights),
            like(weights),
            like(vectors),
            jax.ShapeDtypeStruct((4, 2), SUM),
        ],
        in_specs=[smem, smem] + [hbm] * 5 + [vmem],
        out_specs=[hbm] * 5 + [vmem] * 2,
        scratch_shapes=[
            low(PIECES, 2, 2, 2, 2, 48, TILE),
            full(rows, TILE),
            low(rows, TILE),
            low(3, rows, TILE),
            low(rows, TILE),
            low(rows, TILE),
            low(4, rows, TILE),
            low(4, rows, TILE),
            full(rows, TILE),
            low(rows, TILE),
            full(2, SLOT, TILE),
            full(rows, 128),
            full(3, 4, 4, SLOT),
            full(16, TILE),
            full(2, 2, 2, 2, 48, TILE),
            low(2, 2, 2, 2, 48, HALF),
            low(2, 2, 2, 2, 2, 48, HALF),
            full(2, 2, 2, 2, 48, HALF),
            low(2, 2, 2, 2, 48, HALF),
            low(4, 2, 2, 2, 48, HALF),
            full(2, 2, 2, 48, HALF),
            low(2, 2, 2, 48, HALF),
            low(4, 2, 2, 48, HALF),
            full(2, 48, HALF),
            low(2, 3, 48, HALF),
            low(4, 3, 48, HALF),
            full(SLOT, TILE),
            full(3, 1, TILE),
            full(4, 1, TILE),
            full(8, 128),
            full(2, 8, 8, 128),
            copies(2),
            copies(4),
            copies(2, 4),
            copies(PIECES, 8),
            copies(PIECES, 8),
            copies(7, 2),
            copies(7, 4),
            copies(2, 2, 8),
            copies(4, PIECES),
            copies(2, 2, 8),
            copies(4),
        ],
        compiler_params=pltpu.CompilerParams(
            collective_id=0, has_side_effects=True, vmem_limit_bytes=64 * 2**20
        ),
        cost_estimate=pl.CostEstimate(
            flops=60 * 10**9, bytes_accessed=60 * 10**6, transcendentals=10**7
        ),
    )(
        lengths,
        null_flags,
        tokens,
        cotangent,
        weights,
        moment1,
        moment2,
        vectors,
    )
    output = unit_values * vectors[6] + vectors[7]
    vec_first, vec_second, vec_step = adapt(vec_moment1, vec_moment2, vec_total)
    norm_pairs = jnp.sqrt(squares)
    trust = norm_pairs[:, 0] / (norm_pairs[:, 1] + 1e-06)
    return (
        output,
        input_grad,
        first,
        second,
        new_weights,
        vec_first,
        vec_second,
        vectors - 0.3 * vec_step,
        norm_pairs,
        trust,
    )


def solution(mesh):
    split = P(("dp", "shard"), None)
    flat = P(("dp", "shard"))
    in_specs = (split, split, flat, flat, split, split, split, P(), P(), P())
    out_specs = (split,) * 5 + (P(),) * 5
    body = fused if mesh.shape["dp"] == 8 and mesh.shape["shard"] == 4 else plain
    return jax.shard_map(body, mesh=mesh, in_specs=in_specs, out_specs=out_specs, check_vma=False)
```
